32 devices in a mesh: lon: 8 (over z, x), freq: 4 (over y, core).
Axes of the slice: x: 2, y: 2, z: 4, core: 2. Of those that a mesh axis runs over, the one named last changes fastest.
Arguments:
- spectrum: float32 [32, 36, 24, 1024], P('freq', None, None, 'lon'), may hold values from 0.03 to 1
- east_wind: float32 [24, 1024], P(None, 'lon'), may hold values from -30 to 30
- north_wind: float32 [24, 1024], P(None, 'lon'), may hold values from -30 to 30
- land_sea: int32 [24, 1024], P(None, 'lon'), may hold values from 0 to 2
- edge_rows: int32 [2, 1024], P(None, 'lon'), may hold values from 1 to 3
Outputs:
- energy: float32 [32, 36, 24, 1024], P('freq', None, None, 'lon')
- mean_slope: float32 [24, 1024], P(None, 'lon')
The draws below stay inside these ranges and needn't reach their ends.
All inputs are finite; a program needn't handle non-finite values.
Results may differ from the reference program's by a relative error of at most 0.0001.
Values sent between devices are 32-bit elements; how exact they have to be, the bound alone decides.
No kernel may reach another device: no remote copies, remote signals or barrier semaphores. Data moves between devices by JAX's collectives and lax.ppermute only.
A program may use at most 128 MiB of HBM per device.

```python
import math
import jax
import jax.numpy as jnp
from jax import lax

NF = 32
ND = 36
LAT = 24
STEPS = 2
LON = 1024


def draw_spectrum(key, part):
    key = jax.random.fold_in(key, 11)
    peak_key, rough_key = jax.random.split(key)
    peak_angle = jax.random.uniform(peak_key, (LAT, LON), jnp.float32, 0.0, 2.0 * math.pi)
    angles = jnp.arange(ND).astype(jnp.float32) * (2.0 * math.pi / ND)
    lobe_shape = jnp.maximum(jnp.cos(angles[:, None, None] - peak_angle[None]), 0.0)
    lobe_shape = lobe_shape * lobe_shape
    lobe_shape = lobe_shape * lobe_shape
    lobe_shape = lobe_shape * lobe_shape
    roughness = jnp.exp(jax.random.uniform(rough_key, (NF, ND, LAT, LON), jnp.float32, -0.5, 0.0))
    return jnp.clip((0.05 + 0.95 * lobe_shape[None]) * roughness, 0.03, 1.0)


def with_ends(values, rng, smallest, high):
    shape = values.shape
    index_at = [jax.random.randint(jax.random.fold_in(rng, axis), (), 0, shape[axis]) for axis in range(len(shape))]
    values = values.at[tuple(index_at)].set(smallest)
    longest = shape.index(max(shape))
    index_at[longest] = (index_at[longest] + 1) % shape[longest]
    return values.at[tuple(index_at)].set(high)


def block_scale(key, shape, cuts, low, high):
    gain = 1.0
    for position, parts in cuts:
        draws = jax.random.uniform(jax.random.fold_in(jax.random.fold_in(key, 6), position), (parts,), jnp.float32, low / len(cuts), high / len(cuts))
        gain = gain * jnp.repeat(jnp.exp(draws), shape[position] // parts).reshape((-1,) + (1,) * (len(shape) - 1 - position))
    return gain


def noise(key, shape, scale, most, cuts=(), dtype=jnp.bfloat16):
    drawn = jax.random.normal(key, shape, jnp.float32) * scale
    if len(cuts) > 0:
        drawn = block_scale(key, shape, cuts, -0.22, 0.18) * drawn
    return jnp.clip(drawn, min=-most, max=most).astype(dtype)


def setup_inputs(seed: int = 0) -> dict:
    keys = jax.random.split(jax.random.key(seed), 6)
    return {
        "spectrum": draw_spectrum(jax.random.fold_in(keys[5], 71), 0),
        "east_wind": noise(keys[1], (LAT, LON), 8.0, 30.0, ((1, 8),), jnp.float32),
        "north_wind": noise(keys[2], (LAT, LON), 8.0, 30.0, ((1, 8),), jnp.float32),
        "land_sea": with_ends(jax.random.randint(keys[3], (LAT, LON), 0, 3), jax.random.fold_in(keys[3], 1), 0, 2).astype(jnp.int32),
        "edge_rows": with_ends(jax.random.randint(keys[4], (2, LON), 1, 4), jax.random.fold_in(keys[4], 1), 1, 3).astype(jnp.int32),
    }


COURANT_MAX = 0.9
FREQ_RATIO = 1.1
WIND_REF = 8.0
WIND_CLIP = 2.0
GROWTH = 0.01
BREAKING = 0.3
SATURATION_REF = 0.4
CUMULATIVE = 2.0
SWELL_DAMP = 0.1
ICE_DAMP = 0.5

def beam_warming(padded, courant, along_axis):
    length = padded.shape[along_axis] - 4

    def cut_at(offset):
        return lax.slice_in_dim(padded, 2 + offset, 2 + offset + length, axis=along_axis)
    centre = cut_at(0)
    back_one = cut_at(-1)
    back_two = cut_at(-2)
    ahead_one = cut_at(1)
    ahead_two = cut_at(2)
    forward = jnp.maximum(courant, 0.0)
    backward = jnp.maximum(-courant, 0.0)
    return centre - 0.5 * forward * (3.0 * centre - 4.0 * back_one + back_two) + 0.5 * forward * forward * (centre - 2.0 * back_one + back_two) - 0.5 * backward * (3.0 * centre - 4.0 * ahead_one + ahead_two) + 0.5 * backward * backward * (centre - 2.0 * ahead_one + ahead_two)

def propagate(band_inputs):
    band_layer, along_lon, along_lat = band_inputs
    padded = jnp.pad(band_layer, ((0, 0), (0, 0), (2, 2)), mode='wrap')
    shifted = beam_warming(padded, along_lon[:, None, None], 2)
    padded = jnp.pad(shifted, ((0, 0), (2, 2), (0, 0)), mode='edge')
    return beam_warming(padded, along_lat[:, None, None], 1)

def reference(spectrum, east_wind, north_wind, land_sea, edge_rows):
    sea_mask = (land_sea != 0).astype(jnp.float32)
    ice_mask = (land_sea == 2).astype(jnp.float32)
    row_index = jnp.arange(LAT).astype(jnp.int32)[:, None]
    held_mask = (row_index < edge_rows[0][None, :]) | (row_index >= LAT - edge_rows[1][None, :])
    step_angle = 2.0 * math.pi / ND
    angles = jnp.arange(ND).astype(jnp.float32) * step_angle
    cosines = jnp.cos(angles)
    sines = jnp.sin(angles)
    differ = jnp.cos(angles[:, None] - angles[None, :])
    kernel = jnp.where(differ > 0.0, differ * differ, 0.0) * step_angle
    ratios = jnp.power(FREQ_RATIO, jnp.arange(NF).astype(jnp.float32))
    norm_stress = jnp.sum(ratios * jnp.sqrt(ratios))
    norm_slope = jnp.sum(ratios * ratios)
    courant_lon = COURANT_MAX * cosines[None, :] / ratios[:, None]
    courant_lat = 0.5 * COURANT_MAX * sines[None, :] / ratios[:, None]
    wind_along = cosines[:, None, None] * east_wind[None] + sines[:, None, None] * north_wind[None]
    wind_drive = jnp.minimum(jnp.maximum(wind_along, 0.0) / WIND_REF, WIND_CLIP) ** 2 * (1.0 - ice_mask)[None]
    energy = spectrum
    mean_slope = jnp.zeros((LAT, LON), jnp.float32)
    for step_index in range(STEPS):
        energy = lax.map(propagate, (energy, courant_lon, courant_lat))
        energy = jnp.where(held_mask[None, None], spectrum, jnp.maximum(energy, 0.0)) * sea_mask[None, None]

        def totals(running, band_inputs):
            band_layer, band_ratio = band_inputs
            slope_now, stress_now = running
            slope_now = slope_now + lax.optimization_barrier(jnp.sum(band_layer, 0)) * (band_ratio * band_ratio * step_angle / norm_slope)
            stress_now = stress_now + lax.optimization_barrier(jnp.sum(band_layer * wind_drive, 0)) * (band_ratio * jnp.sqrt(band_ratio) * step_angle / norm_stress)
            return ((slope_now, stress_now), band_ratio)
        start_sums = (jnp.zeros((LAT, LON), jnp.float32), jnp.zeros((LAT, LON), jnp.float32))
        (mean_slope, stress), unused = lax.scan(totals, start_sums, (energy, ratios))
        stress_gain = 1.0 + stress / (stress + 1.0)

        def update(lower_sum, band_inputs):
            band_layer, band_ratio = band_inputs
            root_ratio = jnp.sqrt(band_ratio)
            saturation = jnp.einsum('ij,jlw->ilw', kernel, band_layer, precision=lax.Precision.HIGHEST)
            excess = jnp.maximum(jnp.sqrt(saturation) - math.sqrt(SATURATION_REF), 0.0) ** 2
            net_rate = GROWTH * root_ratio * wind_drive * stress_gain[None] - BREAKING * root_ratio * excess / SATURATION_REF - CUMULATIVE * root_ratio * lower_sum / NF - SWELL_DAMP * root_ratio * (mean_slope / (mean_slope + 1.0))[None] - ICE_DAMP * root_ratio * ice_mask[None]
            return (lower_sum + excess, band_layer * jnp.exp(net_rate))
        unused, energy = lax.scan(update, jnp.zeros((ND, LAT, LON), jnp.float32), (energy, ratios))
    return (energy, mean_slope)
```

```python
import functools
import math

import jax
import jax.numpy as jnp
import numpy as np
from jax import lax
from jax.experimental import pallas as pl
from jax.experimental.pallas import tpu as pltpu
from jax.sharding import PartitionSpec as P

NF = 32
STEPS = 2

COURANT_MAX = 0.9
FREQ_RATIO = 1.1
WIND_REF = 8.0
WIND_CLIP = 2.0
GROWTH = 0.01
BREAKING = 0.3
SATURATION_REF = 0.4
CUMULATIVE = 2.0
SWELL_DAMP = 0.1
ICE_DAMP = 0.5

ND = 36
HALF = ND // 2
QUARTER = ND // 4
DTHETA = 2.0 * math.pi / ND
LOG2E = 1.0 / math.log(2.0)
ROOT_REF = math.sqrt(SATURATION_REF)
TILES = 3
LAT = 8 * TILES
WIDTH = 128
STRIDE = 6 * ND + 8

ANGLES = np.arange(ND) * DTHETA
COS = np.cos(ANGLES)
SIN = np.sin(ANGLES)
COS2 = np.cos(2.0 * ANGLES)
SIN2 = np.sin(2.0 * ANGLES)
BACK_LON = [bool(c >= 0.0) for c in COS]
BACK_LAT = [bool(s >= 0.0) for s in SIN]
RANK = [sum(BACK_LON[:j]) if BACK_LON[j] else j - sum(BACK_LON[:j]) for j in range(ND)]


def one_sided(courant):
    c = np.abs(courant)
    return 1.0 - 1.5 * c + 0.5 * c * c, 2.0 * c - c * c, 0.5 * c * c - 0.5 * c


def make_tables():
    ratios = FREQ_RATIO ** np.arange(NF)
    root = np.sqrt(ratios)
    lon = one_sided(COURANT_MAX * COS[None, :] / ratios[:, None])
    lat = one_sided(0.5 * COURANT_MAX * SIN[None, :] / ratios[:, None])
    scalars = np.zeros((NF, STRIDE))
    for i in range(3):
        scalars[:, i : 6 * ND : 6] = lon[i]
        scalars[:, 3 + i : 6 * ND : 6] = lat[i]
    extra = 6 * ND
    scalars[:, extra + 0] = -BREAKING / SATURATION_REF * root * LOG2E
    scalars[:, extra + 1] = -CUMULATIVE / NF * root * LOG2E
    scalars[:, extra + 2] = ratios * ratios * DTHETA / np.sum(ratios * ratios)
    scalars[:, extra + 3] = ratios * root * DTHETA / np.sum(ratios * root)
    scalars[:, extra + 4] = root * LOG2E
    edge = np.zeros((NF, 4, WIDTH))
    for j in range(ND):
        for r in range(TILES):
            lane = 2 * (TILES * RANK[j] + r)
            if BACK_LON[j]:
                edge[:, 0, lane] = edge[:, 0, lane + 1] = lon[2][:, j]
                edge[:, 1, lane] = lon[1][:, j]
            else:
                edge[:, 2, lane] = edge[:, 2, lane + 1] = lon[2][:, j]
                edge[:, 3, lane + 1] = lon[1][:, j]
    return scalars.reshape(-1).astype(np.float32), edge.astype(np.float32)


SCALARS, EDGE = make_tables()


def lanes():
    return lax.broadcasted_iota(jnp.int32, (8, WIDTH), 1)


def pack_edges(tile_of, right_ref, left_ref):
    pair = lanes() // 2
    for back, out in ((True, right_ref), (False, left_ref)):
        acc = jnp.zeros((8, WIDTH), jnp.float32)
        for j in range(ND):
            if BACK_LON[j] != back:
                continue
            for r in range(TILES):
                place = TILES * RANK[j] + r
                shift = (2 * place - (WIDTH - 2 if back else 0)) % WIDTH
                tile = tile_of(j, r)
                moved = tile if shift == 0 else pltpu.roll(tile, shift, 1)
                acc = jnp.where(pair == place, moved, acc)
        out[0] = acc


def pack_kernel(q_ref, right_ref, left_ref):
    pack_edges(lambda j, r: q_ref[0, j, 8 * r : 8 * r + 8, :], right_ref, left_ref)


def wind_drive_of(j, r, east_ref, north_ref, open_water):
    rows = slice(8 * r, 8 * r + 8)
    along = float(COS[j]) * east_ref[rows, :] + float(SIN[j]) * north_ref[rows, :]
    drive = jnp.minimum(jnp.maximum(along, 0.0) / WIND_REF, WIND_CLIP)
    return drive * drive * open_water


def saturation_of(p):
    half = 0.5 * DTHETA
    diff = [p[b] - p[b + HALF] for b in range(HALF)]
    both = [p[b] + p[b + HALF] for b in range(HALF)]
    total = both[0]
    for b in range(1, HALF):
        total = total + both[b]
    total = total * (0.5 * half)
    fold = [both[b] - both[b + QUARTER] for b in range(QUARTER)]
    total_c = fold[0] * float(0.5 * half * COS2[0])
    total_s = None
    for b in range(1, QUARTER):
        total_c = total_c + fold[b] * float(0.5 * half * COS2[b])
        term = fold[b] * float(0.5 * half * SIN2[b])
        total_s = term if total_s is None else total_s + term
    diff = [d * half for d in diff]
    diff_c = [diff[b] * float(COS2[b]) for b in range(HALF)]
    diff_s = [diff[b] * float(SIN2[b]) for b in range(HALF)]

    def start(x):
        front = x[0]
        for b in range(1, QUARTER):
            front = front + x[b]
        rear = x[QUARTER]
        for b in range(QUARTER + 1, HALF):
            rear = rear + x[b]
        return 0.5 * (front - rear)

    win, win_c, win_s = start(diff), start(diff_c), start(diff_s)
    out = [None] * ND
    level = [None] * HALF
    for a in range(QUARTER):
        turn = total_c * float(COS2[a])
        if a:
            turn = turn + total_s * float(SIN2[a])
        level[a] = total + turn
        level[a + QUARTER] = total - turn
    for a in range(HALF):
        odd = win + win_c * float(COS2[a])
        if a:
            odd = odd + win_s * float(SIN2[a])
        out[a] = level[a] + odd
        out[a + HALF] = level[a] - odd
        new = a + QUARTER
        if a + 1 < HALF:
            if new < HALF:
                win, win_c, win_s = win + diff[new], win_c + diff_c[new], win_s + diff_s[new]
            else:
                new -= HALF
                win, win_c, win_s = win - diff[new], win_c - diff_c[new], win_s - diff_s[new]
    return out


def source_kernel(
    same,
    scal_ref,
    edge_ref,
    q_ref,
    spec_ref,
    from_left_ref,
    from_right_ref,
    own_right_ref,
    own_left_ref,
    east_ref,
    north_ref,
    land_ref,
    rows_ref,
    out_ref,
    sums_ref,
    drive_ref,
    x_ref,
    p_ref,
):
    k = pl.program_id(0)
    band = lax.axis_index("freq") * pl.num_programs(0) + k
    base = band * STRIDE
    lane = lanes()

    @pl.when(k == 0)
    def _():
        sums_ref[...] = jnp.zeros_like(sums_ref)
        for r in range(TILES):
            water = jnp.where(land_ref[8 * r : 8 * r + 8, :] == 2, 0.0, 1.0)
            for j in range(ND):
                drive_ref[j, 8 * r : 8 * r + 8, :] = wind_drive_of(j, r, east_ref, north_ref, water)

    gap_right = from_left_ref[k] - own_right_ref[k]
    gap_left = from_right_ref[k] - own_left_ref[k]
    fix_back = edge_ref[band, 0:1, :] * gap_right + edge_ref[band, 1:2, :] * pltpu.roll(
        gap_right, WIDTH - 1, 1
    )
    fix_ahead = edge_ref[band, 2:3, :] * gap_left + edge_ref[band, 3:4, :] * pltpu.roll(
        gap_left, 1, 1
    )

    held, sea = [], []
    for r in range(TILES):
        row = lax.broadcasted_iota(jnp.int32, (8, WIDTH), 0) + 8 * r
        held.append((row < rows_ref[0:1, :]) | (row >= LAT - rows_ref[1:2, :]))
        sea.append(jnp.where(land_ref[8 * r : 8 * r + 8, :] != 0, 1.0, 0.0))
    slope = [jnp.zeros((8, WIDTH), jnp.float32) for _ in range(TILES)]
    stress = [jnp.zeros((8, WIDTH), jnp.float32) for _ in range(TILES)]
    at_start, at_end = lane < 2, lane >= WIDTH - 2
    for j in range(ND):
        c0, c1, c2, d0, d1, d2 = (scal_ref[base + 6 * j + i] for i in range(6))
        back = BACK_LON[j]
        lead = 8 if BACK_LAT[j] else 0
        for r in range(TILES):
            q = q_ref[0, j, 8 * r : 8 * r + 8, :]
            one = pltpu.roll(q, 1 if back else WIDTH - 1, 1)
            two = pltpu.roll(q, 2 if back else WIDTH - 2, 1)
            place = 2 * (TILES * RANK[j] + r)
            shift = (-place if back else WIDTH - 2 - place) % WIDTH
            fix = fix_back if back else fix_ahead
            fix = fix if shift == 0 else pltpu.roll(fix, shift, 1)
            x = c0 * q + c1 * one + c2 * two + jnp.where(at_start if back else at_end, fix, 0.0)
            x_ref[j, lead + 8 * r : lead + 8 * r + 8, :] = x
            if BACK_LAT[j] and r == 0:
                x_ref[j, 0:8, :] = jnp.broadcast_to(x[0:1, :], (8, WIDTH))
            if not BACK_LAT[j] and r == TILES - 1:
                x_ref[j, LAT : LAT + 8, :] = jnp.broadcast_to(x[7:8, :], (8, WIDTH))
        sign = -1 if BACK_LAT[j] else 1
        for r in range(TILES):
            at = lead + 8 * r
            y = (
                d0 * x_ref[j, at : at + 8, :]
                + d1 * x_ref[j, at + sign : at + sign + 8, :]
                + d2 * x_ref[j, at + 2 * sign : at + 2 * sign + 8, :]
            )
            spec = (q_ref if same else spec_ref)[0, j, 8 * r : 8 * r + 8, :]
            y = jnp.where(held[r], spec, jnp.maximum(y, 0.0)) * sea[r]
            p_ref[j, 8 * r : 8 * r + 8, :] = y
            slope[r] = slope[r] + y
            stress[r] = stress[r] + y * drive_ref[j, 8 * r : 8 * r + 8, :]

    extra = base + 6 * ND
    for r in range(TILES):
        rows = slice(8 * r, 8 * r + 8)
        sums_ref[ND, rows, :] += slope[r] * scal_ref[extra + 2]
        sums_ref[ND + 1, rows, :] += stress[r] * scal_ref[extra + 3]
        p = [p_ref[j, rows, :] for j in range(ND)]
        for j, saturation in enumerate(saturation_of(p)):
            capped = jnp.maximum(saturation, SATURATION_REF)
            excess = capped * lax.rsqrt(capped) - ROOT_REF
            excess = excess * excess
            lower = sums_ref[j, rows, :]
            rate = excess * scal_ref[extra] + lower * scal_ref[extra + 1]
            sums_ref[j, rows, :] = lower + excess
            out_ref[0, j, rows, :] = p_ref[j, rows, :] * jnp.exp2(rate)


def pair_kernel(sums_ref, other_ref, out_ref):
    first = (lax.axis_index("freq") % 2) * HALF
    for i in range(HALF):
        out_ref[i] = sums_ref[first + i] + other_ref[first + i]
    for i in range(2):
        out_ref[HALF + i] = sums_ref[ND + i] + other_ref[ND + i]


def growth_kernel(
    last,
    scal_ref,
    part_ref,
    sums_ref,
    other_ref,
    mine_ref,
    rest_ref,
    east_ref,
    north_ref,
    land_ref,
    out_ref,
    *refs,
):
    rate_ref = refs[-1]
    k = pl.program_id(0)
    freq = lax.axis_index("freq")
    band = freq * pl.num_programs(0) + k

    @pl.when(k == 0)
    def _():
        core = freq % 2
        odd = jnp.where(core == 1, 1.0, 0.0)
        upper = jnp.where(freq >= 2, 1.0, 0.0)
        for r in range(TILES):
            rows = slice(8 * r, 8 * r + 8)
            ice = jnp.where(land_ref[rows, :] == 2, 1.0, 0.0)
            slope = (sums_ref[ND, rows, :] + other_ref[ND, rows, :]) + mine_ref[HALF, rows, :]
            stress = (sums_ref[ND + 1, rows, :] + other_ref[ND + 1, rows, :]) + mine_ref[
                HALF + 1, rows, :
            ]
            if last:
                refs[0][rows, :] = slope
            gain = GROWTH * (1.0 + stress / (stress + 1.0))
            damp = SWELL_DAMP * (slope / (slope + 1.0)) + ICE_DAMP * ice
            for j in range(ND):
                local = j % HALF
                near, far = mine_ref[local, rows, :], rest_ref[local, rows, :]
                in_mine = core == (0 if j < HALF else 1)
                lower = odd * other_ref[j, rows, :] + upper * jnp.where(in_mine, near, far)
                drive = wind_drive_of(j, r, east_ref, north_ref, 1.0 - ice)
                rate_ref[j, rows, :] = gain * drive - damp - (CUMULATIVE / NF) * lower

    root = scal_ref[band * STRIDE + 6 * ND + 4]

    def tile(j, r):
        rows = slice(8 * r, 8 * r + 8)
        value = part_ref[0, j, rows, :] * jnp.exp2(rate_ref[j, rows, :] * root)
        out_ref[0, j, rows, :] = value
        return value

    if last:
        for j in range(ND):
            for r in range(TILES):
                tile(j, r)
    else:
        pack_edges(tile, refs[0], refs[1])


def whole(shape):
    return pl.BlockSpec(shape, lambda k: (0,) * len(shape))


def per_device(spectrum, east_wind, north_wind, land_sea, edge_rows):
    bands, count, lat_rows, width = spectrum.shape
    assert (count, lat_rows, width) == (ND, LAT, WIDTH)
    ring = lax.axis_size("lon")
    assert lax.axis_size("freq") == 4 and bands * 4 == NF
    f32 = jnp.float32
    field = jax.ShapeDtypeStruct(spectrum.shape, f32)
    edges = jax.ShapeDtypeStruct((bands, 8, WIDTH), f32)
    sums = jax.ShapeDtypeStruct((ND + 2, LAT, WIDTH), f32)
    halves = jax.ShapeDtypeStruct((HALF + 2, LAT, WIDTH), f32)
    plane = (LAT, WIDTH)
    band_spec = pl.BlockSpec((1, ND, LAT, WIDTH), lambda k: (k, 0, 0, 0))
    edge_spec = pl.BlockSpec((1, 8, WIDTH), lambda k: (k, 0, 0))
    smem = pl.BlockSpec(memory_space=pltpu.SMEM)
    params = pltpu.CompilerParams(
        dimension_semantics=("arbitrary",), vmem_limit_bytes=40 * 1024 * 1024
    )
    scalars, edge_table = jnp.asarray(SCALARS), jnp.asarray(EDGE)
    swap_core = [(0, 1), (1, 0), (2, 3), (3, 2)]
    swap_chip = [(0, 2), (2, 0), (1, 3), (3, 1)]

    right, left = pl.pallas_call(
        pack_kernel,
        grid=(bands,),
        in_specs=[band_spec],
        out_specs=[edge_spec, edge_spec],
        out_shape=[edges, edges],
        compiler_params=params,
        name="pack_columns",
    )(spectrum)

    energy = spectrum
    for step in range(STEPS):
        last = step == STEPS - 1
        from_left = lax.ppermute(right, "lon", [(i, (i + 1) % ring) for i in range(ring)])
        from_right = lax.ppermute(left, "lon", [((i + 1) % ring, i) for i in range(ring)])
        same = step == 0
        source = pl.BlockSpec((1, 8, 8, WIDTH), lambda k: (0, 0, 0, 0)) if same else band_spec
        part, mine = pl.pallas_call(
            functools.partial(source_kernel, same),
            grid=(bands,),
            in_specs=[smem, whole(EDGE.shape), band_spec, source]
            + [whole((bands, 8, WIDTH))] * 4
            + [whole(plane)] * 3
            + [whole((2, WIDTH))],
            out_specs=[band_spec, whole(sums.shape)],
            out_shape=[field, sums],
            scratch_shapes=[
                pltpu.VMEM((ND, LAT, WIDTH), f32),
                pltpu.VMEM((ND, LAT + 8, WIDTH), f32),
                pltpu.VMEM((ND, LAT, WIDTH), f32),
            ],
            compiler_params=params,
            name="propagate_and_break",
        )(
            scalars, edge_table, energy, spectrum, from_left, from_right, right, left,
            east_wind, north_wind, land_sea, edge_rows,
        )
        other = lax.ppermute(mine, "freq", swap_core)
        pair = pl.pallas_call(
            pair_kernel,
            in_specs=[pl.BlockSpec(memory_space=pltpu.VMEM)] * 2,
            out_specs=pl.BlockSpec(memory_space=pltpu.VMEM),
            out_shape=halves,
            name="pair_sums",
        )(mine, other)
        near = lax.ppermute(pair, "freq", swap_chip)
        far = lax.ppermute(near, "freq", swap_core)
        if last:
            more_specs, more_shapes = [whole(plane)], [jax.ShapeDtypeStruct(plane, f32)]
        else:
            more_specs, more_shapes = [edge_spec, edge_spec], [edges, edges]
        energy, *more = pl.pallas_call(
            functools.partial(growth_kernel, last),
            grid=(bands,),
            in_specs=[smem, band_spec]
            + [whole(sums.shape)] * 2
            + [whole(halves.shape)] * 2
            + [whole(plane)] * 3,
            out_specs=[band_spec] + more_specs,
            out_shape=[field] + more_shapes,
            scratch_shapes=[pltpu.VMEM((ND, LAT, WIDTH), f32)],
            compiler_params=params,
            name="grow",
        )(scalars, part, mine, other, near, far, east_wind, north_wind, land_sea)
        if not last:
            right, left = more
    return energy, more[0]


def solution(mesh):
    in_specs = (
        P("freq", None, None, "lon"),
        P(None, "lon"),
        P(None, "lon"),
        P(None, "lon"),
        P(None, "lon"),
    )
    out_specs = (P("freq", None, None, "lon"), P(None, "lon"))
    return jax.shard_map(
        per_device, mesh=mesh, in_specs=in_specs, out_specs=out_specs, check_vma=False
    )
```

```python
import functools
import math

import jax
import jax.numpy as jnp
import numpy as np
from jax import lax
from jax.experimental import pallas as pl
from jax.experimental.pallas import tpu as pltpu
from jax.sharding import PartitionSpec as P

NF = 32
STEPS = 2

COURANT_MAX = 0.9
FREQ_RATIO = 1.1
WIND_REF = 8.0
WIND_CLIP = 2.0
GROWTH = 0.01
BREAKING = 0.3
SATURATION_REF = 0.4
CUMULATIVE = 2.0
SWELL_DAMP = 0.1
ICE_DAMP = 0.5

ND = 36
HALF = ND // 2
QUARTER = ND // 4
DTHETA = 2.0 * math.pi / ND
LOG2E = 1.0 / math.log(2.0)
ROOT_REF = math.sqrt(SATURATION_REF)
TILES = 3
LAT = 8 * TILES
WIDTH = 128
STRIDE = 6 * ND + 8

ANGLES = np.arange(ND) * DTHETA
COS = np.cos(ANGLES)
SIN = np.sin(ANGLES)
COS2 = np.cos(2.0 * ANGLES)
SIN2 = np.sin(2.0 * ANGLES)
BACK_LON = [bool(c >= 0.0) for c in COS]
BACK_LAT = [bool(s >= 0.0) for s in SIN]
RANK = [sum(BACK_LON[:j]) if BACK_LON[j] else j - sum(BACK_LON[:j]) for j in range(ND)]


def one_sided(courant):
    c = np.abs(courant)
    return 1.0 - 1.5 * c + 0.5 * c * c, 2.0 * c - c * c, 0.5 * c * c - 0.5 * c


def make_tables():
    ratios = FREQ_RATIO ** np.arange(NF)
    root = np.sqrt(ratios)
    lon = one_sided(COURANT_MAX * COS[None, :] / ratios[:, None])
    lat = one_sided(0.5 * COURANT_MAX * SIN[None, :] / ratios[:, None])
    scalars = np.zeros((NF, STRIDE))
    for i in range(3):
        scalars[:, i : 6 * ND : 6] = lon[i]
        scalars[:, 3 + i : 6 * ND : 6] = lat[i]
    extra = 6 * ND
    scalars[:, extra + 0] = -BREAKING / SATURATION_REF * root * LOG2E
    scalars[:, extra + 1] = -CUMULATIVE / NF * root * LOG2E
    scalars[:, extra + 2] = ratios * ratios * DTHETA / np.sum(ratios * ratios)
    scalars[:, extra + 3] = ratios * root * DTHETA / np.sum(ratios * root)
    scalars[:, extra + 4] = root * LOG2E
    edge = np.zeros((NF, 4, WIDTH))
    for j in range(ND):
        for r in range(TILES):
            lane = 2 * (TILES * RANK[j] + r)
            if BACK_LON[j]:
                edge[:, 0, lane] = edge[:, 0, lane + 1] = lon[2][:, j]
                edge[:, 1, lane] = lon[1][:, j]
            else:
                edge[:, 2, lane] = edge[:, 2, lane + 1] = lon[2][:, j]
                edge[:, 3, lane + 1] = lon[1][:, j]
    return scalars.reshape(-1).astype(np.float32), edge.astype(np.float32)


SCALARS, EDGE = make_tables()


def lanes():
    return lax.broadcasted_iota(jnp.int32, (8, WIDTH), 1)


def pack_edges(tile_of, k, right_ref, left_ref):
    pair = lanes() // 2
    for back, out in ((True, right_ref), (False, left_ref)):
        acc = jnp.zeros((8, WIDTH), jnp.float32)
        for j in range(ND):
            if BACK_LON[j] != back:
                continue
            for r in range(TILES):
                place = TILES * RANK[j] + r
                shift = (2 * place - (WIDTH - 2 if back else 0)) % WIDTH
                tile = tile_of(j, r)
                moved = tile if shift == 0 else pltpu.roll(tile, shift, 1)
                acc = jnp.where(pair == place, moved, acc)
        out[k] = acc


def pack_kernel(spec_ref, copy_ref, right_ref, left_ref, arrived):
    bands = copy_ref.shape[0]

    def fetch(k):
        return pltpu.make_async_copy(spec_ref.at[k], copy_ref.at[k], arrived.at[k])

    for k in range(bands):
        fetch(k).start()

    def band(k, carry):
        fetch(k).wait()
        pack_edges(lambda j, r: copy_ref[k, j, 8 * r : 8 * r + 8, :], k, right_ref, left_ref)
        return carry

    lax.fori_loop(0, bands, band, 0)


def wind_drive_of(j, r, east_ref, north_ref, open_water):
    rows = slice(8 * r, 8 * r + 8)
    along = float(COS[j]) * east_ref[rows, :] + float(SIN[j]) * north_ref[rows, :]
    drive = jnp.minimum(jnp.maximum(along, 0.0) / WIND_REF, WIND_CLIP)
    return drive * drive * open_water


def saturation_of(p):
    half = 0.5 * DTHETA
    diff = [p[b] - p[b + HALF] for b in range(HALF)]
    both = [p[b] + p[b + HALF] for b in range(HALF)]
    total = both[0]
    for b in range(1, HALF):
        total = total + both[b]
    total = total * (0.5 * half)
    fold = [both[b] - both[b + QUARTER] for b in range(QUARTER)]
    total_c = fold[0] * float(0.5 * half * COS2[0])
    total_s = None
    for b in range(1, QUARTER):
        total_c = total_c + fold[b] * float(0.5 * half * COS2[b])
        term = fold[b] * float(0.5 * half * SIN2[b])
        total_s = term if total_s is None else total_s + term
    diff = [d * half for d in diff]
    diff_c = [diff[b] * float(COS2[b]) for b in range(HALF)]
    diff_s = [diff[b] * float(SIN2[b]) for b in range(HALF)]

    def start(x):
        front = x[0]
        for b in range(1, QUARTER):
            front = front + x[b]
        rear = x[QUARTER]
        for b in range(QUARTER + 1, HALF):
            rear = rear + x[b]
        return 0.5 * (front - rear)

    win, win_c, win_s = start(diff), start(diff_c), start(diff_s)
    out = [None] * ND
    level = [None] * HALF
    for a in range(QUARTER):
        turn = total_c * float(COS2[a])
        if a:
            turn = turn + total_s * float(SIN2[a])
        level[a] = total + turn
        level[a + QUARTER] = total - turn
    for a in range(HALF):
        odd = win + win_c * float(COS2[a])
        if a:
            odd = odd + win_s * float(SIN2[a])
        out[a] = level[a] + odd
        out[a + HALF] = level[a] - odd
        new = a + QUARTER
        if a + 1 < HALF:
            if new < HALF:
                win, win_c, win_s = win + diff[new], win_c + diff_c[new], win_s + diff_s[new]
            else:
                new -= HALF
                win, win_c, win_s = win - diff[new], win_c - diff_c[new], win_s - diff_s[new]
    return out


def source_kernel(
    scal_ref,
    edge_ref,
    q_ref,
    spec_ref,
    from_left_ref,
    from_right_ref,
    own_right_ref,
    own_left_ref,
    east_ref,
    north_ref,
    land_ref,
    rows_ref,
    out_ref,
    sums_ref,
    drive_ref,
    x_ref,
    p_ref,
):
    bands = q_ref.shape[0]
    sums_ref[...] = jnp.zeros_like(sums_ref)
    for r in range(TILES):
        water = jnp.where(land_ref[8 * r : 8 * r + 8, :] == 2, 0.0, 1.0)
        for j in range(ND):
            drive_ref[j, 8 * r : 8 * r + 8, :] = wind_drive_of(j, r, east_ref, north_ref, water)

    def step(k, carry):
        source_band(
            k, lax.axis_index("freq") * bands + k, scal_ref, edge_ref, q_ref, spec_ref,
            from_left_ref, from_right_ref, own_right_ref, own_left_ref, land_ref, rows_ref,
            out_ref, sums_ref, drive_ref, x_ref, p_ref,
        )
        return carry

    lax.fori_loop(0, bands, step, 0)


def source_band(
    k, band, scal_ref, edge_ref, q_ref, spec_ref,
    from_left_ref, from_right_ref, own_right_ref, own_left_ref, land_ref, rows_ref,
    out_ref, sums_ref, drive_ref, x_ref, p_ref,
):
    base = band * STRIDE
    lane = lanes()
    gap_right = from_left_ref[k] - own_right_ref[k]
    gap_left = from_right_ref[k] - own_left_ref[k]
    fix_back = edge_ref[band, 0:1, :] * gap_right + edge_ref[band, 1:2, :] * pltpu.roll(
        gap_right, WIDTH - 1, 1
    )
    fix_ahead = edge_ref[band, 2:3, :] * gap_left + edge_ref[band, 3:4, :] * pltpu.roll(
        gap_left, 1, 1
    )

    held, sea = [], []
    for r in range(TILES):
        row = lax.broadcasted_iota(jnp.int32, (8, WIDTH), 0) + 8 * r
        held.append((row < rows_ref[0:1, :]) | (row >= LAT - rows_ref[1:2, :]))
        sea.append(jnp.where(land_ref[8 * r : 8 * r + 8, :] != 0, 1.0, 0.0))
    slope = [jnp.zeros((8, WIDTH), jnp.float32) for _ in range(TILES)]
    stress = [jnp.zeros((8, WIDTH), jnp.float32) for _ in range(TILES)]
    at_start, at_end = lane < 2, lane >= WIDTH - 2
    for j in range(ND):
        c0, c1, c2, d0, d1, d2 = (scal_ref[base + 6 * j + i] for i in range(6))
        back = BACK_LON[j]
        lead = 8 if BACK_LAT[j] else 0
        for r in range(TILES):
            q = q_ref[k, j, 8 * r : 8 * r + 8, :]
            one = pltpu.roll(q, 1 if back else WIDTH - 1, 1)
            two = pltpu.roll(q, 2 if back else WIDTH - 2, 1)
            place = 2 * (TILES * RANK[j] + r)
            shift = (-place if back else WIDTH - 2 - place) % WIDTH
            fix = fix_back if back else fix_ahead
            fix = fix if shift == 0 else pltpu.roll(fix, shift, 1)
            x = c0 * q + c1 * one + c2 * two + jnp.where(at_start if back else at_end, fix, 0.0)
            x_ref[j, lead + 8 * r : lead + 8 * r + 8, :] = x
            if BACK_LAT[j] and r == 0:
                x_ref[j, 0:8, :] = jnp.broadcast_to(x[0:1, :], (8, WIDTH))
            if not BACK_LAT[j] and r == TILES - 1:
                x_ref[j, LAT : LAT + 8, :] = jnp.broadcast_to(x[7:8, :], (8, WIDTH))
        sign = -1 if BACK_LAT[j] else 1
        for r in range(TILES):
            at = lead + 8 * r
            y = (
                d0 * x_ref[j, at : at + 8, :]
                + d1 * x_ref[j, at + sign : at + sign + 8, :]
                + d2 * x_ref[j, at + 2 * sign : at + 2 * sign + 8, :]
            )
            spec = spec_ref[k, j, 8 * r : 8 * r + 8, :]
            y = jnp.where(held[r], spec, jnp.maximum(y, 0.0)) * sea[r]
            p_ref[j, 8 * r : 8 * r + 8, :] = y
            slope[r] = slope[r] + y
            stress[r] = stress[r] + y * drive_ref[j, 8 * r : 8 * r + 8, :]

    extra = base + 6 * ND
    for r in range(TILES):
        rows = slice(8 * r, 8 * r + 8)
        sums_ref[ND, rows, :] += slope[r] * scal_ref[extra + 2]
        sums_ref[ND + 1, rows, :] += stress[r] * scal_ref[extra + 3]
        p = [p_ref[j, rows, :] for j in range(ND)]
        for j, saturation in enumerate(saturation_of(p)):
            capped = jnp.maximum(saturation, SATURATION_REF)
            excess = capped * lax.rsqrt(capped) - ROOT_REF
            excess = excess * excess
            lower = sums_ref[j, rows, :]
            rate = excess * scal_ref[extra] + lower * scal_ref[extra + 1]
            sums_ref[j, rows, :] = lower + excess
            out_ref[k, j, rows, :] = p_ref[j, rows, :] * jnp.exp2(rate)


def pair_kernel(sums_ref, other_ref, out_ref):
    first = (lax.axis_index("freq") % 2) * HALF
    for i in range(HALF):
        out_ref[i] = sums_ref[first + i] + other_ref[first + i]
    for i in range(2):
        out_ref[HALF + i] = sums_ref[ND + i] + other_ref[ND + i]


def growth_kernel(
    last,
    scal_ref,
    part_ref,
    sums_ref,
    other_ref,
    mine_ref,
    rest_ref,
    east_ref,
    north_ref,
    land_ref,
    out_ref,
    *refs,
):
    rate_ref = refs[2]
    bands = part_ref.shape[0]
    freq = lax.axis_index("freq")
    core = freq % 2
    odd = jnp.where(core == 1, 1.0, 0.0)
    upper = jnp.where(freq >= 2, 1.0, 0.0)
    for r in range(TILES):
        rows = slice(8 * r, 8 * r + 8)
        ice = jnp.where(land_ref[rows, :] == 2, 1.0, 0.0)
        slope = (sums_ref[ND, rows, :] + other_ref[ND, rows, :]) + mine_ref[HALF, rows, :]
        stress = (sums_ref[ND + 1, rows, :] + other_ref[ND + 1, rows, :]) + mine_ref[
            HALF + 1, rows, :
        ]
        if last:
            refs[0][rows, :] = slope
        gain = GROWTH * (1.0 + stress / (stress + 1.0))
        damp = SWELL_DAMP * (slope / (slope + 1.0)) + ICE_DAMP * ice
        for j in range(ND):
            local = j % HALF
            near, far = mine_ref[local, rows, :], rest_ref[local, rows, :]
            in_mine = core == (0 if j < HALF else 1)
            lower = odd * other_ref[j, rows, :] + upper * jnp.where(in_mine, near, far)
            drive = wind_drive_of(j, r, east_ref, north_ref, 1.0 - ice)
            rate_ref[j, rows, :] = gain * drive - damp - (CUMULATIVE / NF) * lower

    if last:
        field_ref, sent = refs[3], refs[4]

        def send(k):
            return pltpu.make_async_copy(field_ref.at[k], out_ref.at[k], sent.at[k])

    def step(k, carry):
        root = scal_ref[(freq * bands + k) * STRIDE + 6 * ND + 4]
        target = field_ref if last else out_ref

        def tile(j, r):
            rows = slice(8 * r, 8 * r + 8)
            value = part_ref[k, j, rows, :] * jnp.exp2(rate_ref[j, rows, :] * root)
            target[k, j, rows, :] = value
            return value

        if last:
            for j in range(ND):
                for r in range(TILES):
                    tile(j, r)
            send(k).start()
        else:
            pack_edges(tile, k, refs[0], refs[1])
        return carry

    lax.fori_loop(0, bands, step, 0)
    if last:
        for k in range(bands):
            send(k).wait()


def per_device(spectrum, east_wind, north_wind, land_sea, edge_rows):
    bands, count, lat_rows, width = spectrum.shape
    assert (count, lat_rows, width) == (ND, LAT, WIDTH)
    ring = lax.axis_size("lon")
    assert lax.axis_size("freq") == 4 and bands * 4 == NF
    f32 = jnp.float32
    field = jax.ShapeDtypeStruct(spectrum.shape, f32)
    edges = jax.ShapeDtypeStruct((bands, 8, WIDTH), f32)
    sums = jax.ShapeDtypeStruct((ND + 2, LAT, WIDTH), f32)
    halves = jax.ShapeDtypeStruct((HALF + 2, LAT, WIDTH), f32)
    plane = jax.ShapeDtypeStruct((LAT, WIDTH), f32)
    smem = pl.BlockSpec(memory_space=pltpu.SMEM)
    vmem = pl.BlockSpec(memory_space=pltpu.VMEM)
    hbm = pl.BlockSpec(memory_space=pltpu.HBM)
    params = pltpu.CompilerParams(vmem_limit_bytes=24 * 1024 * 1024)
    scalars, edge_table = jnp.asarray(SCALARS), jnp.asarray(EDGE)
    swap_core = [(0, 1), (1, 0), (2, 3), (3, 2)]
    swap_chip = [(0, 2), (2, 0), (1, 3), (3, 1)]

    spectrum, right, left = pl.pallas_call(
        pack_kernel,
        in_specs=[hbm],
        out_specs=[vmem] * 3,
        out_shape=[field, edges, edges],
        scratch_shapes=[pltpu.SemaphoreType.DMA((bands,))],
        compiler_params=params,
        name="pack_columns",
    )(pltpu.with_memory_space_constraint(spectrum, pltpu.HBM))

    energy = spectrum
    for step in range(STEPS):
        last = step == STEPS - 1
        from_left = lax.ppermute(right, "lon", [(i, (i + 1) % ring) for i in range(ring)])
        from_right = lax.ppermute(left, "lon", [((i + 1) % ring, i) for i in range(ring)])
        part, mine = pl.pallas_call(
            source_kernel,
            in_specs=[smem] + [vmem] * 11,
            out_specs=[vmem] * 2,
            out_shape=[field, sums],
            scratch_shapes=[
                pltpu.VMEM((ND, LAT, WIDTH), f32),
                pltpu.VMEM((ND, LAT + 8, WIDTH), f32),
                pltpu.VMEM((ND, LAT, WIDTH), f32),
            ],
            compiler_params=params,
            name="propagate_and_break",
        )(
            scalars, edge_table, energy, spectrum, from_left, from_right, right, left,
            east_wind, north_wind, land_sea, edge_rows,
        )
        other = lax.ppermute(mine, "freq", swap_core)
        pair = pl.pallas_call(
            pair_kernel,
            in_specs=[vmem] * 2,
            out_specs=vmem,
            out_shape=halves,
            compiler_params=params,
            name="pair_sums",
        )(mine, other)
        near = lax.ppermute(pair, "freq", swap_chip)
        far = lax.ppermute(near, "freq", swap_core)
        scratch = [pltpu.VMEM((ND, LAT, WIDTH), f32)]
        if last:
            scratch += [pltpu.VMEM(spectrum.shape, f32), pltpu.SemaphoreType.DMA((bands,))]
        more = [plane, plane] if last else [edges, edges]
        energy, *more = pl.pallas_call(
            functools.partial(growth_kernel, last),
            in_specs=[smem] + [vmem] * 8,
            out_specs=[hbm if last else vmem, vmem, vmem],
            out_shape=[field] + more,
            scratch_shapes=scratch,
            compiler_params=params,
            name="grow",
        )(scalars, part, mine, other, near, far, east_wind, north_wind, land_sea)
        if not last:
            right, left = more
    return energy, more[0]


def solution(mesh):
    in_specs = (
        P("freq", None, None, "lon"),
        P(None, "lon"),
        P(None, "lon"),
        P(None, "lon"),
        P(None, "lon"),
    )
    out_specs = (P("freq", None, None, "lon"), P(None, "lon"))
    return jax.shard_map(
        per_device, mesh=mesh, in_specs=in_specs, out_specs=out_specs, check_vma=False
    )
```

```python
import functools
import math

import jax
import jax.numpy as jnp
import numpy as np
from jax import lax
from jax.experimental import pallas as pl
from jax.experimental.pallas import tpu as pltpu
from jax.sharding import PartitionSpec as P

NF = 32
STEPS = 2

COURANT_MAX = 0.9
FREQ_RATIO = 1.1
WIND_REF = 8.0
WIND_CLIP = 2.0
GROWTH = 0.01
BREAKING = 0.3
SATURATION_REF = 0.4
CUMULATIVE = 2.0
SWELL_DAMP = 0.1
ICE_DAMP = 0.5

ND = 36
HALF = ND // 2
QUARTER = ND // 4
DTHETA = 2.0 * math.pi / ND
LOG2E = 1.0 / math.log(2.0)
ROOT_REF = math.sqrt(SATURATION_REF)
TILES = 3
LAT = 8 * TILES
WIDTH = 128
STRIDE = 6 * ND + 8

ANGLES = np.arange(ND) * DTHETA
COS = np.cos(ANGLES)
SIN = np.sin(ANGLES)
COS2 = np.cos(2.0 * ANGLES)
SIN2 = np.sin(2.0 * ANGLES)
BACK_LON = [bool(c >= 0.0) for c in COS]
BACK_LAT = [bool(s >= 0.0) for s in SIN]
RANK = [sum(BACK_LON[:j]) if BACK_LON[j] else j - sum(BACK_LON[:j]) for j in range(ND)]


def one_sided(courant):
    c = np.abs(courant)
    return 1.0 - 1.5 * c + 0.5 * c * c, 2.0 * c - c * c, 0.5 * c * c - 0.5 * c


GROUP = 32
BANDS = 8
PACKED = ND + 1
SENT = HALF + QUARTER + 1
FIELDS = 5
SLOPE_AT = ND * TILES
STRESS_AT = SLOPE_AT + TILES
PACKED_AT = STRESS_AT + TILES
PACKED_SUMS = 5
SUMS = PACKED_AT + PACKED_SUMS
HALF_SUMS = HALF * TILES + 2 * TILES + PACKED_SUMS


def make_tables():
    ratios = FREQ_RATIO ** np.arange(NF)
    root = np.sqrt(ratios)
    lon = one_sided(COURANT_MAX * COS[None, :] / ratios[:, None])
    lat = one_sided(0.5 * COURANT_MAX * SIN[None, :] / ratios[:, None])
    scalars = np.zeros((NF, STRIDE))
    for i in range(3):
        scalars[:, i : 6 * ND : 6] = lon[i]
        scalars[:, 3 + i : 6 * ND : 6] = lat[i]
    rest = [
        -BREAKING / SATURATION_REF * root,
        -CUMULATIVE / NF * root,
        ratios * ratios * DTHETA / np.sum(ratios * ratios),
        ratios * root * DTHETA / np.sum(ratios * root),
        root,
    ]
    packed = np.zeros((NF // BANDS, PACKED, 8, WIDTH))
    for i, value in enumerate(rest):
        scalars[:, 6 * ND + i] = value
    for lane in range(TILES * GROUP):
        slot, k = lane % 4, lane // 4 % BANDS
        for i in range(3):
            packed[:, :ND, i, lane] = lon[i][k::BANDS]
            packed[:, :ND, 3 + i, lane] = lat[i][k::BANDS]
        for j in range(ND):
            if slot == (0 if BACK_LON[j] else 3):
                packed[:, j, 6, lane] = lon[1][k::BANDS, j]
        for i, value in enumerate(rest):
            packed[:, ND, i, lane] = value[k::BANDS]
    return scalars.reshape(-1).astype(np.float32), packed.astype(np.float32)


SCALARS, PACKED_TABLE = make_tables()


def lanes():
    return lax.broadcasted_iota(jnp.int32, (8, WIDTH), 1)


def sublanes():
    return lax.broadcasted_iota(jnp.int32, (8, WIDTH), 0)


def turn(tile, shift):
    shift = shift % WIDTH
    return tile if shift == 0 else pltpu.roll(tile, shift, 1)


def tile_rows(r):
    return slice(8 * r, 8 * r + 8)


CHUNK = 4


def pack_kernel(spec_ref, *refs):
    sources, (copy_ref, right_ref, left_ref), held_refs = refs[:4], refs[4:7], refs[7:11]
    arrived = refs[11]

    def fetch(c):
        part = pl.ds(CHUNK * c, CHUNK)
        return pltpu.make_async_copy(spec_ref.at[:, part], copy_ref.at[:, part], arrived.at[c])

    small = [
        pltpu.make_async_copy(source, target, arrived.at[ND // CHUNK + i])
        for i, (source, target) in enumerate(zip(sources, held_refs))
    ]
    for c in range(ND // CHUNK):
        fetch(c).start()
    for copy in small:
        copy.start()
    lane = lanes()
    zero = jnp.zeros((8, WIDTH), jnp.float32)
    held = [zero, zero]
    for j in range(ND):
        if j % CHUNK == 0:
            fetch(j // CHUNK).wait()
        wide, narrow = (right_ref, left_ref) if BACK_LON[j] else (left_ref, right_ref)
        half = RANK[j] % 2
        four = zero
        two = zero
        for r in range(TILES):
            for k in range(BANDS):
                tile = copy_ref[k, j, tile_rows(r), :]
                place = GROUP * r + 4 * k
                first, pair = (WIDTH - 4, 0) if BACK_LON[j] else (0, WIDTH - 2)
                four = jnp.where(lane // 4 == place // 4, turn(tile, place - first), four)
                place = place + 2 * half
                two = jnp.where(lane // 2 == place // 2, turn(tile, place - pair), two)
        wide[RANK[j]] = four
        if half:
            slot = lane % 4 < 2
            two = jnp.where(slot, held[BACK_LON[j]], two)
            narrow[HALF + RANK[j] // 2] = two
        else:
            held[BACK_LON[j]] = two
    for copy in small:
        copy.wait()
    east_ref, north_ref, land_ref, rows_ref = held_refs
    fields = [
        [f(r) for r in range(TILES)]
        for f in (
            lambda r: east_ref[tile_rows(r), :],
            lambda r: north_ref[tile_rows(r), :],
            lambda r: land_ref[tile_rows(r), :].astype(jnp.float32),
            lambda r: jnp.broadcast_to(rows_ref[0:1, :].astype(jnp.float32), (8, WIDTH)),
            lambda r: jnp.broadcast_to(rows_ref[1:2, :].astype(jnp.float32), (8, WIDTH)),
        )
    ]
    to_right, to_left = zero, zero
    for i in range(FIELDS):
        for r in range(TILES):
            place = GROUP * r + 4 * i
            here = lane // 2 == place // 2
            to_right = jnp.where(here, turn(fields[i][r], place - (WIDTH - 2)), to_right)
            to_left = jnp.where(here, turn(fields[i][r], place), to_left)
    right_ref[SENT - 1] = to_right
    left_ref[SENT - 1] = to_left


def wind_drive_of(j, r, east_ref, north_ref, open_water):
    rows = tile_rows(r)
    along = float(COS[j]) * east_ref[rows, :] + float(SIN[j]) * north_ref[rows, :]
    drive = jnp.minimum(jnp.maximum(along, 0.0) / WIND_REF, WIND_CLIP)
    return drive * drive * open_water


def saturation_of(p):
    half = 0.5 * DTHETA
    diff = [p[b] - p[b + HALF] for b in range(HALF)]
    both = [p[b] + p[b + HALF] for b in range(HALF)]
    total = both[0]
    for b in range(1, HALF):
        total = total + both[b]
    total = total * (0.5 * half)
    fold = [both[b] - both[b + QUARTER] for b in range(QUARTER)]
    total_c = fold[0] * float(0.5 * half * COS2[0])
    total_s = None
    for b in range(1, QUARTER):
        total_c = total_c + fold[b] * float(0.5 * half * COS2[b])
        term = fold[b] * float(0.5 * half * SIN2[b])
        total_s = term if total_s is None else total_s + term
    diff = [d * half for d in diff]
    diff_c = [diff[b] * float(COS2[b]) for b in range(HALF)]
    diff_s = [diff[b] * float(SIN2[b]) for b in range(HALF)]

    def start(x):
        front = x[0]
        for b in range(1, QUARTER):
            front = front + x[b]
        rear = x[QUARTER]
        for b in range(QUARTER + 1, HALF):
            rear = rear + x[b]
        return 0.5 * (front - rear)

    win, win_c, win_s = start(diff), start(diff_c), start(diff_s)
    out = [None] * ND
    level = [None] * HALF
    for a in range(QUARTER):
        turn = total_c * float(COS2[a])
        if a:
            turn = turn + total_s * float(SIN2[a])
        level[a] = total + turn
        level[a + QUARTER] = total - turn
    for a in range(HALF):
        odd = win + win_c * float(COS2[a])
        if a:
            odd = odd + win_s * float(SIN2[a])
        out[a] = level[a] + odd
        out[a + HALF] = level[a] - odd
        new = a + QUARTER
        if a + 1 < HALF:
            if new < HALF:
                win, win_c, win_s = win + diff[new], win_c + diff_c[new], win_s + diff_s[new]
            else:
                new -= HALF
                win, win_c, win_s = win - diff[new], win_c - diff_c[new], win_s - diff_s[new]
    return out


def drift_kernel(scal_ref, q_ref, out_ref, x_ref):
    bands = q_ref.shape[0]
    lane = lanes()
    one = jnp.ones((8, WIDTH), jnp.float32)
    inside = {
        (True, 1): jnp.where(lane >= 1, one, 0.0),
        (True, 2): jnp.where(lane >= 2, one, 0.0),
        (False, 1): jnp.where(lane < WIDTH - 1, one, 0.0),
        (False, 2): jnp.where(lane < WIDTH - 2, one, 0.0),
    }

    def band(k, carry):
        base = (lax.axis_index("freq") * bands + k) * STRIDE
        for j in range(ND):
            c0, c1, c2, d0, d1, d2 = (scal_ref[base + 6 * j + i] for i in range(6))
            side = 1 if BACK_LON[j] else -1
            c1 = c1 * inside[BACK_LON[j], 1]
            c2 = c2 * inside[BACK_LON[j], 2]
            lead = 8 if BACK_LAT[j] else 0
            for r in range(TILES):
                q = q_ref[k, j, tile_rows(r), :]
                x = c0 * q + c1 * turn(q, side) + c2 * turn(q, 2 * side)
                x_ref[j, lead + 8 * r : lead + 8 * r + 8, :] = x
                if BACK_LAT[j] and r == 0:
                    x_ref[j, 0:8, :] = jnp.broadcast_to(x[0:1, :], (8, WIDTH))
                if not BACK_LAT[j] and r == TILES - 1:
                    x_ref[j, LAT : LAT + 8, :] = jnp.broadcast_to(x[7:8, :], (8, WIDTH))
            sign = -1 if BACK_LAT[j] else 1
            for r in range(TILES):
                at = lead + 8 * r
                out_ref[k, j, tile_rows(r), :] = (
                    d0 * x_ref[j, at : at + 8, :]
                    + d1 * x_ref[j, at + sign : at + sign + 8, :]
                    + d2 * x_ref[j, at + 2 * sign : at + 2 * sign + 8, :]
                )
        return carry

    lax.fori_loop(0, bands, band, 0)


def packed_lat(j, x, d0, d1, d2):
    lane, row = lanes(), sublanes()

    def shifted(x):
        if BACK_LAT[j]:
            moved = pltpu.roll(x, 1, 0)
            over = jnp.where(lane < GROUP, x, turn(moved, GROUP))
            return jnp.where(row >= 1, moved, over)
        moved = pltpu.roll(x, 7, 0)
        over = jnp.where(lane >= (TILES - 1) * GROUP, x, turn(moved, -GROUP))
        return jnp.where(row <= 6, moved, over)

    near = shifted(x)
    return d0 * x + d1 * near + d2 * shifted(near)


def spread(tile, position):
    at_first = lanes() // 4 % BANDS == 0
    tile = jnp.where(at_first, turn(tile, -4 * position), 0.0)
    for step in (1, 2, 4):
        tile = tile + turn(tile, 4 * step)
    return tile


def packed_fix(freq, table_ref, columns_ref, fix_ref):
    for j in range(ND):
        row = [table_ref[freq, j, i : i + 1, :] for i in range(7)]
        tile = columns_ref[j]
        first = row[2] * tile + row[6] * turn(tile, -1 if BACK_LON[j] else 1)
        fix_ref[j] = packed_lat(j, first, *row[3:6])


def packed_start(mine_right_ref, mine_left_ref, left_ref, right_ref, columns_ref, side_refs):
    near_ref, far_ref = side_refs
    lane = lanes()
    slot = lane % 4
    for j in range(ND):
        half = RANK[j] % 2
        narrow = HALF + RANK[j] // 2
        if BACK_LON[j]:
            wide, own = left_ref[RANK[j]], mine_right_ref[RANK[j]]
            other = turn(right_ref[narrow], 2 - 2 * half)
            centre = jnp.where(slot < 2, turn(wide, -2), other)
            near = jnp.where(slot == 2, turn(own, -1), turn(centre, 1))
            near = jnp.where(slot < 2, turn(wide, -1), near)
            far = jnp.where(slot < 2, wide, own)
        else:
            wide, own = right_ref[RANK[j]], mine_left_ref[RANK[j]]
            other = turn(left_ref[narrow], -2 * half)
            centre = jnp.where(slot < 2, other, turn(wide, 2))
            near = jnp.where(slot == 1, turn(own, 1), turn(centre, -1))
            near = jnp.where(slot >= 2, turn(wide, 1), near)
            far = jnp.where(slot < 2, own, wide)
        used = lane < TILES * GROUP
        columns_ref[j] = jnp.where(used, centre, 0.0)
        near_ref[j] = jnp.where(used, near, 0.0)
        far_ref[j] = jnp.where(used, far, 0.0)


def packed_source(
    freq, table_ref, left_ref, right_ref, columns_ref, side_refs,
    sums_ref, part_ref, drive_ref, ice_ref, p_ref,
):
    near_ref, far_ref = side_refs
    lane = lanes()
    slot, place = lane % 4, lane // 4 % BANDS
    both = jnp.where(slot < 2, left_ref[SENT - 1], turn(right_ref[SENT - 1], 2))
    east, north, land, south_rows, north_rows = (spread(both, i) for i in range(FIELDS))
    row = lane // GROUP * 8 + sublanes()
    row = row.astype(jnp.float32)
    held = (row < south_rows) | (row >= LAT - north_rows)
    sea = jnp.where(land > 0.5, 1.0, 0.0)
    ice = jnp.where(land > 1.5, 1.0, 0.0)
    ice_ref[...] = ice
    slope = jnp.zeros((8, WIDTH), jnp.float32)
    stress = slope
    for j in range(ND):
        coef = [table_ref[freq, j, i : i + 1, :] for i in range(6)]
        centre = columns_ref[j]
        x = coef[0] * centre + coef[1] * near_ref[j] + coef[2] * far_ref[j]
        x = packed_lat(j, x, *coef[3:])
        p = jnp.where(held, centre, jnp.maximum(x, 0.0)) * sea
        along = float(COS[j]) * east + float(SIN[j]) * north
        drive = jnp.minimum(jnp.maximum(along, 0.0) / WIND_REF, WIND_CLIP)
        drive = drive * drive * (1.0 - ice)
        drive_ref[j] = drive
        p_ref[j] = p
        slope = slope + p
        stress = stress + p * drive
    coef = [table_ref[freq, ND, i : i + 1, :] for i in range(5)]

    def running(tile):
        for step in (1, 2, 4):
            tile = tile + jnp.where(place >= step, turn(tile, 4 * step), 0.0)
        return tile

    out = [jnp.zeros((8, WIDTH), jnp.float32) for _ in range(PACKED_SUMS)]

    def put(index, tile):
        position = index % BANDS
        moved = turn(tile, 4 * (position - (BANDS - 1)))
        out[index // BANDS] = jnp.where(place == position, moved, out[index // BANDS])

    for j, excess in enumerate(excess_of([p_ref[j] for j in range(ND)])):
        total = running(excess)
        put(j, total)
        rate = excess * coef[0] + (total - excess) * coef[1]
        part_ref[j] = p_ref[j] * jnp.exp(rate)
    put(ND, running(slope * coef[2]))
    put(ND + 1, running(stress * coef[3]))
    for i in range(PACKED_SUMS):
        sums_ref[PACKED_AT + i] = out[i]


def excess_of(p):
    out = []
    for saturation in saturation_of(p):
        capped = jnp.maximum(saturation, SATURATION_REF)
        excess = capped * lax.rsqrt(capped) - ROOT_REF
        out.append(excess * excess)
    return out


def source_kernel(first, *refs):
    scal_ref, table_ref, x_ref, spec_ref, east_ref, north_ref, land_ref, rows_ref = refs[:8]
    refs = refs[8:]
    freq = lax.axis_index("freq")
    bands = x_ref.shape[0]
    if first:
        mine_right_ref, mine_left_ref, left_ref, right_ref = refs[:4]
        p_ref, excess_ref, sums_ref, part_ref, packed_drive_ref, ice_ref = refs[4:10]
        drive_ref, fix_ref, columns_ref, near_ref, far_ref, packed_ref = refs[10:]
        sides = (near_ref, far_ref)
        packed_start(mine_right_ref, mine_left_ref, left_ref, right_ref, columns_ref, sides)
        packed_source(
            freq, table_ref, left_ref, right_ref, columns_ref, sides,
            sums_ref, part_ref, packed_drive_ref, ice_ref, packed_ref,
        )
    else:
        columns_ref, p_ref, excess_ref, sums_ref, drive_ref, fix_ref = refs
        for i in range(PACKED_SUMS):
            sums_ref[PACKED_AT + i] = jnp.zeros((8, WIDTH), jnp.float32)
    packed_fix(freq, table_ref, columns_ref, fix_ref)
    for i in range(PACKED_AT):
        sums_ref[i] = jnp.zeros((8, WIDTH), jnp.float32)
    for r in range(TILES):
        water = jnp.where(land_ref[tile_rows(r), :] == 2, 0.0, 1.0)
        for j in range(ND):
            drive_ref[j, tile_rows(r), :] = wind_drive_of(j, r, east_ref, north_ref, water)

    lane = lanes()
    at_edge = {True: lane < 2, False: lane >= WIDTH - 2}

    def band(k, carry):
        extra = (freq * bands + k) * STRIDE + 6 * ND
        for r in range(TILES):
            rows = tile_rows(r)
            row = sublanes() + 8 * r
            held = (row < rows_ref[0:1, :]) | (row >= LAT - rows_ref[1:2, :])
            sea = jnp.where(land_ref[rows, :] != 0, 1.0, 0.0)
            slope = jnp.zeros((8, WIDTH), jnp.float32)
            stress = slope
            shift = {
                True: jnp.bitwise_and(WIDTH - GROUP * r - 4 * k, WIDTH - 1),
                False: WIDTH - 4 - GROUP * r - 4 * k,
            }
            for j in range(ND):
                back = BACK_LON[j]
                moved = pltpu.roll(fix_ref[j], shift[back], 1)
                p = x_ref[k, j, rows, :] + jnp.where(at_edge[back], moved, 0.0)
                p = jnp.where(held, spec_ref[k, j, rows, :], jnp.maximum(p, 0.0)) * sea
                p_ref[k, j, rows, :] = p
                slope = slope + p
                stress = stress + p * drive_ref[j, rows, :]
            sums_ref[SLOPE_AT + r] += slope * scal_ref[extra + 2]
            sums_ref[STRESS_AT + r] += stress * scal_ref[extra + 3]
            for j, excess in enumerate(excess_of([p_ref[k, j, rows, :] for j in range(ND)])):
                excess_ref[k, j, rows, :] = excess
                sums_ref[TILES * j + r] += excess
        return carry

    lax.fori_loop(0, bands, band, 0)


def local_kernel(scal_ref, p_ref, excess_ref, out_ref):
    bands = p_ref.shape[0]
    first = (lax.axis_index("freq") * bands) * STRIDE + 6 * ND

    def direction(j, carry):
        for r in range(TILES):
            rows = tile_rows(r)
            lower = jnp.zeros((8, WIDTH), jnp.float32)
            for k in range(bands):
                excess = excess_ref[k, j, rows, :]
                at = first + k * STRIDE
                rate = excess * scal_ref[at] + lower * scal_ref[at + 1]
                out_ref[k, j, rows, :] = p_ref[k, j, rows, :] * jnp.exp(rate)
                lower = lower + excess
        return carry

    lax.fori_loop(0, ND, direction, 0)


def pair_kernel(sums_ref, other_ref, out_ref):
    count = HALF * TILES
    first = (lax.axis_index("freq") % 2) * count
    for i in range(count):
        out_ref[i] = sums_ref[first + i] + other_ref[first + i]
    for i in range(HALF_SUMS - count):
        out_ref[count + i] = sums_ref[SLOPE_AT + i] + other_ref[SLOPE_AT + i]


def damp_and_gain(slope, stress, ice):
    damp = SWELL_DAMP * (slope / (slope + 1.0)) + ICE_DAMP * ice
    return damp, GROWTH * (1.0 + stress / (stress + 1.0))


def growth_kernel(last, *refs):
    scal_ref, part_ref, sums_ref, other_ref, mine_ref, rest_ref = refs[:6]
    east_ref, north_ref, land_ref = refs[6:9]
    bands = part_ref.shape[0]
    freq = lax.axis_index("freq")
    core = freq % 2
    odd = jnp.where(core == 1, 1.0, 0.0)
    upper = jnp.where(freq >= 2, 1.0, 0.0)
    after = SLOPE_AT - HALF * TILES
    if last:
        out_ref, slope_ref, rate_ref, field_ref, sent = refs[9:]
    else:
        table_ref, packed_part_ref, packed_drive_ref, ice_ref = refs[9:13]
        out_ref, columns_ref, rate_ref = refs[13:]
        coef = table_ref[freq, ND, 4:5, :]
        total, lower = [], []
        for i in range(PACKED_AT, SUMS):
            total.append((sums_ref[i] + other_ref[i]) + mine_ref[i - after])
            lower.append(odd * other_ref[i] + upper * mine_ref[i - after])
        slope, stress = (spread(total[i // BANDS], i % BANDS) for i in (ND, ND + 1))
        damp, gain = damp_and_gain(slope, stress, ice_ref[...])
        for j in range(ND):
            under = spread(lower[j // BANDS], j % BANDS)
            rate = gain * packed_drive_ref[j] - damp - (CUMULATIVE / NF) * under
            columns_ref[j] = packed_part_ref[j] * jnp.exp(coef * rate)
    for r in range(TILES):
        rows = tile_rows(r)
        ice = jnp.where(land_ref[rows, :] == 2, 1.0, 0.0)
        slope, stress = (
            (sums_ref[at + r] + other_ref[at + r]) + mine_ref[at + r - after]
            for at in (SLOPE_AT, STRESS_AT)
        )
        if last:
            slope_ref[rows, :] = slope
        damp, gain = damp_and_gain(slope, stress, ice)
        for j in range(ND):
            local = (j % HALF) * TILES + r
            near, far = mine_ref[local], rest_ref[local]
            in_mine = core == (0 if j < HALF else 1)
            lower = odd * other_ref[TILES * j + r] + upper * jnp.where(in_mine, near, far)
            drive = wind_drive_of(j, r, east_ref, north_ref, 1.0 - ice)
            rate_ref[j, rows, :] = gain * drive - damp - (CUMULATIVE / NF) * lower

    def send(k):
        return pltpu.make_async_copy(field_ref.at[k], out_ref.at[k], sent.at[k])

    def band(k, carry):
        root = scal_ref[(freq * bands + k) * STRIDE + 6 * ND + 4]
        target = field_ref if last else out_ref
        for j in range(ND):
            for r in range(TILES):
                rows = tile_rows(r)
                factor = jnp.exp(rate_ref[j, rows, :] * root)
                target[k, j, rows, :] = part_ref[k, j, rows, :] * factor
        if last:
            send(k).start()
        return carry

    lax.fori_loop(0, bands, band, 0)
    if last:
        for k in range(bands):
            send(k).wait()


def cost(tiles, ops, moves):
    return pl.CostEstimate(
        flops=tiles * ops * 8 * WIDTH, bytes_accessed=tiles * moves * 32 * WIDTH, transcendentals=0
    )


def per_device(spectrum, east_wind, north_wind, land_sea, edge_rows):
    bands, count, lat_rows, width = spectrum.shape
    assert (bands, count, lat_rows, width) == (BANDS, ND, LAT, WIDTH)
    ring = lax.axis_size("lon")
    assert lax.axis_size("freq") == 4 and bands * 4 == NF
    f32 = jnp.float32

    def tiles(count):
        return jax.ShapeDtypeStruct((count, 8, WIDTH), f32)

    field = jax.ShapeDtypeStruct(spectrum.shape, f32)
    plane = jax.ShapeDtypeStruct((LAT, WIDTH), f32)
    tile = jax.ShapeDtypeStruct((8, WIDTH), f32)
    smem = pl.BlockSpec(memory_space=pltpu.SMEM)
    vmem = pl.BlockSpec(memory_space=pltpu.VMEM)
    hbm = pl.BlockSpec(memory_space=pltpu.HBM)
    params = pltpu.CompilerParams(vmem_limit_bytes=16 * 1024 * 1024)
    scalars, table = jnp.asarray(SCALARS), jnp.asarray(PACKED_TABLE)
    swap_core = [(0, 1), (1, 0), (2, 3), (3, 2)]
    swap_chip = [(0, 2), (2, 0), (1, 3), (3, 1)]
    whole = bands * ND * TILES
    by_direction = pltpu.VMEM((ND, LAT, WIDTH), f32)
    packed = pltpu.VMEM((ND, 8, WIDTH), f32)

    arguments = [spectrum, east_wind, north_wind, land_sea, edge_rows]
    spectrum, right, left, east_wind, north_wind, land_sea, edge_rows = pl.pallas_call(
        pack_kernel,
        in_specs=[hbm] * 5,
        out_specs=[vmem] * 7,
        out_shape=[field, tiles(SENT), tiles(SENT)]
        + [jax.ShapeDtypeStruct(x.shape, x.dtype) for x in arguments[1:]],
        scratch_shapes=[pltpu.SemaphoreType.DMA((ND // CHUNK + 4,))],
        compiler_params=params,
        cost_estimate=cost(whole, 6, 2),
        name="pack_columns",
    )(*(pltpu.with_memory_space_constraint(x, pltpu.HBM) for x in arguments))
    from_left = lax.ppermute(right, "lon", [(i, (i + 1) % ring) for i in range(ring)])
    from_right = lax.ppermute(left, "lon", [((i + 1) % ring, i) for i in range(ring)])

    energy = spectrum
    for step in range(STEPS):
        first, last = step == 0, step == STEPS - 1
        drifted = pl.pallas_call(
            drift_kernel,
            in_specs=[smem, vmem],
            out_specs=vmem,
            out_shape=field,
            scratch_shapes=[pltpu.VMEM((ND, LAT + 8, WIDTH), f32)],
            compiler_params=params,
            cost_estimate=cost(whole, 12, 2),
            name="drift",
        )(scalars, energy)
        operands = [scalars, table, drifted, spectrum, east_wind, north_wind, land_sea, edge_rows]
        operands += [right, left, from_left, from_right] if first else [columns]
        p, excess, mine, *packed_state = pl.pallas_call(
            functools.partial(source_kernel, first),
            in_specs=[smem] + [vmem] * (len(operands) - 1),
            out_specs=[vmem] * (6 if first else 3),
            out_shape=[field, field, tiles(SUMS)] + ([tiles(ND), tiles(ND), tile] if first else []),
            scratch_shapes=[by_direction, packed] + ([packed] * 4 if first else []),
            compiler_params=params,
            cost_estimate=cost(whole, 30, 3),
            name="sources",
        )(*operands)
        other = lax.ppermute(mine, "freq", swap_core)
        pair = pl.pallas_call(
            pair_kernel,
            in_specs=[vmem] * 2,
            out_specs=vmem,
            out_shape=tiles(HALF_SUMS),
            compiler_params=params,
            cost_estimate=cost(HALF_SUMS, 1, 3),
            name="pair_sums",
        )(mine, other)
        near = lax.ppermute(pair, "freq", swap_chip)
        excess, _ = lax.optimization_barrier((excess, pair))
        part = pl.pallas_call(
            local_kernel,
            in_specs=[smem] + [vmem] * 2,
            out_specs=vmem,
            out_shape=field,
            compiler_params=params,
            cost_estimate=cost(whole, 8, 3),
            name="local_rate",
        )(scalars, p, excess)
        near, part = lax.optimization_barrier((near, part))
        far = lax.ppermute(near, "freq", swap_core)
        operands = [scalars, part, mine, other, near, far, east_wind, north_wind, land_sea]
        scratch = [by_direction]
        if last:
            scratch += [pltpu.VMEM(spectrum.shape, f32), pltpu.SemaphoreType.DMA((bands,))]
        else:
            operands += [table] + packed_state
        energy, columns = pl.pallas_call(
            functools.partial(growth_kernel, last),
            in_specs=[smem] + [vmem] * (len(operands) - 1),
            out_specs=[hbm if last else vmem, vmem],
            out_shape=[field, plane if last else tiles(ND)],
            scratch_shapes=scratch,
            compiler_params=params,
            cost_estimate=cost(whole, 6, 2),
            name="grow",
        )(*operands)
    return energy, columns


def solution(mesh):
    in_specs = (
        P("freq", None, None, "lon"),
        P(None, "lon"),
        P(None, "lon"),
        P(None, "lon"),
        P(None, "lon"),
    )
    out_specs = (P("freq", None, None, "lon"), P(None, "lon"))
    return jax.shard_map(
        per_device, mesh=mesh, in_specs=in_specs, out_specs=out_specs, check_vma=False
    )
```

```python
import functools
import math

import jax
import jax.numpy as jnp
import numpy as np
from jax import lax
from jax.experimental import pallas as pl
from jax.experimental.pallas import tpu as pltpu
from jax.sharding import PartitionSpec as P

NF = 32
STEPS = 2

COURANT_MAX = 0.9
FREQ_RATIO = 1.1
WIND_REF = 8.0
WIND_CLIP = 2.0
GROWTH = 0.01
BREAKING = 0.3
SATURATION_REF = 0.4
CUMULATIVE = 2.0
SWELL_DAMP = 0.1
ICE_DAMP = 0.5

ND = 36
HALF = ND // 2
QUARTER = ND // 4
DTHETA = 2.0 * math.pi / ND
LOG2E = 1.0 / math.log(2.0)
ROOT_REF = math.sqrt(SATURATION_REF)
TILES = 3
LAT = 8 * TILES
WIDTH = 128
STRIDE = 6 * ND + 8

ANGLES = np.arange(ND) * DTHETA
COS = np.cos(ANGLES)
SIN = np.sin(ANGLES)
COS2 = np.cos(2.0 * ANGLES)
SIN2 = np.sin(2.0 * ANGLES)
BACK_LON = [bool(c >= 0.0) for c in COS]
BACK_LAT = [bool(s >= 0.0) for s in SIN]
RANK = [sum(BACK_LON[:j]) if BACK_LON[j] else j - sum(BACK_LON[:j]) for j in range(ND)]


def one_sided(courant):
    c = np.abs(courant)
    return 1.0 - 1.5 * c + 0.5 * c * c, 2.0 * c - c * c, 0.5 * c * c - 0.5 * c


GROUP = 32
BANDS = 8
SENT = HALF + QUARTER + 1
FIELDS = 5
SLOPE_AT = ND * TILES
STRESS_AT = SLOPE_AT + TILES
PACKED_AT = STRESS_AT + TILES
PACKED_SUMS = 5
HALF_TILES = HALF * TILES
SCALE = 0.25 * DTHETA
CAP = SATURATION_REF / SCALE
ROOT_CAP = math.sqrt(CAP)
LOWER = CUMULATIVE / NF * SCALE


def make_tables():
    ratios = FREQ_RATIO ** np.arange(NF)
    root = np.sqrt(ratios)
    lon = one_sided(COURANT_MAX * COS[None, :] / ratios[:, None])
    lat = one_sided(0.5 * COURANT_MAX * SIN[None, :] / ratios[:, None])
    scalars = np.zeros((NF, STRIDE))
    for i in range(3):
        scalars[:, i : 6 * ND : 6] = lon[i]
        scalars[:, 3 + i : 6 * ND : 6] = lat[i]
    rest = [
        -BREAKING / SATURATION_REF * SCALE * root,
        -LOWER * root,
        ratios * ratios * DTHETA / np.sum(ratios * ratios),
        ratios * root * DTHETA / np.sum(ratios * root),
        root,
        1.0 / ratios,
    ]
    packed = np.zeros((NF // BANDS, len(rest), 8, WIDTH))
    for i, value in enumerate(rest):
        scalars[:, 6 * ND + i] = value
        for lane in range(TILES * GROUP):
            packed[:, i, :, lane] = value[lane // 4 % BANDS :: BANDS, None]
    return scalars.reshape(-1).astype(np.float32), packed.astype(np.float32)


SCALARS, PACKED_TABLE = make_tables()


def lanes():
    return lax.broadcasted_iota(jnp.int32, (8, WIDTH), 1)


def sublanes():
    return lax.broadcasted_iota(jnp.int32, (8, WIDTH), 0)


def turn(tile, shift):
    shift = shift % WIDTH
    return tile if shift == 0 else pltpu.roll(tile, shift, 1)


def tile_rows(r):
    return pl.ds(r, 8, stride=TILES)


CHUNK = 4


def pack_kernel(spec_ref, *refs):
    sources, (copy_ref, right_ref, left_ref), held_refs = refs[:4], refs[4:7], refs[7:11]
    to_even_ref, to_odd_ref, arrived = refs[11:]

    def fetch(c):
        part = pl.ds(CHUNK * c, CHUNK)
        return pltpu.make_async_copy(spec_ref.at[:, part], copy_ref.at[:, part], arrived.at[c])

    small = [
        pltpu.make_async_copy(source, target, arrived.at[ND // CHUNK + i])
        for i, (source, target) in enumerate(zip(sources, held_refs))
    ]
    for c in range(ND // CHUNK):
        fetch(c).start()
    for copy in small:
        copy.start()
    lane = lanes()
    zero = jnp.zeros((8, WIDTH), jnp.float32)
    held = [zero, zero]
    for j in range(ND):
        if j % CHUNK == 0:
            fetch(j // CHUNK).wait()
        back = BACK_LON[j]
        wide, narrow = (right_ref, left_ref) if back else (left_ref, right_ref)
        half = RANK[j] % 2
        first, aside = (WIDTH - 4, 4) if back else (0, -2)
        four = zero
        two = zero
        for r in range(TILES):
            for k in range(BANDS):
                place = GROUP * r + 4 * k
                tile = turn(copy_ref[k, j, tile_rows(r), :], place - first)
                four = jnp.where(lane // 4 == place // 4, tile, four)
                two = jnp.where(lane // 2 == (place + aside) % WIDTH // 2, tile, two)
        wide[RANK[j]] = four
        two = turn(two, 2 * half - aside)
        if half:
            narrow[HALF + RANK[j] // 2] = jnp.where(lane % 4 < 2, held[back], two)
        else:
            held[back] = two
    for copy in small:
        copy.wait()
    east_ref, north_ref, land_ref, rows_ref = held_refs
    fields = [
        [f(r) for r in range(TILES)]
        for f in (
            lambda r: east_ref[tile_rows(r), :],
            lambda r: north_ref[tile_rows(r), :],
            lambda r: land_ref[tile_rows(r), :].astype(jnp.float32),
            lambda r: jnp.broadcast_to(rows_ref[0:1, :].astype(jnp.float32), (8, WIDTH)),
            lambda r: jnp.broadcast_to(rows_ref[1:2, :].astype(jnp.float32), (8, WIDTH)),
        )
    ]
    to_right, to_left = zero, zero
    for i in range(FIELDS):
        for r in range(TILES):
            place = GROUP * r + 4 * i
            here = lane // 2 == place // 2
            to_right = jnp.where(here, turn(fields[i][r], place - (WIDTH - 2)), to_right)
            to_left = jnp.where(here, turn(fields[i][r], place), to_left)
    right_ref[SENT - 1] = to_right
    left_ref[SENT - 1] = to_left
    odd = lax.axis_index("lon") % 2 == 1
    for i in range(SENT):
        right, left = right_ref[i], left_ref[i]
        to_even_ref[i] = jnp.where(odd, left, right)
        to_odd_ref[i] = jnp.where(odd, right, left)


def drive_of(j, east, north, open_water):
    along = float(COS[j]) * east + float(SIN[j]) * north
    drive = jnp.minimum(jnp.maximum(along, 0.0) / WIND_REF, WIND_CLIP)
    return drive * drive * open_water


def saturation_of(p):
    diff = [p[b] - p[b + HALF] for b in range(HALF)]
    both = [p[b] + p[b + HALF] for b in range(HALF)]
    total = both[0]
    for b in range(1, HALF):
        total = total + both[b]
    fold = [both[b] - both[b + QUARTER] for b in range(QUARTER)]
    total_c, total_s = fold[0], None
    for b in range(1, QUARTER):
        total_c = total_c + fold[b] * float(COS2[b])
        term = fold[b] * float(SIN2[b])
        total_s = term if total_s is None else total_s + term
    level = [None] * HALF
    for a in range(QUARTER):
        wave = total_c * float(COS2[a])
        if a:
            wave = wave + total_s * float(SIN2[a])
        level[a] = total + wave
        level[a + QUARTER] = total - wave

    def at(b):
        return diff[b % HALF], b // HALF % 2 == 1

    def plus(x, b):
        value, negative = at(b)
        return x - value if negative else x + value

    def minus(x, b):
        value, negative = at(b)
        return x + value if negative else x - value

    plain, waves = diff[0], []
    for a in range(2):
        wave = diff[a]
        for d in range(1, QUARTER):
            pair = minus(diff[a + d], a - d + HALF)
            wave = wave + pair * float(COS2[d])
            if a == 0:
                plain = plain + pair
        waves.append(wave)
    twice = float(2.0 * COS2[1])
    odd = [None] * HALF
    odd[0] = plain + waves[0]
    window, before, now = plain, waves[0], waves[1]
    for a in range(1, QUARTER + 1):
        window = plus(minus(window, a - 9), a + 8)
        odd[a] = window + now
        if a < QUARTER:
            step = minus(plus(twice * now - before, a + 8), a + 10)
            before, now = now, step
    window, after, now = plain, waves[1], waves[0]
    for a in range(0, -(QUARTER - 1), -1):
        step = minus(plus(twice * now - after, a + 8), a + 10)
        after, now = now, step
        window = minus(plus(window, a - 9 + 2 * HALF), a + 8)
        odd[a - 1 + HALF] = -(window + now)
    out = [None] * ND
    for a in range(HALF):
        out[a] = level[a] + odd[a]
        out[a + HALF] = level[a] - odd[a]
    return out


def inside_masks():
    lane = lanes()
    one = jnp.ones((8, WIDTH), jnp.float32)
    return {
        (True, 1): jnp.where(lane >= 1, one, 0.0),
        (True, 2): jnp.where(lane >= 2, one, 0.0),
        (False, 1): jnp.where(lane < WIDTH - 1, one, 0.0),
        (False, 2): jnp.where(lane < WIDTH - 2, one, 0.0),
    }


def drift(j, base, tiles, scal_ref, inside):
    c0, c1, c2, d0, d1, d2 = (scal_ref[base + 6 * j + i] for i in range(6))
    side = 1 if BACK_LON[j] else -1
    c1 = c1 * inside[BACK_LON[j], 1]
    c2 = c2 * inside[BACK_LON[j], 2]
    x = [c0 * q + c1 * turn(q, side) + c2 * turn(q, 2 * side) for q in tiles]
    row = sublanes()
    if BACK_LAT[j]:
        over = [jnp.where(row == 0, x[0], pltpu.roll(x[r], 1, 0)) for r in (1, 2)]
        near = [over[1], x[0], x[1]]
        far = [over[0], over[1], x[0]]
    else:
        over = [jnp.where(row == 7, x[2], pltpu.roll(x[r], 7, 0)) for r in (0, 1)]
        near = [x[1], x[2], over[0]]
        far = [x[2], over[0], over[1]]
    return [d0 * x[r] + d1 * near[r] + d2 * far[r] for r in range(TILES)]


def drift_kernel(scal_ref, q_ref, out_ref):
    bands = q_ref.shape[0]
    inside = inside_masks()

    def band(k, carry):
        base = (lax.axis_index("freq") * bands + k) * STRIDE
        for j in range(ND):
            tiles = [q_ref[k, j, tile_rows(r), :] for r in range(TILES)]
            for r, tile in enumerate(drift(j, base, tiles, scal_ref, inside)):
                out_ref[k, j, r] = tile
        return carry

    lax.fori_loop(0, bands, band, 0)


def packed_lat(j, x, d0, d1, d2):
    lane, row = lanes(), sublanes()
    first, last = lane < GROUP, lane >= (TILES - 1) * GROUP
    if BACK_LAT[j]:
        moved, one = pltpu.roll(x, 1, 0), turn(x, GROUP)
        near = jnp.where(first, jnp.where(row == 0, x, turn(moved, -2 * GROUP)), one)
        far = jnp.where(row == 0, jnp.where(first, x, one), turn(moved, -GROUP))
        far = jnp.where(last, turn(x, 2 * GROUP), far)
    else:
        moved, one = pltpu.roll(x, 7, 0), turn(x, -GROUP)
        near = jnp.where(last, jnp.where(row == 7, x, turn(moved, 2 * GROUP)), one)
        far = jnp.where(row == 7, jnp.where(last, x, one), turn(moved, GROUP))
        far = jnp.where(first, turn(x, -2 * GROUP), far)
    return d0 * x + d1 * near + d2 * far


def spread(tile, position):
    at_first = lanes() // 4 % BANDS == 0
    tile = jnp.where(at_first, turn(tile, -4 * position), 0.0)
    for step in (1, 2, 4):
        tile = tile + turn(tile, 4 * step)
    return tile


def packed_coefficients(inverse, speed):
    c = inverse * abs(float(speed))
    return 1.0 + c * (0.5 * c - 1.5), c * (2.0 - c), c * (0.5 * c - 0.5)


def packed_fix(table, columns_ref, fix_ref):
    slot = lanes() % 4
    inverse = table(5)
    for j in range(ND):
        back = BACK_LON[j]
        _, c1, c2 = packed_coefficients(inverse, COURANT_MAX * COS[j])
        tile = columns_ref[j]
        next_one = jnp.where(slot == (0 if back else 3), turn(tile, -1 if back else 1), 0.0)
        first = c2 * tile + c1 * next_one
        lat = packed_coefficients(inverse, 0.5 * COURANT_MAX * SIN[j])
        fix_ref[j] = packed_lat(j, first, *lat)


def packed_start(mine_right_ref, mine_left_ref, left_ref, right_ref, columns_ref, side_refs):
    near_ref, far_ref = side_refs
    lane = lanes()
    slot = lane % 4
    used = lane < TILES * GROUP
    for j in range(ND):
        half = RANK[j] % 2
        narrow = HALF + RANK[j] // 2
        if BACK_LON[j]:
            wide, own = left_ref[RANK[j]], mine_right_ref[RANK[j]]
            other = turn(right_ref[narrow], 2 - 2 * half)
            centre = jnp.where(slot < 2, turn(wide, -2), other)
            near = jnp.where(slot == 2, turn(own, -1), turn(centre, 1))
            near = jnp.where(slot < 2, turn(wide, -1), near)
            far = jnp.where(slot < 2, wide, own)
        else:
            wide, own = right_ref[RANK[j]], mine_left_ref[RANK[j]]
            other = turn(left_ref[narrow], -2 * half)
            centre = jnp.where(slot < 2, other, turn(wide, 2))
            near = jnp.where(slot == 1, turn(own, 1), turn(centre, -1))
            near = jnp.where(slot >= 2, turn(wide, 1), near)
            far = jnp.where(slot < 2, own, wide)
        columns_ref[j] = jnp.where(used, centre, 0.0)
        near_ref[j] = jnp.where(used, near, 0.0)
        far_ref[j] = jnp.where(used, far, 0.0)


def packed_source(
    table, left_ref, right_ref, columns_ref, side_refs, sums_ref, part_ref, drive_ref, ice_ref, p_ref
):
    near_ref, far_ref = side_refs
    lane = lanes()
    slot, place = lane % 4, lane // 4 % BANDS
    both = jnp.where(slot < 2, left_ref[SENT - 1], turn(right_ref[SENT - 1], 2))
    east, north, land, south_rows, north_rows = (spread(both, i) for i in range(FIELDS))
    row = (TILES * sublanes() + lane // GROUP).astype(jnp.float32)
    held = (row < south_rows) | (row >= LAT - north_rows)
    sea = jnp.where(land > 0.5, 1.0, 0.0)
    ice = jnp.where(land > 1.5, 1.0, 0.0)
    ice_ref[...] = ice
    inverse = table(5)
    slope = jnp.zeros((8, WIDTH), jnp.float32)
    stress = slope
    for j in range(ND):
        lon = packed_coefficients(inverse, COURANT_MAX * COS[j])
        lat = packed_coefficients(inverse, 0.5 * COURANT_MAX * SIN[j])
        centre = columns_ref[j]
        x = lon[0] * centre + lon[1] * near_ref[j] + lon[2] * far_ref[j]
        x = packed_lat(j, x, *lat)
        p = jnp.where(held, centre, jnp.maximum(x, 0.0)) * sea
        drive = drive_of(j, east, north, 1.0 - ice)
        drive_ref[j] = drive
        p_ref[j] = p
        slope = slope + p
        stress = stress + p * drive

    def running(tile):
        for step in (1, 2, 4):
            tile = tile + jnp.where(place >= step, turn(tile, 4 * step), 0.0)
        return tile

    out = [jnp.zeros((8, WIDTH), jnp.float32) for _ in range(PACKED_SUMS)]

    def put(index, tile):
        position = index % BANDS
        moved = turn(tile, 4 * (position - (BANDS - 1)))
        out[index // BANDS] = jnp.where(place == position, moved, out[index // BANDS])

    for j, excess in enumerate(excess_of([p_ref[j] for j in range(ND)])):
        total = running(excess)
        put(j, total)
        rate = excess * table(0) + (total - excess) * table(1)
        part_ref[j] = p_ref[j] * jnp.exp(rate)
    put(ND, running(slope * table(2)))
    put(ND + 1, running(stress * table(3)))
    for i in range(PACKED_SUMS):
        sums_ref[PACKED_AT + i] = out[i]


def excess_of(p):
    out = []
    for saturation in saturation_of(p):
        capped = jnp.maximum(saturation, CAP)
        excess = capped * lax.rsqrt(capped) - ROOT_CAP
        out.append(excess * excess)
    return out


def source_kernel(first, *refs):
    scal_ref, table_ref, x_ref, spec_ref, east_ref, north_ref, land_ref, rows_ref = refs[:8]
    refs = refs[8:]
    freq = lax.axis_index("freq")
    bands = x_ref.shape[0]

    def table(i):
        return table_ref[freq, i]

    if first:
        mine_right_ref, mine_left_ref, even_ref, odd_ref = refs[:4]
        p_ref, excess_ref, sums_ref, part_ref, packed_drive_ref, ice_ref = refs[4:10]
        drive_ref, fix_ref, left_ref, right_ref, columns_ref, near_ref, far_ref, packed_ref = refs[10:]
        odd = lax.axis_index("lon") % 2 == 1
        for i in range(SENT):
            even, other = even_ref[i], odd_ref[i]
            left_ref[i] = jnp.where(odd, even, other)
            right_ref[i] = jnp.where(odd, other, even)
        sides = (near_ref, far_ref)
        packed_start(mine_right_ref, mine_left_ref, left_ref, right_ref, columns_ref, sides)
        packed_source(
            table, left_ref, right_ref, columns_ref, sides,
            sums_ref, part_ref, packed_drive_ref, ice_ref, packed_ref,
        )
    else:
        columns_ref, p_ref, excess_ref, sums_ref, drive_ref, fix_ref = refs
    packed_fix(table, columns_ref, fix_ref)
    for i in range(PACKED_AT):
        sums_ref[i] = jnp.zeros((8, WIDTH), jnp.float32)
    for r in range(TILES):
        rows = tile_rows(r)
        water = jnp.where(land_ref[rows, :] == 2, 0.0, 1.0)
        east, north = east_ref[rows, :], north_ref[rows, :]
        for j in range(ND):
            drive_ref[j, r] = drive_of(j, east, north, water)

    lane = lanes()
    at_edge = {True: lane < 2, False: lane >= WIDTH - 2}

    def band(k, carry):
        extra = (freq * bands + k) * STRIDE + 6 * ND
        for r in range(TILES):
            rows = tile_rows(r)
            row = TILES * sublanes() + r
            held = (row < rows_ref[0:1, :]) | (row >= LAT - rows_ref[1:2, :])
            sea = jnp.where(land_ref[rows, :] != 0, 1.0, 0.0)
            slope = jnp.zeros((8, WIDTH), jnp.float32)
            stress = slope
            shift = {
                True: jnp.bitwise_and(WIDTH - GROUP * r - 4 * k, WIDTH - 1),
                False: WIDTH - 4 - GROUP * r - 4 * k,
            }
            for j in range(ND):
                back = BACK_LON[j]
                moved = pltpu.roll(fix_ref[j], shift[back], 1)
                p = x_ref[k, j, r] + jnp.where(at_edge[back], moved, 0.0)
                p = jnp.where(held, spec_ref[k, j, rows, :], jnp.maximum(p, 0.0)) * sea
                p_ref[k, j, r] = p
                slope = slope + p
                stress = stress + p * drive_ref[j, r]
            sums_ref[SLOPE_AT + r] += slope * scal_ref[extra + 2]
            sums_ref[STRESS_AT + r] += stress * scal_ref[extra + 3]
            for j, excess in enumerate(excess_of([p_ref[k, j, r] for j in range(ND)])):
                excess_ref[k, j, r] = excess
                sums_ref[TILES * j + r] += excess
        return carry

    lax.fori_loop(0, bands, band, 0)


def local_kernel(scal_ref, p_ref, excess_ref, out_ref):
    bands = p_ref.shape[0]
    first = (lax.axis_index("freq") * bands) * STRIDE + 6 * ND
    some = 6

    def directions(group, carry):
        for i in range(some):
            j = group * some + i
            for r in range(TILES):
                lower = jnp.zeros((8, WIDTH), jnp.float32)
                for k in range(bands):
                    excess = excess_ref[k, j, r]
                    at = first + k * STRIDE
                    rate = excess * scal_ref[at] + lower * scal_ref[at + 1]
                    out_ref[k, j, r] = p_ref[k, j, r] * jnp.exp(rate)
                    lower = lower + excess
        return carry

    lax.fori_loop(0, ND // some, directions, 0)


def pair_kernel(sums_ref, other_ref, out_ref):
    first = (lax.axis_index("freq") % 2) * HALF_TILES
    for i in range(HALF_TILES):
        out_ref[i] = sums_ref[first + i] + other_ref[first + i]
    for i in range(out_ref.shape[0] - HALF_TILES):
        out_ref[HALF_TILES + i] = sums_ref[SLOPE_AT + i] + other_ref[SLOPE_AT + i]


def damp_and_gain(slope, stress, ice):
    damp = SWELL_DAMP * (slope / (slope + 1.0)) + ICE_DAMP * ice
    return damp, GROWTH * (1.0 + stress / (stress + 1.0))


def grow_half(half, last, near, refs):
    scal_ref, part_ref, sums_ref, other_ref, mine_ref, lower_ref = refs[:6]
    east_ref, north_ref, land_ref, out_ref, rate_ref, field_ref, sent = refs[6:]
    bands = part_ref.shape[0]
    freq = lax.axis_index("freq")
    odd = jnp.where(freq % 2 == 1, 1.0, 0.0)
    upper = jnp.where(freq >= 2, 1.0, 0.0)
    after = SLOPE_AT - HALF_TILES
    for r in range(TILES):
        rows = tile_rows(r)
        ice = jnp.where(land_ref[rows, :] == 2, 1.0, 0.0)
        slope, stress = (
            (sums_ref[at + r] + other_ref[at + r]) + mine_ref[at + r - after]
            for at in (SLOPE_AT, STRESS_AT)
        )
        damp, gain = damp_and_gain(slope, stress, ice)
        east, north = east_ref[rows, :], north_ref[rows, :]
        for i in range(HALF):
            j = half * HALF + i
            lower = odd * other_ref[TILES * j + r] + upper * lower_ref[TILES * i + r]
            drive = drive_of(j, east, north, 1.0 - ice)
            rate_ref[i, r] = gain * drive - damp - LOWER * lower

    inside = None if last else inside_masks()

    def send(k):
        place = pl.ds(half * HALF, HALF)
        return pltpu.make_async_copy(field_ref.at[k], out_ref.at[k, place], sent.at[k])

    def band(k, carry):
        base = (freq * bands + k) * STRIDE
        root = scal_ref[base + 6 * ND + 4]
        for i in range(HALF):
            j = half * HALF + i
            tiles = [part_ref[k, j, r] * jnp.exp(rate_ref[i, r] * root) for r in range(TILES)]
            if last:
                for r in range(TILES):
                    field_ref[k, i, tile_rows(r), :] = tiles[r]
            else:
                for r, tile in enumerate(drift(j, base, tiles, scal_ref, inside)):
                    out_ref[k, j, r] = tile
        if last:
            send(k).start()
        return carry

    lax.fori_loop(0, bands, band, 0)
    if last:
        for k in range(bands):
            send(k).wait()


def growth_kernel(last, near, *refs):
    operands, refs = refs[:9], refs[9:]
    scal_ref, part_ref, sums_ref, other_ref, mine_ref = operands[:5]
    freq = lax.axis_index("freq")
    rest = (None, None)
    if near and last:
        out_ref, slope_ref, rate_ref, *rest = refs
        for r in range(TILES):
            at = SLOPE_AT + r
            total = (sums_ref[at] + other_ref[at]) + mine_ref[at - SLOPE_AT + HALF_TILES]
            slope_ref[tile_rows(r), :] = total
    elif near:
        table_ref, packed_part_ref, packed_drive_ref, ice_ref, out_ref, columns_ref, rate_ref = refs
        odd = jnp.where(freq % 2 == 1, 1.0, 0.0)
        upper = jnp.where(freq >= 2, 1.0, 0.0)
        total, lower = [], []
        for i in range(PACKED_SUMS):
            here, there = PACKED_AT + i, HALF_TILES + 2 * TILES + i
            total.append((sums_ref[here] + other_ref[here]) + mine_ref[there])
            lower.append(odd * other_ref[here] + upper * mine_ref[there])
        slope, stress = (spread(total[i // BANDS], i % BANDS) for i in (ND, ND + 1))
        damp, gain = damp_and_gain(slope, stress, ice_ref[...])
        root = table_ref[freq, 4]
        for j in range(ND):
            under = spread(lower[j // BANDS], j % BANDS)
            rate = gain * packed_drive_ref[j] - damp - LOWER * under
            columns_ref[j] = packed_part_ref[j] * jnp.exp(root * rate)
    else:
        _, out_ref, rate_ref, *rest = refs
        rest = rest or (None, None)
    for half in range(2):

        @pl.when(freq % 2 == (half if near else 1 - half))
        def _():
            grow_half(half, last, near, operands + (out_ref, rate_ref, *rest))


def cost(tiles, ops, moves):
    return pl.CostEstimate(
        flops=tiles * ops * 8 * WIDTH, bytes_accessed=tiles * moves * 32 * WIDTH, transcendentals=0
    )


def per_device(spectrum, east_wind, north_wind, land_sea, edge_rows):
    bands, count, lat_rows, width = spectrum.shape
    assert (bands, count, lat_rows, width) == (BANDS, ND, LAT, WIDTH)
    ring = lax.axis_size("lon")
    assert lax.axis_size("freq") == 4 and bands * 4 == NF and ring % 2 == 0
    f32 = jnp.float32

    def tiles(count):
        return jax.ShapeDtypeStruct((count, 8, WIDTH), f32)

    field = jax.ShapeDtypeStruct(spectrum.shape, f32)
    spread_field = jax.ShapeDtypeStruct((bands, ND, TILES, 8, WIDTH), f32)
    plane = jax.ShapeDtypeStruct((LAT, WIDTH), f32)
    tile = jax.ShapeDtypeStruct((8, WIDTH), f32)
    smem = pl.BlockSpec(memory_space=pltpu.SMEM)
    vmem = pl.BlockSpec(memory_space=pltpu.VMEM)
    hbm = pl.BlockSpec(memory_space=pltpu.HBM)
    params = pltpu.CompilerParams(vmem_limit_bytes=16 * 1024 * 1024)
    scalars, table = jnp.asarray(SCALARS), jnp.asarray(PACKED_TABLE)
    swap_core = [(0, 1), (1, 0), (2, 3), (3, 2)]
    swap_chip = [(0, 2), (2, 0), (1, 3), (3, 1)]
    swap_even = [(i, i ^ 1) for i in range(ring)]
    swap_odd = [(i, (i + (1 if i % 2 else -1)) % ring) for i in range(ring)]
    whole = bands * ND * TILES
    by_direction = pltpu.VMEM((ND, TILES, 8, WIDTH), f32)
    packed = pltpu.VMEM((ND, 8, WIDTH), f32)
    received = pltpu.VMEM((SENT, 8, WIDTH), f32)

    arguments = [spectrum, east_wind, north_wind, land_sea, edge_rows]
    spectrum, right, left, east_wind, north_wind, land_sea, edge_rows, even, odd = pl.pallas_call(
        pack_kernel,
        in_specs=[hbm] * 5,
        out_specs=[vmem] * 9,
        out_shape=[field, tiles(SENT), tiles(SENT)]
        + [jax.ShapeDtypeStruct(x.shape, x.dtype) for x in arguments[1:]]
        + [tiles(SENT), tiles(SENT)],
        scratch_shapes=[pltpu.SemaphoreType.DMA((ND // CHUNK + 4,))],
        compiler_params=params,
        cost_estimate=cost(whole, 6, 2),
        name="pack_columns",
    )(*(pltpu.with_memory_space_constraint(x, pltpu.HBM) for x in arguments))
    even = lax.ppermute(even, "lon", swap_even)
    odd = lax.ppermute(odd, "lon", swap_odd)
    drifted = pl.pallas_call(
        drift_kernel,
        in_specs=[smem, vmem],
        out_specs=vmem,
        out_shape=spread_field,
        compiler_params=params,
        cost_estimate=cost(whole, 12, 2),
        name="drift",
    )(scalars, spectrum)

    fields = [east_wind, north_wind, land_sea]
    for step in range(STEPS):
        first, last = step == 0, step == STEPS - 1
        sums = PACKED_AT + (PACKED_SUMS if first else 0)
        half_sums = sums - SLOPE_AT + HALF_TILES
        operands = [scalars, table, drifted, spectrum, *fields, edge_rows]
        operands += [right, left, even, odd] if first else [columns]
        p, excess, mine, *packed_state = pl.pallas_call(
            functools.partial(source_kernel, first),
            in_specs=[smem] + [vmem] * (len(operands) - 1),
            out_specs=[vmem] * (6 if first else 3),
            out_shape=[spread_field, spread_field, tiles(sums)]
            + ([tiles(ND), tiles(ND), tile] if first else []),
            scratch_shapes=[by_direction, packed]
            + ([received] * 2 + [packed] * 4 if first else []),
            compiler_params=params,
            cost_estimate=cost(whole, 30, 3),
            name="sources",
        )(*operands)
        other = lax.ppermute(mine, "freq", swap_core)
        pair = pl.pallas_call(
            pair_kernel,
            in_specs=[vmem] * 2,
            out_specs=vmem,
            out_shape=tiles(half_sums),
            compiler_params=params,
            cost_estimate=cost(half_sums, 1, 3),
            name="pair_sums",
        )(mine, other)
        near = lax.ppermute(pair, "freq", swap_chip)
        excess, _ = lax.optimization_barrier((excess, pair))
        part = pl.pallas_call(
            local_kernel,
            in_specs=[smem] + [vmem] * 2,
            out_specs=vmem,
            out_shape=spread_field,
            compiler_params=params,
            cost_estimate=cost(whole, 8, 3),
            name="local_rate",
        )(scalars, p, excess)
        near, part = lax.optimization_barrier((near, part))
        far = lax.ppermute(near, "freq", swap_core)

        def grow(is_near, lower, extra, more_specs, more_shapes, alias):
            operands = [scalars, part, mine, other, near, lower, *fields] + extra
            scratch = [pltpu.VMEM((HALF, TILES, 8, WIDTH), f32)]
            if last:
                scratch += [
                    pltpu.VMEM((bands, HALF, LAT, WIDTH), f32),
                    pltpu.SemaphoreType.DMA((bands,)),
                ]
            specs = [smem] + [vmem] * (len(operands) - 1)
            if alias and last:
                specs[-1] = hbm
            return pl.pallas_call(
                functools.partial(growth_kernel, last, is_near),
                in_specs=specs,
                out_specs=[hbm if last else vmem] + more_specs,
                out_shape=[field if last else spread_field] + more_shapes,
                input_output_aliases={len(operands) - 1: 0} if alias else {},
                scratch_shapes=scratch,
                compiler_params=params,
                cost_estimate=cost(whole, 6 if last else 12, 1),
                name="grow_near" if is_near else "grow_far",
            )(*operands)

        extra = [] if last else [table, *packed_state]
        made, columns = grow(True, near, extra, [vmem], [plane if last else tiles(ND)], False)
        (drifted,) = grow(False, far, [made], [], [], True)
    return drifted, columns


def solution(mesh):
    in_specs = (
        P("freq", None, None, "lon"),
        P(None, "lon"),
        P(None, "lon"),
        P(None, "lon"),
        P(None, "lon"),
    )
    out_specs = (P("freq", None, None, "lon"), P(None, "lon"))
    return jax.shard_map(
        per_device, mesh=mesh, in_specs=in_specs, out_specs=out_specs, check_vma=False
    )
```

```python
import functools
import math

import jax
import jax.numpy as jnp
import numpy as np
from jax import lax
from jax.experimental import pallas as pl
from jax.experimental.pallas import tpu as pltpu
from jax.sharding import PartitionSpec as P

NF = 32
STEPS = 2

COURANT_MAX = 0.9
FREQ_RATIO = 1.1
WIND_REF = 8.0
WIND_CLIP = 2.0
GROWTH = 0.01
BREAKING = 0.3
SATURATION_REF = 0.4
CUMULATIVE = 2.0
SWELL_DAMP = 0.1
ICE_DAMP = 0.5

ND = 36
HALF = ND // 2
QUARTER = ND // 4
DTHETA = 2.0 * math.pi / ND
LOG2E = 1.0 / math.log(2.0)
ROOT_REF = math.sqrt(SATURATION_REF)
TILES = 3
LAT = 8 * TILES
WIDTH = 128
STRIDE = 6 * ND + 8

ANGLES = np.arange(ND) * DTHETA
COS = np.cos(ANGLES)
SIN = np.sin(ANGLES)
COS2 = np.cos(2.0 * ANGLES)
SIN2 = np.sin(2.0 * ANGLES)
BACK_LON = [bool(c >= 0.0) for c in COS]
BACK_LAT = [bool(s >= 0.0) for s in SIN]
RANK = [sum(BACK_LON[:j]) if BACK_LON[j] else j - sum(BACK_LON[:j]) for j in range(ND)]


def one_sided(courant):
    c = np.abs(courant)
    return 1.0 - 1.5 * c + 0.5 * c * c, 2.0 * c - c * c, 0.5 * c * c - 0.5 * c


GROUP = 32
BANDS = 8
SENT = HALF + QUARTER + 1
FIELDS = 5
SLOPE_AT = ND * TILES
STRESS_AT = SLOPE_AT + TILES
PACKED_AT = STRESS_AT + TILES
PACKED_SUMS = 5
HALF_TILES = HALF * TILES
SCALE = 0.25 * DTHETA
CAP = SATURATION_REF / SCALE
ROOT_CAP = math.sqrt(CAP)
LOWER = CUMULATIVE / NF * SCALE


def make_tables():
    ratios = FREQ_RATIO ** np.arange(NF)
    root = np.sqrt(ratios)
    lon = one_sided(COURANT_MAX * COS[None, :] / ratios[:, None])
    lat = one_sided(0.5 * COURANT_MAX * SIN[None, :] / ratios[:, None])
    scalars = np.zeros((NF, STRIDE))
    for i in range(3):
        scalars[:, i : 6 * ND : 6] = lon[i]
        scalars[:, 3 + i : 6 * ND : 6] = lat[i]
    rest = [
        -BREAKING / SATURATION_REF * SCALE * root,
        -LOWER * root,
        ratios * ratios * DTHETA / np.sum(ratios * ratios),
        ratios * root * DTHETA / np.sum(ratios * root),
        root,
        1.0 / ratios,
    ]
    packed = np.zeros((NF // BANDS, len(rest), 8, WIDTH))
    for i, value in enumerate(rest):
        scalars[:, 6 * ND + i] = value
        for lane in range(TILES * GROUP):
            packed[:, i, :, lane] = value[lane // 4 % BANDS :: BANDS, None]
    return scalars.reshape(-1).astype(np.float32), packed.astype(np.float32)


SCALARS, PACKED_TABLE = make_tables()


def lanes():
    return lax.broadcasted_iota(jnp.int32, (8, WIDTH), 1)


def sublanes():
    return lax.broadcasted_iota(jnp.int32, (8, WIDTH), 0)


def turn(tile, shift):
    shift = shift % WIDTH
    return tile if shift == 0 else pltpu.roll(tile, shift, 1)


def tile_rows(r):
    return pl.ds(r, 8, stride=TILES)


CHUNK = 4


def pack_kernel(spec_ref, *refs):
    sources, (copy_ref, right_ref, left_ref), held_refs = refs[:4], refs[4:7], refs[7:11]
    to_even_ref, to_odd_ref, arrived = refs[11:]

    def fetch(c):
        part = pl.ds(CHUNK * c, CHUNK)
        return pltpu.make_async_copy(spec_ref.at[:, part], copy_ref.at[:, part], arrived.at[c])

    small = [
        pltpu.make_async_copy(source, target, arrived.at[ND // CHUNK + i])
        for i, (source, target) in enumerate(zip(sources, held_refs))
    ]
    for c in range(ND // CHUNK):
        fetch(c).start()
    for copy in small:
        copy.start()
    lane = lanes()
    zero = jnp.zeros((8, WIDTH), jnp.float32)
    held = [zero, zero]
    for j in range(ND):
        if j % CHUNK == 0:
            fetch(j // CHUNK).wait()
        back = BACK_LON[j]
        wide, narrow = (right_ref, left_ref) if back else (left_ref, right_ref)
        half = RANK[j] % 2
        first, aside = (WIDTH - 4, 4) if back else (0, -2)
        four = zero
        two = zero
        for r in range(TILES):
            for k in range(BANDS):
                place = GROUP * r + 4 * k
                tile = turn(copy_ref[k, j, tile_rows(r), :], place - first)
                four = jnp.where(lane // 4 == place // 4, tile, four)
                two = jnp.where(lane // 2 == (place + aside) % WIDTH // 2, tile, two)
        wide[RANK[j]] = four
        two = turn(two, 2 * half - aside)
        if half:
            narrow[HALF + RANK[j] // 2] = jnp.where(lane % 4 < 2, held[back], two)
        else:
            held[back] = two
    for copy in small:
        copy.wait()
    east_ref, north_ref, land_ref, rows_ref = held_refs
    fields = [
        [f(r) for r in range(TILES)]
        for f in (
            lambda r: east_ref[tile_rows(r), :],
            lambda r: north_ref[tile_rows(r), :],
            lambda r: land_ref[tile_rows(r), :].astype(jnp.float32),
            lambda r: jnp.broadcast_to(rows_ref[0:1, :].astype(jnp.float32), (8, WIDTH)),
            lambda r: jnp.broadcast_to(rows_ref[1:2, :].astype(jnp.float32), (8, WIDTH)),
        )
    ]
    to_right, to_left = zero, zero
    for i in range(FIELDS):
        for r in range(TILES):
            place = GROUP * r + 4 * i
            here = lane // 2 == place // 2
            to_right = jnp.where(here, turn(fields[i][r], place - (WIDTH - 2)), to_right)
            to_left = jnp.where(here, turn(fields[i][r], place), to_left)
    right_ref[SENT - 1] = to_right
    left_ref[SENT - 1] = to_left
    odd = lax.axis_index("lon") % 2 == 1
    for i in range(SENT):
        right, left = right_ref[i], left_ref[i]
        to_even_ref[i] = jnp.where(odd, left, right)
        to_odd_ref[i] = jnp.where(odd, right, left)


def drive_of(j, east, north, open_water):
    along = float(COS[j]) * east + float(SIN[j]) * north
    drive = jnp.minimum(jnp.maximum(along, 0.0) / WIND_REF, WIND_CLIP)
    return drive * drive * open_water


def tree(values):
    values = list(values)
    while len(values) > 1:
        values = [sum(values[i + 1 : i + 2], values[i]) for i in range(0, len(values), 2)]
    return values[0]


def saturation_of(p):
    diff = [p[b] - p[b + HALF] for b in range(HALF)]
    both = [p[b] + p[b + HALF] for b in range(HALF)]
    folded = [both[b] + both[b + QUARTER] for b in range(QUARTER)]
    total = tree(folded)
    fold = [both[b] - both[b + QUARTER] for b in range(QUARTER)]
    total_c = tree([fold[0]] + [fold[b] * float(COS2[b]) for b in range(1, QUARTER)])
    total_s = tree([fold[b] * float(SIN2[b]) for b in range(1, QUARTER)])
    level = [None] * HALF
    for a in range(QUARTER):
        wave = total_c * float(COS2[a])
        if a:
            wave = wave + total_s * float(SIN2[a])
        level[a] = total + wave
        level[a + QUARTER] = total - wave

    def at(b):
        return diff[b % HALF], b // HALF % 2 == 1

    def minus(a, b):
        x, flip_x = at(a)
        y, flip_y = at(b)
        if flip_x:
            return y - x if flip_y else None, (x, y)
        return x + y if flip_y else x - y, None

    def plus_minus(value, a, b):
        gap, opposite = minus(a, b)
        if gap is None:
            return value - (opposite[0] + opposite[1])
        return value + gap

    waves = []
    for a in range(2):
        pairs = [minus(a + d, a - d + HALF)[0] for d in range(1, QUARTER)]
        weighted = [pairs[d - 1] * float(COS2[d]) for d in range(1, QUARTER)]
        waves.append(tree([diff[a]] + weighted))
        if a == 0:
            plain = tree([diff[0]] + pairs)
    twice = float(2.0 * COS2[1])
    odd, below = [None] * HALF, [None] * HALF
    odd[0] = plain + waves[0]
    window, before, now = plain, waves[0], waves[1]
    for a in range(1, QUARTER + 1):
        window = plus_minus(window, a + 8, a - 9)
        odd[a] = window + now
        if a < QUARTER:
            rest = plus_minus(before, a + 10, a + 8)
            before, now = now, twice * now - rest
    window, after, now = plain, waves[1], waves[0]
    for a in range(0, -(QUARTER - 1), -1):
        rest = plus_minus(after, a + 10, a + 8)
        after, now = now, twice * now - rest
        window = plus_minus(window, a - 9 + 2 * HALF, a + 8)
        below[a - 1 + HALF] = window + now
    out = [None] * ND
    for a in range(HALF):
        if odd[a] is not None:
            out[a], out[a + HALF] = level[a] + odd[a], level[a] - odd[a]
        else:
            out[a], out[a + HALF] = level[a] - below[a], level[a] + below[a]
    return out


def inside_masks():
    lane = lanes()
    one = jnp.ones((8, WIDTH), jnp.float32)
    return {
        (True, 1): jnp.where(lane >= 1, one, 0.0),
        (True, 2): jnp.where(lane >= 2, one, 0.0),
        (False, 1): jnp.where(lane < WIDTH - 1, one, 0.0),
        (False, 2): jnp.where(lane < WIDTH - 2, one, 0.0),
    }


def drift(j, base, tiles, scal_ref, inside):
    c0, c1, c2, d0, d1, d2 = (scal_ref[base + 6 * j + i] for i in range(6))
    side = 1 if BACK_LON[j] else -1
    c1 = c1 * inside[BACK_LON[j], 1]
    c2 = c2 * inside[BACK_LON[j], 2]
    x = [c0 * q + c1 * turn(q, side) + c2 * turn(q, 2 * side) for q in tiles]
    row = sublanes()
    if BACK_LAT[j]:
        over = [jnp.where(row == 0, x[0], pltpu.roll(x[r], 1, 0)) for r in (1, 2)]
        near = [over[1], x[0], x[1]]
        far = [over[0], over[1], x[0]]
    else:
        over = [jnp.where(row == 7, x[2], pltpu.roll(x[r], 7, 0)) for r in (0, 1)]
        near = [x[1], x[2], over[0]]
        far = [x[2], over[0], over[1]]
    return [d0 * x[r] + d1 * near[r] + d2 * far[r] for r in range(TILES)]


def drift_kernel(scal_ref, q_ref, out_ref):
    bands = q_ref.shape[0]
    inside = inside_masks()

    def band(k, carry):
        base = (lax.axis_index("freq") * bands + k) * STRIDE
        for j in range(ND):
            tiles = [q_ref[k, j, tile_rows(r), :] for r in range(TILES)]
            for r, tile in enumerate(drift(j, base, tiles, scal_ref, inside)):
                out_ref[k, j, r] = tile
        return carry

    lax.fori_loop(0, bands, band, 0)


def packed_lat(j, x, d0, d1, d2):
    lane, row = lanes(), sublanes()
    first, last = lane < GROUP, lane >= (TILES - 1) * GROUP
    if BACK_LAT[j]:
        moved, one = pltpu.roll(x, 1, 0), turn(x, GROUP)
        near = jnp.where(first, jnp.where(row == 0, x, turn(moved, -2 * GROUP)), one)
        far = jnp.where(row == 0, jnp.where(first, x, one), turn(moved, -GROUP))
        far = jnp.where(last, turn(x, 2 * GROUP), far)
    else:
        moved, one = pltpu.roll(x, 7, 0), turn(x, -GROUP)
        near = jnp.where(last, jnp.where(row == 7, x, turn(moved, 2 * GROUP)), one)
        far = jnp.where(row == 7, jnp.where(last, x, one), turn(moved, GROUP))
        far = jnp.where(first, turn(x, -2 * GROUP), far)
    return d0 * x + d1 * near + d2 * far


def spread(tile, position):
    at_first = lanes() // 4 % BANDS == 0
    tile = jnp.where(at_first, turn(tile, -4 * position), 0.0)
    for step in (1, 2, 4):
        tile = tile + turn(tile, 4 * step)
    return tile


def packed_coefficients(inverse, speed):
    c = inverse * abs(float(speed))
    return 1.0 + c * (0.5 * c - 1.5), c * (2.0 - c), c * (0.5 * c - 0.5)


AHEAD = [j for j in range(ND) if not BACK_LON[j]]
BACK = [j for j in range(ND) if BACK_LON[j]]


def packed_fix(table, columns_ref, fix_ref):
    slot = lanes() % 4
    inverse = table(5)

    def one(j):
        back = BACK_LON[j]
        _, c1, c2 = packed_coefficients(inverse, COURANT_MAX * COS[j])
        tile = columns_ref[j]
        next_one = jnp.where(slot == (0 if back else 3), turn(tile, -1 if back else 1), 0.0)
        first = c2 * tile + c1 * next_one
        lat = packed_coefficients(inverse, 0.5 * COURANT_MAX * SIN[j])
        return packed_lat(j, first, *lat)

    for i in range(HALF):
        fix_ref[i] = jnp.where(slot < 2, one(BACK[i]), turn(one(AHEAD[i]), -4))


def packed_start(mine_right_ref, mine_left_ref, left_ref, right_ref, columns_ref, side_refs):
    near_ref, far_ref = side_refs
    lane = lanes()
    slot = lane % 4
    used = lane < TILES * GROUP
    for j in range(ND):
        half = RANK[j] % 2
        narrow = HALF + RANK[j] // 2
        if BACK_LON[j]:
            wide, own = left_ref[RANK[j]], mine_right_ref[RANK[j]]
            other = turn(right_ref[narrow], 2 - 2 * half)
            centre = jnp.where(slot < 2, turn(wide, -2), other)
            near = turn(jnp.where(slot == 3, own, wide), -1)
            near = jnp.where(slot == 3, turn(centre, 1), near)
            far = jnp.where(slot < 2, wide, own)
        else:
            wide, own = right_ref[RANK[j]], mine_left_ref[RANK[j]]
            other = turn(left_ref[narrow], -2 * half)
            centre = jnp.where(slot < 2, other, turn(wide, 2))
            near = turn(jnp.where(slot == 0, own, wide), 1)
            near = jnp.where(slot == 0, turn(centre, -1), near)
            far = jnp.where(slot < 2, own, wide)
        columns_ref[j] = jnp.where(used, centre, 0.0)
        near_ref[j] = jnp.where(used, near, 0.0)
        far_ref[j] = jnp.where(used, far, 0.0)


def packed_source(
    table, left_ref, right_ref, columns_ref, side_refs, sums_ref, part_ref, drive_ref, ice_ref
):
    near_ref, far_ref = side_refs
    lane = lanes()
    slot, place = lane % 4, lane // 4 % BANDS
    both = jnp.where(slot < 2, left_ref[SENT - 1], turn(right_ref[SENT - 1], 2))
    east, north, land, south_rows, north_rows = (spread(both, i) for i in range(FIELDS))
    row = (TILES * sublanes() + lane // GROUP).astype(jnp.float32)
    held = (row < south_rows) | (row >= LAT - north_rows)
    sea = jnp.where(land > 0.5, 1.0, 0.0)
    ice = jnp.where(land > 1.5, 1.0, 0.0)
    ice_ref[...] = ice
    inverse = table(5)
    p, stress = [], []
    for j in range(ND):
        lon = packed_coefficients(inverse, COURANT_MAX * COS[j])
        lat = packed_coefficients(inverse, 0.5 * COURANT_MAX * SIN[j])
        centre = columns_ref[j]
        x = lon[0] * centre + lon[1] * near_ref[j] + lon[2] * far_ref[j]
        x = packed_lat(j, x, *lat)
        p.append(jnp.where(held, centre, jnp.maximum(x, 0.0)) * sea)
        drive = drive_of(j, east, north, 1.0 - ice)
        drive_ref[j] = drive
        stress.append(p[j] * drive)
    slope, stress = tree(p), tree(stress)

    def running(tile):
        for step in (1, 2, 4):
            tile = tile + jnp.where(place >= step, turn(tile, 4 * step), 0.0)
        return tile

    out = [jnp.zeros((8, WIDTH), jnp.float32) for _ in range(PACKED_SUMS)]

    def put(index, tile):
        position = index % BANDS
        moved = turn(tile, 4 * (position - (BANDS - 1)))
        out[index // BANDS] = jnp.where(place == position, moved, out[index // BANDS])

    for j, excess in enumerate(excess_of(p)):
        total = running(excess)
        put(j, total)
        rate = excess * table(0) + (total - excess) * table(1)
        part_ref[j] = p[j] * jnp.exp(rate)
    put(ND, running(slope * table(2)))
    put(ND + 1, running(stress * table(3)))
    for i in range(PACKED_SUMS):
        sums_ref[PACKED_AT + i] = out[i]


def excess_of(p):
    out = []
    for saturation in saturation_of(p):
        capped = jnp.maximum(saturation, CAP)
        excess = capped * lax.rsqrt(capped) - ROOT_CAP
        out.append(excess * excess)
    return out


def source_kernel(first, *refs):
    scal_ref, table_ref, x_ref, spec_ref, east_ref, north_ref, land_ref, rows_ref = refs[:8]
    refs = refs[8:]
    freq = lax.axis_index("freq")
    bands = x_ref.shape[0]

    def table(i):
        return table_ref[freq, i]

    if first:
        mine_right_ref, mine_left_ref, even_ref, odd_ref = refs[:4]
        p_ref, excess_ref, sums_ref, part_ref, packed_drive_ref, ice_ref = refs[4:10]
        drive_ref, fix_ref, left_ref, right_ref, columns_ref, near_ref, far_ref = refs[10:]
        odd = lax.axis_index("lon") % 2 == 1
        for i in range(SENT):
            even, other = even_ref[i], odd_ref[i]
            left_ref[i] = jnp.where(odd, even, other)
            right_ref[i] = jnp.where(odd, other, even)
        sides = (near_ref, far_ref)
        packed_start(mine_right_ref, mine_left_ref, left_ref, right_ref, columns_ref, sides)
        packed_source(
            table, left_ref, right_ref, columns_ref, sides,
            sums_ref, part_ref, packed_drive_ref, ice_ref,
        )
    else:
        columns_ref, p_ref, excess_ref, sums_ref, drive_ref, fix_ref = refs
    packed_fix(table, columns_ref, fix_ref)
    for i in range(PACKED_AT):
        sums_ref[i] = jnp.zeros((8, WIDTH), jnp.float32)
    for r in range(TILES):
        rows = tile_rows(r)
        water = jnp.where(land_ref[rows, :] == 2, 0.0, 1.0)
        east, north = east_ref[rows, :], north_ref[rows, :]
        for j in range(ND):
            drive_ref[j, r] = drive_of(j, east, north, water)

    lane = lanes()
    at_edge = {True: lane < 2, False: lane >= WIDTH - 2}

    def band(k, carry):
        extra = (freq * bands + k) * STRIDE + 6 * ND
        for r in range(TILES):
            rows = tile_rows(r)
            row = TILES * sublanes() + r
            held = (row < rows_ref[0:1, :]) | (row >= LAT - rows_ref[1:2, :])
            sea = jnp.where(land_ref[rows, :] != 0, 1.0, 0.0)
            shift = jnp.bitwise_and(WIDTH - GROUP * r - 4 * k, WIDTH - 1)
            p = [None] * ND
            for i in range(HALF):
                moved = pltpu.roll(fix_ref[i], shift, 1)
                for j in (BACK[i], AHEAD[i]):
                    x = x_ref[k, j, r] + jnp.where(at_edge[BACK_LON[j]], moved, 0.0)
                    x = jnp.where(held, spec_ref[k, j, rows, :], jnp.maximum(x, 0.0)) * sea
                    p_ref[k, j, r] = x
                    p[j] = x
            slope = tree(p)
            stress = tree([p[j] * drive_ref[j, r] for j in range(ND)])
            sums_ref[SLOPE_AT + r] += slope * scal_ref[extra + 2]
            sums_ref[STRESS_AT + r] += stress * scal_ref[extra + 3]
            for j, excess in enumerate(excess_of(p)):
                excess_ref[k, j, r] = excess
                sums_ref[TILES * j + r] += excess
        return carry

    lax.fori_loop(0, bands, band, 0)


def local_kernel(scal_ref, p_ref, excess_ref, out_ref):
    bands = p_ref.shape[0]
    first = (lax.axis_index("freq") * bands) * STRIDE + 6 * ND
    some = 6

    def directions(group, carry):
        for i in range(some):
            j = group * some + i
            for r in range(TILES):
                lower = jnp.zeros((8, WIDTH), jnp.float32)
                for k in range(bands):
                    excess = excess_ref[k, j, r]
                    at = first + k * STRIDE
                    rate = excess * scal_ref[at] + lower * scal_ref[at + 1]
                    out_ref[k, j, r] = p_ref[k, j, r] * jnp.exp(rate)
                    lower = lower + excess
        return carry

    lax.fori_loop(0, ND // some, directions, 0)


def pair_kernel(sums_ref, other_ref, out_ref):
    first = (lax.axis_index("freq") % 2) * HALF_TILES
    for i in range(HALF_TILES):
        out_ref[i] = sums_ref[first + i] + other_ref[first + i]
    for i in range(out_ref.shape[0] - HALF_TILES):
        out_ref[HALF_TILES + i] = sums_ref[SLOPE_AT + i] + other_ref[SLOPE_AT + i]


def damp_and_gain(slope, stress, ice):
    damp = SWELL_DAMP * (slope / (slope + 1.0)) + ICE_DAMP * ice
    return damp, GROWTH * (1.0 + stress / (stress + 1.0))


def grow_half(half, last, near, refs):
    scal_ref, part_ref, sums_ref, other_ref, mine_ref, lower_ref = refs[:6]
    east_ref, north_ref, land_ref, out_ref, rate_ref, near_ref, field_ref, sent = refs[6:]
    bands = part_ref.shape[0]
    freq = lax.axis_index("freq")
    odd = jnp.where(freq % 2 == 1, 1.0, 0.0)
    upper = jnp.where(freq >= 2, 1.0, 0.0)
    after = SLOPE_AT - HALF_TILES
    for r in range(TILES):
        rows = tile_rows(r)
        ice = jnp.where(land_ref[rows, :] == 2, 1.0, 0.0)
        slope, stress = (
            (sums_ref[at + r] + other_ref[at + r]) + mine_ref[at + r - after]
            for at in (SLOPE_AT, STRESS_AT)
        )
        damp, gain = damp_and_gain(slope, stress, ice)
        east, north = east_ref[rows, :], north_ref[rows, :]
        for i in range(HALF):
            j = half * HALF + i
            lower = odd * other_ref[TILES * j + r] + upper * lower_ref[TILES * i + r]
            drive = drive_of(j, east, north, 1.0 - ice)
            rate_ref[i, r] = gain * drive - damp - LOWER * lower

    inside = None if last else inside_masks()
    target_ref = out_ref if near else field_ref

    def send(k, mine):
        source, which = (field_ref, half) if mine else (near_ref, 1 - half)
        place = out_ref.at[k, pl.ds(which * HALF, HALF)]
        return pltpu.make_async_copy(source.at[k], place, sent.at[int(mine), k])

    def band(k, carry):
        base = (freq * bands + k) * STRIDE
        root = scal_ref[base + 6 * ND + 4]
        for i in range(HALF):
            j = half * HALF + i
            tiles = [part_ref[k, j, r] * jnp.exp(rate_ref[i, r] * root) for r in range(TILES)]
            if last:
                for r in range(TILES):
                    target_ref[k, i, tile_rows(r), :] = tiles[r]
            else:
                for r, tile in enumerate(drift(j, base, tiles, scal_ref, inside)):
                    out_ref[k, j, r] = tile
        if last and not near:
            send(k, True).start()
        return carry

    write = last and not near
    if write:
        for k in range(bands):
            send(k, False).start()
    lax.fori_loop(0, bands, band, 0)
    if write:
        for k in range(bands):
            send(k, False).wait()
            send(k, True).wait()


def growth_kernel(last, near, *refs):
    operands, refs = refs[:9], refs[9:]
    scal_ref, part_ref, sums_ref, other_ref, mine_ref = operands[:5]
    freq = lax.axis_index("freq")
    rest = (None,) * 3
    if near and last:
        out_ref, slope_ref, rate_ref = refs
        for r in range(TILES):
            at = SLOPE_AT + r
            total = (sums_ref[at] + other_ref[at]) + mine_ref[at - SLOPE_AT + HALF_TILES]
            slope_ref[tile_rows(r), :] = total
    elif near:
        table_ref, packed_part_ref, packed_drive_ref, ice_ref, out_ref, columns_ref, rate_ref = refs
        odd = jnp.where(freq % 2 == 1, 1.0, 0.0)
        upper = jnp.where(freq >= 2, 1.0, 0.0)
        total, lower = [], []
        for i in range(PACKED_SUMS):
            here, there = PACKED_AT + i, HALF_TILES + 2 * TILES + i
            total.append((sums_ref[here] + other_ref[here]) + mine_ref[there])
            lower.append(odd * other_ref[here] + upper * mine_ref[there])
        slope, stress = (spread(total[i // BANDS], i % BANDS) for i in (ND, ND + 1))
        damp, gain = damp_and_gain(slope, stress, ice_ref[...])
        root = table_ref[freq, 4]
        for j in range(ND):
            under = spread(lower[j // BANDS], j % BANDS)
            rate = gain * packed_drive_ref[j] - damp - LOWER * under
            columns_ref[j] = packed_part_ref[j] * jnp.exp(root * rate)
    else:
        before_ref, out_ref, rate_ref, *rest = refs
        rest = (before_ref, *rest) if last else (None,) * 3
    for half in range(2):

        @pl.when(freq % 2 == (half if near else 1 - half))
        def _():
            grow_half(half, last, near, operands + (out_ref, rate_ref, *rest))


def cost(tiles, ops, moves):
    return pl.CostEstimate(
        flops=tiles * ops * 8 * WIDTH, bytes_accessed=tiles * moves * 32 * WIDTH, transcendentals=0
    )


def per_device(spectrum, east_wind, north_wind, land_sea, edge_rows):
    bands, count, lat_rows, width = spectrum.shape
    assert (bands, count, lat_rows, width) == (BANDS, ND, LAT, WIDTH)
    ring = lax.axis_size("lon")
    assert lax.axis_size("freq") == 4 and bands * 4 == NF and ring % 2 == 0
    f32 = jnp.float32

    def tiles(count):
        return jax.ShapeDtypeStruct((count, 8, WIDTH), f32)

    field = jax.ShapeDtypeStruct(spectrum.shape, f32)
    spread_field = jax.ShapeDtypeStruct((bands, ND, TILES, 8, WIDTH), f32)
    plane = jax.ShapeDtypeStruct((LAT, WIDTH), f32)
    tile = jax.ShapeDtypeStruct((8, WIDTH), f32)
    smem = pl.BlockSpec(memory_space=pltpu.SMEM)
    vmem = pl.BlockSpec(memory_space=pltpu.VMEM)
    hbm = pl.BlockSpec(memory_space=pltpu.HBM)
    params = pltpu.CompilerParams(vmem_limit_bytes=16 * 1024 * 1024)
    scalars, table = jnp.asarray(SCALARS), jnp.asarray(PACKED_TABLE)
    swap_core = [(0, 1), (1, 0), (2, 3), (3, 2)]
    swap_chip = [(0, 2), (2, 0), (1, 3), (3, 1)]
    swap_even = [(i, i ^ 1) for i in range(ring)]
    swap_odd = [(i, (i + (1 if i % 2 else -1)) % ring) for i in range(ring)]
    whole = bands * ND * TILES
    by_direction = pltpu.VMEM((ND, TILES, 8, WIDTH), f32)
    packed = pltpu.VMEM((ND, 8, WIDTH), f32)
    received = pltpu.VMEM((SENT, 8, WIDTH), f32)

    arguments = [spectrum, east_wind, north_wind, land_sea, edge_rows]
    spectrum, right, left, east_wind, north_wind, land_sea, edge_rows, even, odd = pl.pallas_call(
        pack_kernel,
        in_specs=[hbm] * 5,
        out_specs=[vmem] * 9,
        out_shape=[field, tiles(SENT), tiles(SENT)]
        + [jax.ShapeDtypeStruct(x.shape, x.dtype) for x in arguments[1:]]
        + [tiles(SENT), tiles(SENT)],
        scratch_shapes=[pltpu.SemaphoreType.DMA((ND // CHUNK + 4,))],
        compiler_params=params,
        cost_estimate=cost(whole, 6, 2),
        name="pack_columns",
    )(*(pltpu.with_memory_space_constraint(x, pltpu.HBM) for x in arguments))
    even = lax.ppermute(even, "lon", swap_even)
    odd = lax.ppermute(odd, "lon", swap_odd)
    drifted = pl.pallas_call(
        drift_kernel,
        in_specs=[smem, vmem],
        out_specs=vmem,
        out_shape=spread_field,
        compiler_params=params,
        cost_estimate=cost(whole, 12, 2),
        name="drift",
    )(scalars, spectrum)

    fields = [east_wind, north_wind, land_sea]
    for step in range(STEPS):
        first, last = step == 0, step == STEPS - 1
        sums = PACKED_AT + (PACKED_SUMS if first else 0)
        half_sums = sums - SLOPE_AT + HALF_TILES
        operands = [scalars, table, drifted, spectrum, *fields, edge_rows]
        operands += [right, left, even, odd] if first else [columns]
        p, excess, mine, *packed_state = pl.pallas_call(
            functools.partial(source_kernel, first),
            in_specs=[smem] + [vmem] * (len(operands) - 1),
            out_specs=[vmem] * (6 if first else 3),
            out_shape=[spread_field, spread_field, tiles(sums)]
            + ([tiles(ND), tiles(ND), tile] if first else []),
            scratch_shapes=[by_direction, packed]
            + ([received] * 2 + [packed] * 3 if first else []),
            compiler_params=params,
            cost_estimate=cost(whole, 30, 3),
            name="sources",
        )(*operands)
        other = lax.ppermute(mine, "freq", swap_core)
        pair = pl.pallas_call(
            pair_kernel,
            in_specs=[vmem] * 2,
            out_specs=vmem,
            out_shape=tiles(half_sums),
            compiler_params=params,
            cost_estimate=cost(half_sums, 1, 3),
            name="pair_sums",
        )(mine, other)
        near = lax.ppermute(pair, "freq", swap_chip)
        excess, _ = lax.optimization_barrier((excess, pair))
        part = pl.pallas_call(
            local_kernel,
            in_specs=[smem] + [vmem] * 2,
            out_specs=vmem,
            out_shape=spread_field,
            compiler_params=params,
            cost_estimate=cost(whole, 8, 3),
            name="local_rate",
        )(scalars, p, excess)
        near, part = lax.optimization_barrier((near, part))
        far = lax.ppermute(near, "freq", swap_core)

        near_half = jax.ShapeDtypeStruct((bands, HALF, LAT, WIDTH), f32)

        def grow(is_near, operands, shapes):
            write = last and not is_near
            scratch = [pltpu.VMEM((HALF, TILES, 8, WIDTH), f32)]
            if write:
                scratch += [pltpu.VMEM(near_half.shape, f32), pltpu.SemaphoreType.DMA((2, bands))]
            alias = not last and not is_near
            return pl.pallas_call(
                functools.partial(growth_kernel, last, is_near),
                in_specs=[smem] + [vmem] * (len(operands) - 1),
                out_specs=[hbm if write else vmem] * len(shapes),
                out_shape=shapes,
                input_output_aliases={len(operands) - 1: 0} if alias else {},
                scratch_shapes=scratch,
                compiler_params=params,
                cost_estimate=cost(whole, 6 if last else 12, 1),
                name="grow_near" if is_near else "grow_far",
            )(*operands)

        operands = [scalars, part, mine, other, near]
        extra = [] if last else [table, *packed_state]
        shapes = [near_half, plane] if last else [spread_field, tiles(ND)]
        made, columns = grow(True, operands + [near, *fields, *extra], shapes)
        shapes = [field if last else spread_field]
        (drifted,) = grow(False, operands + [far, *fields, made], shapes)
    return drifted, columns


def solution(mesh):
    in_specs = (
        P("freq", None, None, "lon"),
        P(None, "lon"),
        P(None, "lon"),
        P(None, "lon"),
        P(None, "lon"),
    )
    out_specs = (P("freq", None, None, "lon"), P(None, "lon"))
    return jax.shard_map(
        per_device, mesh=mesh, in_specs=in_specs, out_specs=out_specs, check_vma=False
    )
```

```python
import functools
import math

import jax
import jax.numpy as jnp
import numpy as np
from jax import lax
from jax.experimental import pallas as pl
from jax.experimental.pallas import tpu as pltpu
from jax.sharding import PartitionSpec as P

NF = 32
STEPS = 2

COURANT_MAX = 0.9
FREQ_RATIO = 1.1
WIND_REF = 8.0
WIND_CLIP = 2.0
GROWTH = 0.01
BREAKING = 0.3
SATURATION_REF = 0.4
CUMULATIVE = 2.0
SWELL_DAMP = 0.1
ICE_DAMP = 0.5

ND = 36
HALF = ND // 2
QUARTER = ND // 4
DTHETA = 2.0 * math.pi / ND
LOG2E = 1.0 / math.log(2.0)
ROOT_REF = math.sqrt(SATURATION_REF)
TILES = 3
LAT = 8 * TILES
WIDTH = 128
STRIDE = 6 * ND + 8

ANGLES = np.arange(ND) * DTHETA
COS = np.cos(ANGLES)
SIN = np.sin(ANGLES)
COS2 = np.cos(2.0 * ANGLES)
SIN2 = np.sin(2.0 * ANGLES)
BACK_LON = [bool(c >= 0.0) for c in COS]
BACK_LAT = [bool(s >= 0.0) for s in SIN]
RANK = [sum(BACK_LON[:j]) if BACK_LON[j] else j - sum(BACK_LON[:j]) for j in range(ND)]


def one_sided(courant):
    c = np.abs(courant)
    return 1.0 - 1.5 * c + 0.5 * c * c, 2.0 * c - c * c, 0.5 * c * c - 0.5 * c


GROUP = 32
BANDS = 8
SENT = HALF + QUARTER + 1
FIELDS = 5
SLOPE_AT = ND * TILES
STRESS_AT = SLOPE_AT + TILES
PACKED_AT = STRESS_AT + TILES
PACKED_SUMS = 5
HALF_TILES = HALF * TILES
SCALE = 0.25 * DTHETA
CAP = SATURATION_REF / SCALE
ROOT_CAP = math.sqrt(CAP)
LOWER = CUMULATIVE / NF * SCALE


def make_tables():
    ratios = FREQ_RATIO ** np.arange(NF)
    root = np.sqrt(ratios)
    lon = one_sided(COURANT_MAX * COS[None, :] / ratios[:, None])
    lat = one_sided(0.5 * COURANT_MAX * SIN[None, :] / ratios[:, None])
    scalars = np.zeros((NF, STRIDE))
    for i, value in enumerate(
        (lon[1] / lon[0], lon[2] / lon[0], lat[1] / lat[0], lat[2] / lat[0], lon[0] * lat[0])
    ):
        scalars[:, i : 6 * ND : 6] = value
    rest = [
        -BREAKING / SATURATION_REF * SCALE * root,
        -LOWER * root,
        ratios * ratios * DTHETA / np.sum(ratios * ratios),
        ratios * root * DTHETA / np.sum(ratios * root),
        root,
        1.0 / ratios,
    ]
    packed = np.zeros((NF // BANDS, len(rest), 8, WIDTH))
    for i, value in enumerate(rest):
        scalars[:, 6 * ND + i] = value
        for lane in range(TILES * GROUP):
            packed[:, i, :, lane] = value[lane // 4 % BANDS :: BANDS, None]
    return scalars.reshape(-1).astype(np.float32), packed.astype(np.float32)


SCALARS, PACKED_TABLE = make_tables()


def lanes():
    return lax.broadcasted_iota(jnp.int32, (8, WIDTH), 1)


def sublanes():
    return lax.broadcasted_iota(jnp.int32, (8, WIDTH), 0)


def turn(tile, shift):
    shift = shift % WIDTH
    return tile if shift == 0 else pltpu.roll(tile, shift, 1)


def tile_rows(r):
    return slice(8 * r, 8 * r + 8)


CHUNK = 4


def pack_kernel(spec_ref, *refs):
    sources, (copy_ref, right_ref, left_ref), held_refs = refs[:4], refs[4:7], refs[7:11]
    to_even_ref, to_odd_ref, arrived = refs[11:]

    def fetch(c):
        part = pl.ds(CHUNK * c, CHUNK)
        return pltpu.make_async_copy(spec_ref.at[:, part], copy_ref.at[:, part], arrived.at[c])

    small = [
        pltpu.make_async_copy(source, target, arrived.at[ND // CHUNK + i])
        for i, (source, target) in enumerate(zip(sources, held_refs))
    ]
    for c in range(ND // CHUNK):
        fetch(c).start()
    for copy in small:
        copy.start()
    lane = lanes()
    zero = jnp.zeros((8, WIDTH), jnp.float32)
    held = [zero, zero]
    for j in range(ND):
        if j % CHUNK == 0:
            fetch(j // CHUNK).wait()
        back = BACK_LON[j]
        wide, narrow = (right_ref, left_ref) if back else (left_ref, right_ref)
        half = RANK[j] % 2
        first, aside = (WIDTH - 4, 4) if back else (0, -2)
        four = zero
        two = zero
        for r in range(TILES):
            for k in range(BANDS):
                place = GROUP * r + 4 * k
                tile = turn(copy_ref[k, j, tile_rows(r), :], place - first)
                four = jnp.where(lane // 4 == place // 4, tile, four)
                two = jnp.where(lane // 2 == (place + aside) % WIDTH // 2, tile, two)
        wide[RANK[j]] = four
        two = turn(two, 2 * half - aside)
        if half:
            narrow[HALF + RANK[j] // 2] = jnp.where(lane % 4 < 2, held[back], two)
        else:
            held[back] = two
    for copy in small:
        copy.wait()
    east_ref, north_ref, land_ref, rows_ref = held_refs
    fields = [
        [f(r) for r in range(TILES)]
        for f in (
            lambda r: east_ref[tile_rows(r), :],
            lambda r: north_ref[tile_rows(r), :],
            lambda r: land_ref[tile_rows(r), :].astype(jnp.float32),
            lambda r: jnp.broadcast_to(rows_ref[0:1, :].astype(jnp.float32), (8, WIDTH)),
            lambda r: jnp.broadcast_to(rows_ref[1:2, :].astype(jnp.float32), (8, WIDTH)),
        )
    ]
    to_right, to_left = zero, zero
    for i in range(FIELDS):
        for r in range(TILES):
            place = GROUP * r + 4 * i
            here = lane // 2 == place // 2
            to_right = jnp.where(here, turn(fields[i][r], place - (WIDTH - 2)), to_right)
            to_left = jnp.where(here, turn(fields[i][r], place), to_left)
    right_ref[SENT - 1] = to_right
    left_ref[SENT - 1] = to_left
    odd = lax.axis_index("lon") % 2 == 1
    for i in range(SENT):
        right, left = right_ref[i], left_ref[i]
        to_even_ref[i] = jnp.where(odd, left, right)
        to_odd_ref[i] = jnp.where(odd, right, left)


def drive_of(j, east, north, open_water):
    along = float(COS[j]) * east + float(SIN[j]) * north
    drive = jnp.minimum(jnp.maximum(along, 0.0) / WIND_REF, WIND_CLIP)
    return drive * drive * open_water


def tree(values):
    values = list(values)
    while len(values) > 1:
        values = [sum(values[i + 1 : i + 2], values[i]) for i in range(0, len(values), 2)]
    return values[0]


def saturation_of(p):
    diff = [p[b] - p[b + HALF] for b in range(HALF)]
    both = [p[b] + p[b + HALF] for b in range(HALF)]
    folded = [both[b] + both[b + QUARTER] for b in range(QUARTER)]
    total = tree(folded)
    fold = [both[b] - both[b + QUARTER] for b in range(QUARTER)]
    total_c = tree([fold[0]] + [fold[b] * float(COS2[b]) for b in range(1, QUARTER)])
    total_s = tree([fold[b] * float(SIN2[b]) for b in range(1, QUARTER)])
    level = [None] * HALF
    for a in range(QUARTER):
        wave = total_c * float(COS2[a])
        if a:
            wave = wave + total_s * float(SIN2[a])
        level[a] = total + wave
        level[a + QUARTER] = total - wave

    def at(b):
        return diff[b % HALF], b // HALF % 2 == 1

    def minus(a, b):
        x, flip_x = at(a)
        y, flip_y = at(b)
        if flip_x:
            return y - x if flip_y else None, (x, y)
        return x + y if flip_y else x - y, None

    def plus_minus(value, a, b):
        gap, opposite = minus(a, b)
        if gap is None:
            return value - (opposite[0] + opposite[1])
        return value + gap

    waves = []
    for a in range(2):
        pairs = [minus(a + d, a - d + HALF)[0] for d in range(1, QUARTER)]
        weighted = [pairs[d - 1] * float(COS2[d]) for d in range(1, QUARTER)]
        waves.append(tree([diff[a]] + weighted))
        if a == 0:
            plain = tree([diff[0]] + pairs)
    twice = float(2.0 * COS2[1])
    odd, below = [None] * HALF, [None] * HALF
    odd[0] = plain + waves[0]
    window, before, now = plain, waves[0], waves[1]
    for a in range(1, QUARTER + 1):
        window = plus_minus(window, a + 8, a - 9)
        odd[a] = window + now
        if a < QUARTER:
            rest = plus_minus(before, a + 10, a + 8)
            before, now = now, twice * now - rest
    window, after, now = plain, waves[1], waves[0]
    for a in range(0, -(QUARTER - 1), -1):
        rest = plus_minus(after, a + 10, a + 8)
        after, now = now, twice * now - rest
        window = plus_minus(window, a - 9 + 2 * HALF, a + 8)
        below[a - 1 + HALF] = window + now
    out = [None] * ND
    for a in range(HALF):
        if odd[a] is not None:
            out[a], out[a + HALF] = level[a] + odd[a], level[a] - odd[a]
        else:
            out[a], out[a + HALF] = level[a] - below[a], level[a] + below[a]
    return out


def inside_masks():
    lane = lanes()
    one = jnp.ones((8, WIDTH), jnp.float32)
    return {
        (True, 1): jnp.where(lane >= 1, one, 0.0),
        (True, 2): jnp.where(lane >= 2, one, 0.0),
        (False, 1): jnp.where(lane < WIDTH - 1, one, 0.0),
        (False, 2): jnp.where(lane < WIDTH - 2, one, 0.0),
    }


def drift(j, base, tiles, scal_ref, inside):
    c1, c2, d1, d2 = (scal_ref[base + 6 * j + i] for i in range(4))
    side = 1 if BACK_LON[j] else -1
    c1 = c1 * inside[BACK_LON[j], 1]
    c2 = c2 * inside[BACK_LON[j], 2]
    x = [q + c1 * turn(q, side) + c2 * turn(q, 2 * side) for q in tiles]
    row = sublanes()
    one, two = (1, 2) if BACK_LAT[j] else (7, 6)
    at_edge = (row < 1, row < 2) if BACK_LAT[j] else (row >= 7, row >= 6)
    order = range(TILES) if BACK_LAT[j] else range(TILES - 1, -1, -1)
    moved = [[pltpu.roll(tile, by, 0) for tile in x] for by in (one, two)]
    y = [None] * TILES
    before = None
    for r in order:
        first = x[r] if before is None else moved[0][before]
        near = jnp.where(at_edge[0], first, moved[0][r])
        second = near if before is None else moved[1][before]
        far = jnp.where(at_edge[1], second, moved[1][r])
        y[r] = x[r] + d1 * near + d2 * far
        before = r
    return y


def drift_kernel(scal_ref, q_ref, out_ref):
    bands = q_ref.shape[0]
    inside = inside_masks()

    def band(k, carry):
        base = (lax.axis_index("freq") * bands + k) * STRIDE
        for j in range(ND):
            factor = scal_ref[base + 6 * j + 4]
            tiles = [q_ref[k, j, tile_rows(r), :] * factor for r in range(TILES)]
            for r, tile in enumerate(drift(j, base, tiles, scal_ref, inside)):
                out_ref[k, j, r] = tile
        return carry

    lax.fori_loop(0, bands, band, 0)


def packed_lat(j, x, d0, d1, d2):
    lane, row = lanes(), sublanes()

    def shifted(x):
        if BACK_LAT[j]:
            moved = pltpu.roll(x, 1, 0)
            over = jnp.where(lane < GROUP, x, turn(moved, GROUP))
            return jnp.where(row >= 1, moved, over)
        moved = pltpu.roll(x, 7, 0)
        over = jnp.where(lane >= (TILES - 1) * GROUP, x, turn(moved, -GROUP))
        return jnp.where(row <= 6, moved, over)

    near = shifted(x)
    return d0 * x + d1 * near + d2 * shifted(near)


def spread(tile, position):
    at_first = lanes() // 4 % BANDS == 0
    tile = jnp.where(at_first, turn(tile, -4 * position), 0.0)
    for step in (1, 2, 4):
        tile = tile + turn(tile, 4 * step)
    return tile


def packed_coefficients(inverse, speed):
    c = inverse * abs(float(speed))
    return 1.0 + c * (0.5 * c - 1.5), c * (2.0 - c), c * (0.5 * c - 0.5)


AHEAD = [j for j in range(ND) if not BACK_LON[j]]
BACK = [j for j in range(ND) if BACK_LON[j]]


def packed_fix(table, columns_ref, fix_ref):
    slot = lanes() % 4
    inverse = table(5)

    def one(j):
        back = BACK_LON[j]
        _, c1, c2 = packed_coefficients(inverse, COURANT_MAX * COS[j])
        tile = columns_ref[j]
        next_one = jnp.where(slot == (0 if back else 3), turn(tile, -1 if back else 1), 0.0)
        first = c2 * tile + c1 * next_one
        lat = packed_coefficients(inverse, 0.5 * COURANT_MAX * SIN[j])
        return packed_lat(j, first, *lat)

    for i in range(HALF):
        fix_ref[i] = jnp.where(slot < 2, one(BACK[i]), turn(one(AHEAD[i]), -4))


def packed_start(mine_right_ref, mine_left_ref, left_ref, right_ref, columns_ref, side_refs):
    near_ref, far_ref = side_refs
    lane = lanes()
    slot = lane % 4
    used = lane < TILES * GROUP
    for j in range(ND):
        half = RANK[j] % 2
        narrow = HALF + RANK[j] // 2
        if BACK_LON[j]:
            wide, own = left_ref[RANK[j]], mine_right_ref[RANK[j]]
            other = turn(right_ref[narrow], 2 - 2 * half)
            centre = jnp.where(slot < 2, turn(wide, -2), other)
            near = turn(jnp.where(slot == 3, own, wide), -1)
            near = jnp.where(slot == 3, turn(centre, 1), near)
            far = jnp.where(slot < 2, wide, own)
        else:
            wide, own = right_ref[RANK[j]], mine_left_ref[RANK[j]]
            other = turn(left_ref[narrow], -2 * half)
            centre = jnp.where(slot < 2, other, turn(wide, 2))
            near = turn(jnp.where(slot == 0, own, wide), 1)
            near = jnp.where(slot == 0, turn(centre, -1), near)
            far = jnp.where(slot < 2, own, wide)
        columns_ref[j] = jnp.where(used, centre, 0.0)
        near_ref[j] = jnp.where(used, near, 0.0)
        far_ref[j] = jnp.where(used, far, 0.0)


def packed_source(
    table, left_ref, right_ref, columns_ref, side_refs, sums_ref, part_ref, drive_ref, ice_ref
):
    near_ref, far_ref = side_refs
    lane = lanes()
    slot, place = lane % 4, lane // 4 % BANDS
    both = jnp.where(slot < 2, left_ref[SENT - 1], turn(right_ref[SENT - 1], 2))
    east, north, land, south_rows, north_rows = (spread(both, i) for i in range(FIELDS))
    row = (sublanes() + lane // GROUP * 8).astype(jnp.float32)
    held = (row < south_rows) | (row >= LAT - north_rows)
    sea = jnp.where(land > 0.5, 1.0, 0.0)
    ice = jnp.where(land > 1.5, 1.0, 0.0)
    ice_ref[...] = ice
    inverse = table(5)
    p, stress = [], []
    for j in range(ND):
        lon = packed_coefficients(inverse, COURANT_MAX * COS[j])
        lat = packed_coefficients(inverse, 0.5 * COURANT_MAX * SIN[j])
        centre = columns_ref[j]
        x = lon[0] * centre + lon[1] * near_ref[j] + lon[2] * far_ref[j]
        x = packed_lat(j, x, *lat)
        p.append(jnp.where(held, centre, jnp.maximum(x, 0.0)) * sea)
        drive = drive_of(j, east, north, 1.0 - ice)
        drive_ref[j] = drive
        stress.append(p[j] * drive)
    slope, stress = tree(p), tree(stress)

    def running(tile):
        for step in (1, 2, 4):
            tile = tile + jnp.where(place >= step, turn(tile, 4 * step), 0.0)
        return tile

    out = [jnp.zeros((8, WIDTH), jnp.float32) for _ in range(PACKED_SUMS)]

    def put(index, tile):
        position = index % BANDS
        moved = turn(tile, 4 * (position - (BANDS - 1)))
        out[index // BANDS] = jnp.where(place == position, moved, out[index // BANDS])

    for j, excess in enumerate(excess_of(p)):
        total = running(excess)
        put(j, total)
        rate = excess * table(0) + (total - excess) * table(1)
        part_ref[j] = p[j] * jnp.exp(rate)
    put(ND, running(slope * table(2)))
    put(ND + 1, running(stress * table(3)))
    for i in range(PACKED_SUMS):
        sums_ref[PACKED_AT + i] = out[i]


def excess_of(p):
    out = []
    for saturation in saturation_of(p):
        capped = jnp.maximum(saturation, CAP)
        excess = capped * lax.rsqrt(capped) - ROOT_CAP
        out.append(excess * excess)
    return out


def held_and_sea(r, land_ref, rows_ref):
    row = sublanes() + 8 * r
    held = (row < rows_ref[0:1, :]) | (row >= LAT - rows_ref[1:2, :])
    return held, jnp.where(land_ref[tile_rows(r), :] != 0, 1.0, 0.0)


def source_kernel(first, *refs):
    scal_ref, table_ref, x_ref, spec_ref, east_ref, north_ref, land_ref, rows_ref = refs[:8]
    refs = refs[8:]
    freq = lax.axis_index("freq")
    bands = x_ref.shape[0]

    def table(i):
        return table_ref[freq, i]

    if first:
        mine_right_ref, mine_left_ref, even_ref, odd_ref = refs[:4]
        p_ref, excess_ref, sums_ref, part_ref, packed_drive_ref, ice_ref = refs[4:10]
        drive_ref, fix_ref, left_ref, right_ref, columns_ref, near_ref, far_ref = refs[10:]
        odd = lax.axis_index("lon") % 2 == 1
        for i in range(SENT):
            even, other = even_ref[i], odd_ref[i]
            left_ref[i] = jnp.where(odd, even, other)
            right_ref[i] = jnp.where(odd, other, even)
        sides = (near_ref, far_ref)
        packed_start(mine_right_ref, mine_left_ref, left_ref, right_ref, columns_ref, sides)
        packed_source(
            table, left_ref, right_ref, columns_ref, sides,
            sums_ref, part_ref, packed_drive_ref, ice_ref,
        )
    else:
        columns_ref, p_ref, excess_ref, sums_ref, drive_ref, fix_ref = refs
    packed_fix(table, columns_ref, fix_ref)
    for i in range(PACKED_AT):
        sums_ref[i] = jnp.zeros((8, WIDTH), jnp.float32)
    for r in range(TILES):
        rows = tile_rows(r)
        water = jnp.where(land_ref[rows, :] == 2, 0.0, 1.0)
        east, north = east_ref[rows, :], north_ref[rows, :]
        for j in range(ND):
            drive_ref[j, r] = drive_of(j, east, north, water)

    lane = lanes()
    at_edge = {True: lane < 2, False: lane >= WIDTH - 2}

    def band(k, carry):
        extra = (freq * bands + k) * STRIDE + 6 * ND
        for r in range(TILES):
            rows = tile_rows(r)
            held, sea = held_and_sea(r, land_ref, rows_ref)
            if not first:
                free = jnp.where(held, 0.0, sea)
            shift = jnp.bitwise_and(WIDTH - GROUP * r - 4 * k, WIDTH - 1)
            p = [None] * ND
            for i in range(HALF):
                moved = pltpu.roll(fix_ref[i], shift, 1)
                for j in (BACK[i], AHEAD[i]):
                    x = x_ref[k, j, r] + jnp.where(at_edge[BACK_LON[j]], moved, 0.0)
                    if first:
                        x = jnp.where(held, spec_ref[k, j, rows, :], jnp.maximum(x, 0.0)) * sea
                    else:
                        x = jnp.maximum(x * free, spec_ref[k, j, r])
                    p_ref[k, j, r] = x
                    p[j] = x
            slope = tree(p)
            stress = tree([p[j] * drive_ref[j, r] for j in range(ND)])
            sums_ref[SLOPE_AT + r] += slope * scal_ref[extra + 2]
            sums_ref[STRESS_AT + r] += stress * scal_ref[extra + 3]
            for j, excess in enumerate(excess_of(p)):
                excess_ref[k, j, r] = excess
                sums_ref[TILES * j + r] += excess
        return carry

    lax.fori_loop(0, bands, band, 0)


def local_kernel(last, scal_ref, p_ref, excess_ref, *refs):
    if last:
        (out_ref,) = refs
    else:
        spec_ref, land_ref, rows_ref, out_ref, held_ref = refs
    bands = p_ref.shape[0]
    first = (lax.axis_index("freq") * bands) * STRIDE
    extra = first + 6 * ND
    some = 6

    def directions(group, carry):
        for r in range(TILES):
            if not last:
                held, sea = held_and_sea(r, land_ref, rows_ref)
                kept = jnp.where(held, sea, 0.0)
            for i in range(some):
                j = group * some + i
                lower = jnp.zeros((8, WIDTH), jnp.float32)
                for k in range(bands):
                    excess = excess_ref[k, j, r]
                    at = extra + k * STRIDE
                    rate = excess * scal_ref[at] + lower * scal_ref[at + 1]
                    value = p_ref[k, j, r] * jnp.exp(rate)
                    if not last:
                        value = value * scal_ref[first + k * STRIDE + 6 * j + 4]
                        held_ref[k, j, r] = spec_ref[k, j, tile_rows(r), :] * kept
                    out_ref[k, j, r] = value
                    lower = lower + excess
        return carry

    lax.fori_loop(0, ND // some, directions, 0)


def pair_kernel(sums_ref, other_ref, out_ref):
    first = (lax.axis_index("freq") % 2) * HALF_TILES
    for i in range(HALF_TILES):
        out_ref[i] = sums_ref[first + i] + other_ref[first + i]
    for i in range(out_ref.shape[0] - HALF_TILES):
        out_ref[HALF_TILES + i] = sums_ref[SLOPE_AT + i] + other_ref[SLOPE_AT + i]


def damp_and_gain(slope, stress, ice):
    damp = SWELL_DAMP * (slope / (slope + 1.0)) + ICE_DAMP * ice
    return damp, GROWTH * (1.0 + stress / (stress + 1.0))


def grow_half(half, last, near, refs):
    scal_ref, part_ref, sums_ref, other_ref, mine_ref, lower_ref = refs[:6]
    east_ref, north_ref, land_ref, out_ref, rate_ref, near_ref, field_ref, sent = refs[6:]
    bands = part_ref.shape[0]
    freq = lax.axis_index("freq")
    odd = jnp.where(freq % 2 == 1, 1.0, 0.0)
    upper = jnp.where(freq >= 2, 1.0, 0.0)
    after = SLOPE_AT - HALF_TILES
    for r in range(TILES):
        rows = tile_rows(r)
        ice = jnp.where(land_ref[rows, :] == 2, 1.0, 0.0)
        slope, stress = (
            (sums_ref[at + r] + other_ref[at + r]) + mine_ref[at + r - after]
            for at in (SLOPE_AT, STRESS_AT)
        )
        damp, gain = damp_and_gain(slope, stress, ice)
        east, north = east_ref[rows, :], north_ref[rows, :]
        for i in range(HALF):
            j = half * HALF + i
            lower = odd * other_ref[TILES * j + r] + upper * lower_ref[TILES * i + r]
            drive = drive_of(j, east, north, 1.0 - ice)
            rate_ref[i, r] = gain * drive - damp - LOWER * lower

    inside = None if last else inside_masks()
    target_ref = out_ref if near else field_ref

    def send(k, mine):
        source, which = (field_ref, half) if mine else (near_ref, 1 - half)
        place = out_ref.at[k, pl.ds(which * HALF, HALF)]
        return pltpu.make_async_copy(source.at[k], place, sent.at[int(mine), k])

    def band(k, carry):
        base = (freq * bands + k) * STRIDE
        root = scal_ref[base + 6 * ND + 4]
        for i in range(HALF):
            j = half * HALF + i
            tiles = [part_ref[k, j, r] * jnp.exp(rate_ref[i, r] * root) for r in range(TILES)]
            if last:
                for r in range(TILES):
                    target_ref[k, i, tile_rows(r), :] = tiles[r]
            else:
                for r, tile in enumerate(drift(j, base, tiles, scal_ref, inside)):
                    out_ref[k, j, r] = tile
        if last and not near:
            send(k, True).start()
        return carry

    write = last and not near
    if write:
        for k in range(bands):
            send(k, False).start()
    lax.fori_loop(0, bands, band, 0)
    if write:
        for k in range(bands):
            send(k, False).wait()
            send(k, True).wait()


def growth_kernel(last, near, *refs):
    operands, refs = refs[:9], refs[9:]
    scal_ref, part_ref, sums_ref, other_ref, mine_ref = operands[:5]
    freq = lax.axis_index("freq")
    rest = (None,) * 3
    if near and last:
        out_ref, slope_ref, rate_ref = refs
        for r in range(TILES):
            at = SLOPE_AT + r
            total = (sums_ref[at] + other_ref[at]) + mine_ref[at - SLOPE_AT + HALF_TILES]
            slope_ref[tile_rows(r), :] = total
    elif near:
        table_ref, packed_part_ref, packed_drive_ref, ice_ref, out_ref, columns_ref, rate_ref = refs
        odd = jnp.where(freq % 2 == 1, 1.0, 0.0)
        upper = jnp.where(freq >= 2, 1.0, 0.0)
        total, lower = [], []
        for i in range(PACKED_SUMS):
            here, there = PACKED_AT + i, HALF_TILES + 2 * TILES + i
            total.append((sums_ref[here] + other_ref[here]) + mine_ref[there])
            lower.append(odd * other_ref[here] + upper * mine_ref[there])
        slope, stress = (spread(total[i // BANDS], i % BANDS) for i in (ND, ND + 1))
        damp, gain = damp_and_gain(slope, stress, ice_ref[...])
        root = table_ref[freq, 4]
        for j in range(ND):
            under = spread(lower[j // BANDS], j % BANDS)
            rate = gain * packed_drive_ref[j] - damp - LOWER * under
            columns_ref[j] = packed_part_ref[j] * jnp.exp(root * rate)
    else:
        before_ref, out_ref, rate_ref, *rest = refs
        rest = (before_ref, *rest) if last else (None,) * 3
    for half in range(2):

        @pl.when(freq % 2 == (half if near else 1 - half))
        def _():
            grow_half(half, last, near, operands + (out_ref, rate_ref, *rest))


def cost(tiles, ops, moves):
    return pl.CostEstimate(
        flops=tiles * ops * 8 * WIDTH, bytes_accessed=tiles * moves * 32 * WIDTH, transcendentals=0
    )


def per_device(spectrum, east_wind, north_wind, land_sea, edge_rows):
    bands, count, lat_rows, width = spectrum.shape
    assert (bands, count, lat_rows, width) == (BANDS, ND, LAT, WIDTH)
    ring = lax.axis_size("lon")
    assert lax.axis_size("freq") == 4 and bands * 4 == NF and ring % 2 == 0
    f32 = jnp.float32

    def tiles(count):
        return jax.ShapeDtypeStruct((count, 8, WIDTH), f32)

    field = jax.ShapeDtypeStruct(spectrum.shape, f32)
    spread_field = jax.ShapeDtypeStruct((bands, ND, TILES, 8, WIDTH), f32)
    plane = jax.ShapeDtypeStruct((LAT, WIDTH), f32)
    tile = jax.ShapeDtypeStruct((8, WIDTH), f32)
    smem = pl.BlockSpec(memory_space=pltpu.SMEM)
    vmem = pl.BlockSpec(memory_space=pltpu.VMEM)
    hbm = pl.BlockSpec(memory_space=pltpu.HBM)
    params = pltpu.CompilerParams(vmem_limit_bytes=16 * 1024 * 1024)
    scalars, table = jnp.asarray(SCALARS), jnp.asarray(PACKED_TABLE)
    swap_core = [(0, 1), (1, 0), (2, 3), (3, 2)]
    swap_chip = [(0, 2), (2, 0), (1, 3), (3, 1)]
    swap_even = [(i, i ^ 1) for i in range(ring)]
    swap_odd = [(i, (i + (1 if i % 2 else -1)) % ring) for i in range(ring)]
    whole = bands * ND * TILES
    by_direction = pltpu.VMEM((ND, TILES, 8, WIDTH), f32)
    packed = pltpu.VMEM((ND, 8, WIDTH), f32)
    received = pltpu.VMEM((SENT, 8, WIDTH), f32)

    arguments = [spectrum, east_wind, north_wind, land_sea, edge_rows]
    spectrum, right, left, east_wind, north_wind, land_sea, edge_rows, even, odd = pl.pallas_call(
        pack_kernel,
        in_specs=[hbm] * 5,
        out_specs=[vmem] * 9,
        out_shape=[field, tiles(SENT), tiles(SENT)]
        + [jax.ShapeDtypeStruct(x.shape, x.dtype) for x in arguments[1:]]
        + [tiles(SENT), tiles(SENT)],
        scratch_shapes=[pltpu.SemaphoreType.DMA((ND // CHUNK + 4,))],
        compiler_params=params,
        cost_estimate=cost(whole, 6, 2),
        name="pack_columns",
    )(*(pltpu.with_memory_space_constraint(x, pltpu.HBM) for x in arguments))
    even = lax.ppermute(even, "lon", swap_even)
    odd = lax.ppermute(odd, "lon", swap_odd)
    drifted = pl.pallas_call(
        drift_kernel,
        in_specs=[smem, vmem],
        out_specs=vmem,
        out_shape=spread_field,
        compiler_params=params,
        cost_estimate=cost(whole, 12, 2),
        name="drift",
    )(scalars, spectrum)

    fields = [east_wind, north_wind, land_sea]
    for step in range(STEPS):
        first, last = step == 0, step == STEPS - 1
        sums = PACKED_AT + (PACKED_SUMS if first else 0)
        half_sums = sums - SLOPE_AT + HALF_TILES
        operands = [scalars, table, drifted, spectrum if first else kept, *fields, edge_rows]
        operands += [right, left, even, odd] if first else [columns]
        p, excess, mine, *packed_state = pl.pallas_call(
            functools.partial(source_kernel, first),
            in_specs=[smem] + [vmem] * (len(operands) - 1),
            out_specs=[vmem] * (6 if first else 3),
            out_shape=[spread_field, spread_field, tiles(sums)]
            + ([tiles(ND), tiles(ND), tile] if first else []),
            scratch_shapes=[by_direction, packed]
            + ([received] * 2 + [packed] * 3 if first else []),
            compiler_params=params,
            cost_estimate=cost(whole, 30, 3),
            name="sources",
        )(*operands)
        other = lax.ppermute(mine, "freq", swap_core)
        pair = pl.pallas_call(
            pair_kernel,
            in_specs=[vmem] * 2,
            out_specs=vmem,
            out_shape=tiles(half_sums),
            compiler_params=params,
            cost_estimate=cost(half_sums, 1, 3),
            name="pair_sums",
        )(mine, other)
        near = lax.ppermute(pair, "freq", swap_chip)
        excess, _ = lax.optimization_barrier((excess, pair))
        operands = [scalars, p, excess] + ([] if last else [spectrum, land_sea, edge_rows])
        part, *kept = pl.pallas_call(
            functools.partial(local_kernel, last),
            in_specs=[smem] + [vmem] * (len(operands) - 1),
            out_specs=[vmem] * (1 if last else 2),
            out_shape=[spread_field] * (1 if last else 2),
            compiler_params=params,
            cost_estimate=cost(whole, 8, 3),
            name="local_rate",
        )(*operands)
        kept = None if last else kept[0]
        near, part = lax.optimization_barrier((near, part))
        far = lax.ppermute(near, "freq", swap_core)

        near_half = jax.ShapeDtypeStruct((bands, HALF, LAT, WIDTH), f32)

        def grow(is_near, operands, shapes):
            write = last and not is_near
            scratch = [pltpu.VMEM((HALF, TILES, 8, WIDTH), f32)]
            if write:
                scratch += [pltpu.VMEM(near_half.shape, f32), pltpu.SemaphoreType.DMA((2, bands))]
            alias = not last and not is_near
            return pl.pallas_call(
                functools.partial(growth_kernel, last, is_near),
                in_specs=[smem] + [vmem] * (len(operands) - 1),
                out_specs=[hbm if write else vmem] * len(shapes),
                out_shape=shapes,
                input_output_aliases={len(operands) - 1: 0} if alias else {},
                scratch_shapes=scratch,
                compiler_params=params,
                cost_estimate=cost(whole, 6 if last else 12, 1),
                name="grow_near" if is_near else "grow_far",
            )(*operands)

        operands = [scalars, part, mine, other, near]
        extra = [] if last else [table, *packed_state]
        shapes = [near_half, plane] if last else [spread_field, tiles(ND)]
        made, columns = grow(True, operands + [near, *fields, *extra], shapes)
        shapes = [field if last else spread_field]
        (drifted,) = grow(False, operands + [far, *fields, made], shapes)
    return drifted, columns


def solution(mesh):
    in_specs = (
        P("freq", None, None, "lon"),
        P(None, "lon"),
        P(None, "lon"),
        P(None, "lon"),
        P(None, "lon"),
    )
    out_specs = (P("freq", None, None, "lon"), P(None, "lon"))
    return jax.shard_map(
        per_device, mesh=mesh, in_specs=in_specs, out_specs=out_specs, check_vma=False
    )
```

```python
import functools
import math

import jax
import jax.numpy as jnp
import numpy as np
from jax import lax
from jax.experimental import pallas as pl
from jax.experimental.pallas import tpu as pltpu
from jax.sharding import PartitionSpec as P

NF = 32
STEPS = 2

COURANT_MAX = 0.9
FREQ_RATIO = 1.1
WIND_REF = 8.0
WIND_CLIP = 2.0
GROWTH = 0.01
BREAKING = 0.3
SATURATION_REF = 0.4
CUMULATIVE = 2.0
SWELL_DAMP = 0.1
ICE_DAMP = 0.5

ND = 36
HALF = ND // 2
QUARTER = ND // 4
DTHETA = 2.0 * math.pi / ND
LOG2E = 1.0 / math.log(2.0)
ROOT_REF = math.sqrt(SATURATION_REF)
TILES = 3
LAT = 8 * TILES
WIDTH = 128
STRIDE = 6 * ND + 8

ANGLES = np.arange(ND) * DTHETA
COS = np.cos(ANGLES)
SIN = np.sin(ANGLES)
COS2 = np.cos(2.0 * ANGLES)
SIN2 = np.sin(2.0 * ANGLES)
BACK_LON = [bool(c >= 0.0) for c in COS]
BACK_LAT = [bool(s >= 0.0) for s in SIN]
RANK = [sum(BACK_LON[:j]) if BACK_LON[j] else j - sum(BACK_LON[:j]) for j in range(ND)]


def one_sided(courant):
    c = np.abs(courant)
    return 1.0 - 1.5 * c + 0.5 * c * c, 2.0 * c - c * c, 0.5 * c * c - 0.5 * c


GROUP = 32
BANDS = 8
SENT = HALF + QUARTER + 1
FIELDS = 5
SLOPE_AT = ND * TILES
STRESS_AT = SLOPE_AT + TILES
PACKED_AT = STRESS_AT + TILES
PACKED_SUMS = 5
HALF_TILES = HALF * TILES
SCALE = 0.25 * DTHETA
CAP = SATURATION_REF / SCALE
ROOT_CAP = math.sqrt(CAP)
LOWER = CUMULATIVE / NF * SCALE


def make_tables():
    ratios = FREQ_RATIO ** np.arange(NF)
    root = np.sqrt(ratios)
    lon = one_sided(COURANT_MAX * COS[None, :] / ratios[:, None])
    lat = one_sided(0.5 * COURANT_MAX * SIN[None, :] / ratios[:, None])
    scalars = np.zeros((NF, STRIDE))
    for i, value in enumerate(
        (lon[1] / lon[0], lon[2] / lon[0], lat[1] / lat[0], lat[2] / lat[0], lon[0] * lat[0])
    ):
        scalars[:, i : 6 * ND : 6] = value
    rest = [
        -BREAKING / SATURATION_REF * SCALE * root,
        -LOWER * root,
        ratios * ratios * DTHETA / np.sum(ratios * ratios),
        ratios * root * DTHETA / np.sum(ratios * root),
        root,
        1.0 / ratios,
    ]
    packed = np.zeros((NF // BANDS, len(rest), 8, WIDTH))
    for i, value in enumerate(rest):
        scalars[:, 6 * ND + i] = value
        for lane in range(TILES * GROUP):
            packed[:, i, :, lane] = value[lane // 4 % BANDS :: BANDS, None]
    return scalars.reshape(-1).astype(np.float32), packed.astype(np.float32)


SCALARS, PACKED_TABLE = make_tables()


def lanes():
    return lax.broadcasted_iota(jnp.int32, (8, WIDTH), 1)


def sublanes():
    return lax.broadcasted_iota(jnp.int32, (8, WIDTH), 0)


def turn(tile, shift):
    shift = shift % WIDTH
    return tile if shift == 0 else pltpu.roll(tile, shift, 1)


def tile_rows(r):
    return slice(8 * r, 8 * r + 8)


CHUNK = 4


def pack_kernel(spec_ref, *refs):
    sources, (copy_ref, right_ref, left_ref), held_refs = refs[:4], refs[4:7], refs[7:11]
    to_even_ref, to_odd_ref, arrived = refs[11:]

    def fetch(c):
        part = pl.ds(CHUNK * c, CHUNK)
        return pltpu.make_async_copy(spec_ref.at[:, part], copy_ref.at[:, part], arrived.at[c])

    small = [
        pltpu.make_async_copy(source, target, arrived.at[ND // CHUNK + i])
        for i, (source, target) in enumerate(zip(sources, held_refs))
    ]
    for c in range(ND // CHUNK):
        fetch(c).start()
    for copy in small:
        copy.start()
    lane = lanes()
    zero = jnp.zeros((8, WIDTH), jnp.float32)
    held = [zero, zero]
    spot = {True: (lane + (WIDTH - 4)) % WIDTH, False: (lane + 2) % WIDTH}
    for j in range(ND):
        if j % CHUNK == 0:
            fetch(j // CHUNK).wait()
        back = BACK_LON[j]
        wide, narrow = (right_ref, left_ref) if back else (left_ref, right_ref)
        half = RANK[j] % 2
        first, aside = (WIDTH - 4, 4) if back else (0, -2)
        fours, twos = [], []
        for r in range(TILES):
            four, two = zero, zero
            for k in range(BANDS):
                place = GROUP * r + 4 * k
                tile = turn(copy_ref[k, j, tile_rows(r), :], place - first)
                four = jnp.where(lane // 4 % BANDS == k, tile, four)
                two = jnp.where(spot[back] // 4 % BANDS == k, tile, two)
            fours.append(four)
            twos.append(two)
        four = jnp.where(lane < GROUP, fours[0], jnp.where(lane < 2 * GROUP, fours[1], fours[2]))
        two = jnp.where(
            spot[back] < GROUP, twos[0], jnp.where(spot[back] < 2 * GROUP, twos[1], twos[2])
        )
        four = jnp.where(lane < TILES * GROUP, four, 0.0)
        wide[RANK[j]] = four
        two = turn(two, 2 * half - aside)
        if half:
            narrow[HALF + RANK[j] // 2] = jnp.where(lane % 4 < 2, held[back], two)
        else:
            held[back] = two
    for copy in small:
        copy.wait()
    east_ref, north_ref, land_ref, rows_ref = held_refs
    fields = [
        [f(r) for r in range(TILES)]
        for f in (
            lambda r: east_ref[tile_rows(r), :],
            lambda r: north_ref[tile_rows(r), :],
            lambda r: land_ref[tile_rows(r), :].astype(jnp.float32),
            lambda r: jnp.broadcast_to(rows_ref[0:1, :].astype(jnp.float32), (8, WIDTH)),
            lambda r: jnp.broadcast_to(rows_ref[1:2, :].astype(jnp.float32), (8, WIDTH)),
        )
    ]
    to_right, to_left = zero, zero
    for i in range(FIELDS):
        for r in range(TILES):
            place = GROUP * r + 4 * i
            here = lane // 2 == place // 2
            to_right = jnp.where(here, turn(fields[i][r], place - (WIDTH - 2)), to_right)
            to_left = jnp.where(here, turn(fields[i][r], place), to_left)
    right_ref[SENT - 1] = to_right
    left_ref[SENT - 1] = to_left
    odd = lax.axis_index("lon") % 2 == 1
    for i in range(SENT):
        right, left = right_ref[i], left_ref[i]
        to_even_ref[i] = jnp.where(odd, left, right)
        to_odd_ref[i] = jnp.where(odd, right, left)


def drive_of(j, east, north, open_water):
    along = float(COS[j] / WIND_REF) * east + float(SIN[j] / WIND_REF) * north
    drive = jnp.minimum(jnp.maximum(along, 0.0), WIND_CLIP)
    return drive * drive * open_water


def tree(values):
    values = list(values)
    while len(values) > 1:
        values = [sum(values[i + 1 : i + 2], values[i]) for i in range(0, len(values), 2)]
    return values[0]


def saturation_of(p):
    diff = [p[b] - p[b + HALF] for b in range(HALF)]
    both = [p[b] + p[b + HALF] for b in range(HALF)]
    folded = [both[b] + both[b + QUARTER] for b in range(QUARTER)]
    total = tree(folded)
    fold = [both[b] - both[b + QUARTER] for b in range(QUARTER)]
    total_c = tree([fold[0]] + [fold[b] * float(COS2[b]) for b in range(1, QUARTER)])
    total_s = tree([fold[b] * float(SIN2[b]) for b in range(1, QUARTER)])
    level = [None] * HALF
    for a in range(QUARTER):
        wave = total_c * float(COS2[a])
        if a:
            wave = wave + total_s * float(SIN2[a])
        level[a] = total + wave
        level[a + QUARTER] = total - wave

    def at(b):
        return diff[b % HALF], b // HALF % 2 == 1

    def minus(a, b):
        x, flip_x = at(a)
        y, flip_y = at(b)
        if flip_x:
            return y - x if flip_y else None, (x, y)
        return x + y if flip_y else x - y, None

    def plus_minus(value, a, b):
        gap, opposite = minus(a, b)
        if gap is None:
            return value - (opposite[0] + opposite[1])
        return value + gap

    waves = []
    for a in range(2):
        pairs = [minus(a + d, a - d + HALF)[0] for d in range(1, QUARTER)]
        weighted = [pairs[d - 1] * float(COS2[d]) for d in range(1, QUARTER)]
        waves.append(tree([diff[a]] + weighted))
        if a == 0:
            plain = tree([diff[0]] + pairs)
    twice = float(2.0 * COS2[1])
    odd, below = [None] * HALF, [None] * HALF
    odd[0] = plain + waves[0]
    window, before, now = plain, waves[0], waves[1]
    for a in range(1, QUARTER + 1):
        window = plus_minus(window, a + 8, a - 9)
        odd[a] = window + now
        if a < QUARTER:
            rest = plus_minus(before, a + 10, a + 8)
            before, now = now, twice * now - rest
    window, after, now = plain, waves[1], waves[0]
    for a in range(0, -(QUARTER - 1), -1):
        rest = plus_minus(after, a + 10, a + 8)
        after, now = now, twice * now - rest
        window = plus_minus(window, a - 9 + 2 * HALF, a + 8)
        below[a - 1 + HALF] = window + now
    out = [None] * ND
    for a in range(HALF):
        if odd[a] is not None:
            out[a], out[a + HALF] = level[a] + odd[a], level[a] - odd[a]
        else:
            out[a], out[a + HALF] = level[a] - below[a], level[a] + below[a]
    return out


def inside_masks():
    lane = lanes()
    one = jnp.ones((8, WIDTH), jnp.float32)
    return {
        (True, 1): jnp.where(lane >= 1, one, 0.0),
        (True, 2): jnp.where(lane >= 2, one, 0.0),
        (False, 1): jnp.where(lane < WIDTH - 1, one, 0.0),
        (False, 2): jnp.where(lane < WIDTH - 2, one, 0.0),
    }


def drift(j, base, tiles, scal_ref, inside):
    c1, c2, d1, d2 = (scal_ref[base + 6 * j + i] for i in range(4))
    side = 1 if BACK_LON[j] else -1
    c1 = c1 * inside[BACK_LON[j], 1]
    c2 = c2 * inside[BACK_LON[j], 2]
    x = [q + c1 * turn(q, side) + c2 * turn(q, 2 * side) for q in tiles]
    row = sublanes()
    one, two = (1, 2) if BACK_LAT[j] else (7, 6)
    at_edge = (row < 1, row < 2) if BACK_LAT[j] else (row >= 7, row >= 6)
    order = range(TILES) if BACK_LAT[j] else range(TILES - 1, -1, -1)
    moved = [[pltpu.roll(tile, by, 0) for tile in x] for by in (one, two)]
    y = [None] * TILES
    before = None
    for r in order:
        first = x[r] if before is None else moved[0][before]
        near = jnp.where(at_edge[0], first, moved[0][r])
        second = near if before is None else moved[1][before]
        far = jnp.where(at_edge[1], second, moved[1][r])
        y[r] = x[r] + d1 * near + d2 * far
        before = r
    return y


def drift_kernel(scal_ref, q_ref, east_ref, north_ref, land_ref, out_ref, drive_ref):
    bands = q_ref.shape[0]
    for r in range(TILES):
        rows = tile_rows(r)
        water = jnp.where(land_ref[rows, :] == 2, 0.0, 1.0)
        east, north = east_ref[rows, :], north_ref[rows, :]
        for j in range(ND):
            drive_ref[j, r] = drive_of(j, east, north, water)
    inside = inside_masks()

    def band(k, carry):
        base = (lax.axis_index("freq") * bands + k) * STRIDE
        for j in range(ND):
            factor = scal_ref[base + 6 * j + 4]
            tiles = [q_ref[k, j, tile_rows(r), :] * factor for r in range(TILES)]
            for r, tile in enumerate(drift(j, base, tiles, scal_ref, inside)):
                out_ref[k, j, r] = tile
        return carry

    lax.fori_loop(0, bands, band, 0)


def packed_lat(j, x, d0, d1, d2):
    lane, row = lanes(), sublanes()

    def shifted(x):
        if BACK_LAT[j]:
            moved = pltpu.roll(x, 1, 0)
            over = jnp.where(lane < GROUP, x, turn(moved, GROUP))
            return jnp.where(row >= 1, moved, over)
        moved = pltpu.roll(x, 7, 0)
        over = jnp.where(lane >= (TILES - 1) * GROUP, x, turn(moved, -GROUP))
        return jnp.where(row <= 6, moved, over)

    near = shifted(x)
    return d0 * x + d1 * near + d2 * shifted(near)


def spread(tile, position):
    at_first = lanes() // 4 % BANDS == 0
    tile = jnp.where(at_first, turn(tile, -4 * position), 0.0)
    for step in (1, 2, 4):
        tile = tile + turn(tile, 4 * step)
    return tile


def packed_coefficients(inverse, speed):
    c = inverse * abs(float(speed))
    return 1.0 + c * (0.5 * c - 1.5), c * (2.0 - c), c * (0.5 * c - 0.5)


AHEAD = [j for j in range(ND) if not BACK_LON[j]]
BACK = [j for j in range(ND) if BACK_LON[j]]


def packed_fix(table, columns_ref, fix_ref):
    slot = lanes() % 4
    inverse = table(5)

    def one(j):
        back = BACK_LON[j]
        _, c1, c2 = packed_coefficients(inverse, COURANT_MAX * COS[j])
        tile = columns_ref[j]
        next_one = jnp.where(slot == (0 if back else 3), turn(tile, -1 if back else 1), 0.0)
        first = c2 * tile + c1 * next_one
        lat = packed_coefficients(inverse, 0.5 * COURANT_MAX * SIN[j])
        return packed_lat(j, first, *lat)

    for i in range(HALF):
        fix_ref[i] = jnp.where(slot < 2, one(BACK[i]), turn(one(AHEAD[i]), -4))


def packed_start(mine_right_ref, mine_left_ref, left_ref, right_ref, columns_ref, side_refs):
    near_ref, far_ref = side_refs
    lane = lanes()
    slot = lane % 4
    used = lane < TILES * GROUP
    for j in range(ND):
        half = RANK[j] % 2
        narrow = HALF + RANK[j] // 2
        if BACK_LON[j]:
            wide, own = left_ref[RANK[j]], mine_right_ref[RANK[j]]
            other = turn(right_ref[narrow], 2 - 2 * half)
            centre = jnp.where(slot < 2, turn(wide, -2), other)
            near = turn(jnp.where(slot == 3, own, wide), -1)
            near = jnp.where(slot == 3, turn(centre, 1), near)
            far = jnp.where(slot < 2, wide, own)
        else:
            wide, own = right_ref[RANK[j]], mine_left_ref[RANK[j]]
            other = turn(left_ref[narrow], -2 * half)
            centre = jnp.where(slot < 2, other, turn(wide, 2))
            near = turn(jnp.where(slot == 0, own, wide), 1)
            near = jnp.where(slot == 0, turn(centre, -1), near)
            far = jnp.where(slot < 2, own, wide)
        columns_ref[j] = jnp.where(used, centre, 0.0)
        near_ref[j] = jnp.where(used, near, 0.0)
        far_ref[j] = jnp.where(used, far, 0.0)


def packed_source(
    table, left_ref, right_ref, columns_ref, side_refs, sums_ref, part_ref, drive_ref, ice_ref
):
    near_ref, far_ref = side_refs
    lane = lanes()
    slot, place = lane % 4, lane // 4 % BANDS
    both = jnp.where(slot < 2, left_ref[SENT - 1], turn(right_ref[SENT - 1], 2))
    east, north, land, south_rows, north_rows = (spread(both, i) for i in range(FIELDS))
    row = (sublanes() + lane // GROUP * 8).astype(jnp.float32)
    held = (row < south_rows) | (row >= LAT - north_rows)
    sea = jnp.where(land > 0.5, 1.0, 0.0)
    ice = jnp.where(land > 1.5, 1.0, 0.0)
    ice_ref[...] = ice
    inverse = table(5)
    p, stress = [], []
    for j in range(ND):
        lon = packed_coefficients(inverse, COURANT_MAX * COS[j])
        lat = packed_coefficients(inverse, 0.5 * COURANT_MAX * SIN[j])
        centre = columns_ref[j]
        x = lon[0] * centre + lon[1] * near_ref[j] + lon[2] * far_ref[j]
        x = packed_lat(j, x, *lat)
        p.append(jnp.where(held, centre, jnp.maximum(x, 0.0)) * sea)
        drive = drive_of(j, east, north, 1.0 - ice)
        drive_ref[j] = drive
        stress.append(p[j] * drive)
    slope, stress = tree(p), tree(stress)

    def running(tile):
        for step in (1, 2, 4):
            tile = tile + jnp.where(place >= step, turn(tile, 4 * step), 0.0)
        return tile

    out = [jnp.zeros((8, WIDTH), jnp.float32) for _ in range(PACKED_SUMS)]

    def put(index, tile):
        position = index % BANDS
        moved = turn(tile, 4 * (position - (BANDS - 1)))
        out[index // BANDS] = jnp.where(place == position, moved, out[index // BANDS])

    for j, excess in enumerate(excess_of(p)):
        total = running(excess)
        put(j, total)
        rate = excess * table(0) + (total - excess) * table(1)
        part_ref[j] = p[j] * jnp.exp(rate)
    put(ND, running(slope * table(2)))
    put(ND + 1, running(stress * table(3)))
    for i in range(PACKED_SUMS):
        sums_ref[PACKED_AT + i] = out[i]


def excess_of(p):
    out = []
    for saturation in saturation_of(p):
        capped = jnp.maximum(saturation, CAP)
        excess = capped * lax.rsqrt(capped) - ROOT_CAP
        out.append(excess * excess)
    return out


def held_and_sea(r, land_ref, rows_ref):
    row = sublanes() + 8 * r
    held = (row < rows_ref[0:1, :]) | (row >= LAT - rows_ref[1:2, :])
    return held, jnp.where(land_ref[tile_rows(r), :] != 0, 1.0, 0.0)


def source_kernel(first, *refs):
    scal_ref, table_ref, x_ref, spec_ref, drive_ref, land_ref, rows_ref = refs[:7]
    refs = refs[7:]
    freq = lax.axis_index("freq")
    bands = x_ref.shape[0]

    def table(i):
        return table_ref[freq, i]

    if first:
        mine_right_ref, mine_left_ref, even_ref, odd_ref = refs[:4]
        p_ref, excess_ref, sums_ref, part_ref, packed_drive_ref, ice_ref = refs[4:10]
        fix_ref, left_ref, right_ref, columns_ref, near_ref, far_ref = refs[10:]
        odd = lax.axis_index("lon") % 2 == 1
        for i in range(SENT):
            even, other = even_ref[i], odd_ref[i]
            left_ref[i] = jnp.where(odd, even, other)
            right_ref[i] = jnp.where(odd, other, even)
        sides = (near_ref, far_ref)
        packed_start(mine_right_ref, mine_left_ref, left_ref, right_ref, columns_ref, sides)
        packed_source(
            table, left_ref, right_ref, columns_ref, sides,
            sums_ref, part_ref, packed_drive_ref, ice_ref,
        )
    else:
        columns_ref, p_ref, excess_ref, sums_ref, fix_ref = refs
    packed_fix(table, columns_ref, fix_ref)
    for i in range(PACKED_AT):
        sums_ref[i] = jnp.zeros((8, WIDTH), jnp.float32)

    lane = lanes()
    at_edge = {True: lane < 2, False: lane >= WIDTH - 2}

    def band(k, carry):
        extra = (freq * bands + k) * STRIDE + 6 * ND
        for r in range(TILES):
            rows = tile_rows(r)
            held, sea = held_and_sea(r, land_ref, rows_ref)
            if not first:
                free = jnp.where(held, 0.0, sea)
            shift = jnp.bitwise_and(WIDTH - GROUP * r - 4 * k, WIDTH - 1)
            p = [None] * ND
            for i in range(HALF):
                moved = pltpu.roll(fix_ref[i], shift, 1)
                for j in (BACK[i], AHEAD[i]):
                    x = x_ref[k, j, r] + jnp.where(at_edge[BACK_LON[j]], moved, 0.0)
                    if first:
                        x = jnp.where(held, spec_ref[k, j, rows, :], jnp.maximum(x, 0.0)) * sea
                    else:
                        x = jnp.maximum(x * free, spec_ref[k, j, r])
                    p_ref[k, j, r] = x
                    p[j] = x
            slope = tree(p)
            stress = tree([p[j] * drive_ref[j, r] for j in range(ND)])
            sums_ref[SLOPE_AT + r] += slope * scal_ref[extra + 2]
            sums_ref[STRESS_AT + r] += stress * scal_ref[extra + 3]
            for j, excess in enumerate(excess_of(p)):
                excess_ref[k, j, r] = excess
                sums_ref[TILES * j + r] += excess
        return carry

    lax.fori_loop(0, bands, band, 0)


def local_kernel(last, scal_ref, p_ref, excess_ref, *refs):
    if last:
        (out_ref,) = refs
    else:
        spec_ref, land_ref, rows_ref, out_ref, held_ref = refs
    bands = p_ref.shape[0]
    first = (lax.axis_index("freq") * bands) * STRIDE
    extra = first + 6 * ND
    some = 6

    def directions(group, carry):
        for r in range(TILES):
            if not last:
                held, sea = held_and_sea(r, land_ref, rows_ref)
                kept = jnp.where(held, sea, 0.0)
            for i in range(some):
                j = group * some + i
                lower = jnp.zeros((8, WIDTH), jnp.float32)
                for k in range(bands):
                    excess = excess_ref[k, j, r]
                    at = extra + k * STRIDE
                    rate = excess * scal_ref[at] + lower * scal_ref[at + 1]
                    value = p_ref[k, j, r] * jnp.exp(rate)
                    if not last:
                        value = value * scal_ref[first + k * STRIDE + 6 * j + 4]
                        held_ref[k, j, r] = spec_ref[k, j, tile_rows(r), :] * kept
                    out_ref[k, j, r] = value
                    lower = lower + excess
        return carry

    lax.fori_loop(0, ND // some, directions, 0)


def pair_kernel(sums_ref, other_ref, out_ref):
    first = (lax.axis_index("freq") % 2) * HALF_TILES
    for i in range(HALF_TILES):
        out_ref[i] = sums_ref[first + i] + other_ref[first + i]
    for i in range(out_ref.shape[0] - HALF_TILES):
        out_ref[HALF_TILES + i] = sums_ref[SLOPE_AT + i] + other_ref[SLOPE_AT + i]


def damp_and_gain(slope, stress, ice):
    damp = SWELL_DAMP * (slope / (slope + 1.0)) + ICE_DAMP * ice
    return damp, GROWTH * (1.0 + stress / (stress + 1.0))


def grow_half(half, last, near, refs):
    scal_ref, part_ref, sums_ref, other_ref, mine_ref, lower_ref = refs[:6]
    drive_ref, land_ref, out_ref, rate_ref, near_ref, field_ref, sent = refs[6:]
    bands = part_ref.shape[0]
    freq = lax.axis_index("freq")
    odd = jnp.where(freq % 2 == 1, 1.0, 0.0)
    upper = jnp.where(freq >= 2, 1.0, 0.0)
    after = SLOPE_AT - HALF_TILES
    for r in range(TILES):
        rows = tile_rows(r)
        ice = jnp.where(land_ref[rows, :] == 2, 1.0, 0.0)
        slope, stress = (
            (sums_ref[at + r] + other_ref[at + r]) + mine_ref[at + r - after]
            for at in (SLOPE_AT, STRESS_AT)
        )
        damp, gain = damp_and_gain(slope, stress, ice)
        for i in range(HALF):
            j = half * HALF + i
            lower = odd * other_ref[TILES * j + r] + upper * lower_ref[TILES * i + r]
            rate_ref[i, r] = gain * drive_ref[j, r] - damp - LOWER * lower

    inside = None if last else inside_masks()
    target_ref = out_ref if near else field_ref

    def send(k, mine):
        source, which = (field_ref, half) if mine else (near_ref, 1 - half)
        place = out_ref.at[k, pl.ds(which * HALF, HALF)]
        return pltpu.make_async_copy(source.at[k], place, sent.at[int(mine), k])

    def band(k, carry):
        base = (freq * bands + k) * STRIDE
        root = scal_ref[base + 6 * ND + 4]
        for i in range(HALF):
            j = half * HALF + i
            tiles = [part_ref[k, j, r] * jnp.exp(rate_ref[i, r] * root) for r in range(TILES)]
            if last:
                for r in range(TILES):
                    target_ref[k, i, tile_rows(r), :] = tiles[r]
            else:
                for r, tile in enumerate(drift(j, base, tiles, scal_ref, inside)):
                    out_ref[k, j, r] = tile
        if last and not near:
            send(k, True).start()
        return carry

    write = last and not near
    if write:
        for k in range(bands):
            send(k, False).start()
    lax.fori_loop(0, bands, band, 0)
    if write:
        for k in range(bands):
            send(k, False).wait()
            send(k, True).wait()


def growth_kernel(last, near, *refs):
    operands, refs = refs[:8], refs[8:]
    scal_ref, part_ref, sums_ref, other_ref, mine_ref = operands[:5]
    freq = lax.axis_index("freq")
    rest = (None,) * 3
    if near and last:
        out_ref, slope_out_ref, rate_ref, slope_ref, slope_sent = refs
        for r in range(TILES):
            at = SLOPE_AT + r
            total = (sums_ref[at] + other_ref[at]) + mine_ref[at - SLOPE_AT + HALF_TILES]
            slope_ref[tile_rows(r), :] = total
        slope_copy = pltpu.make_async_copy(slope_ref, slope_out_ref, slope_sent)
        slope_copy.start()
    elif near:
        table_ref, packed_part_ref, packed_drive_ref, ice_ref, out_ref, columns_ref, rate_ref = refs
        odd = jnp.where(freq % 2 == 1, 1.0, 0.0)
        upper = jnp.where(freq >= 2, 1.0, 0.0)
        total, lower = [], []
        for i in range(PACKED_SUMS):
            here, there = PACKED_AT + i, HALF_TILES + 2 * TILES + i
            total.append((sums_ref[here] + other_ref[here]) + mine_ref[there])
            lower.append(odd * other_ref[here] + upper * mine_ref[there])
        slope, stress = (spread(total[i // BANDS], i % BANDS) for i in (ND, ND + 1))
        damp, gain = damp_and_gain(slope, stress, ice_ref[...])
        root = table_ref[freq, 4]
        for j in range(ND):
            under = spread(lower[j // BANDS], j % BANDS)
            rate = gain * packed_drive_ref[j] - damp - LOWER * under
            columns_ref[j] = packed_part_ref[j] * jnp.exp(root * rate)
    else:
        before_ref, out_ref, rate_ref, *rest = refs
        rest = (before_ref, *rest) if last else (None,) * 3
    for half in range(2):

        @pl.when(freq % 2 == (half if near else 1 - half))
        def _():
            grow_half(half, last, near, operands + (out_ref, rate_ref, *rest))

    if near and last:
        slope_copy.wait()


def cost(tiles, ops, moves):
    return pl.CostEstimate(
        flops=tiles * ops * 8 * WIDTH, bytes_accessed=tiles * moves * 32 * WIDTH, transcendentals=0
    )


def per_device(spectrum, east_wind, north_wind, land_sea, edge_rows):
    bands, count, lat_rows, width = spectrum.shape
    assert (bands, count, lat_rows, width) == (BANDS, ND, LAT, WIDTH)
    ring = lax.axis_size("lon")
    assert lax.axis_size("freq") == 4 and bands * 4 == NF and ring % 2 == 0
    f32 = jnp.float32

    def tiles(count):
        return jax.ShapeDtypeStruct((count, 8, WIDTH), f32)

    field = jax.ShapeDtypeStruct(spectrum.shape, f32)
    spread_field = jax.ShapeDtypeStruct((bands, ND, TILES, 8, WIDTH), f32)
    plane = jax.ShapeDtypeStruct((LAT, WIDTH), f32)
    tile = jax.ShapeDtypeStruct((8, WIDTH), f32)
    smem = pl.BlockSpec(memory_space=pltpu.SMEM)
    vmem = pl.BlockSpec(memory_space=pltpu.VMEM)
    hbm = pl.BlockSpec(memory_space=pltpu.HBM)
    params = pltpu.CompilerParams(vmem_limit_bytes=16 * 1024 * 1024)
    scalars, table = jnp.asarray(SCALARS), jnp.asarray(PACKED_TABLE)
    swap_core = [(0, 1), (1, 0), (2, 3), (3, 2)]
    swap_chip = [(0, 2), (2, 0), (1, 3), (3, 1)]
    swap_even = [(i, i ^ 1) for i in range(ring)]
    swap_odd = [(i, (i + (1 if i % 2 else -1)) % ring) for i in range(ring)]
    whole = bands * ND * TILES
    packed = pltpu.VMEM((ND, 8, WIDTH), f32)
    received = pltpu.VMEM((SENT, 8, WIDTH), f32)

    arguments = [spectrum, east_wind, north_wind, land_sea, edge_rows]
    spectrum, right, left, east_wind, north_wind, land_sea, edge_rows, even, odd = pl.pallas_call(
        pack_kernel,
        in_specs=[hbm] * 5,
        out_specs=[vmem] * 9,
        out_shape=[field, tiles(SENT), tiles(SENT)]
        + [jax.ShapeDtypeStruct(x.shape, x.dtype) for x in arguments[1:]]
        + [tiles(SENT), tiles(SENT)],
        scratch_shapes=[pltpu.SemaphoreType.DMA((ND // CHUNK + 4,))],
        compiler_params=params,
        cost_estimate=cost(whole, 6, 2),
        name="pack_columns",
    )(*(pltpu.with_memory_space_constraint(x, pltpu.HBM) for x in arguments))
    even = lax.ppermute(even, "lon", swap_even)
    odd = lax.ppermute(odd, "lon", swap_odd)
    drifted, drive = pl.pallas_call(
        drift_kernel,
        in_specs=[smem] + [vmem] * 4,
        out_specs=[vmem] * 2,
        out_shape=[spread_field, jax.ShapeDtypeStruct((ND, TILES, 8, WIDTH), f32)],
        compiler_params=params,
        cost_estimate=cost(whole, 12, 2),
        name="drift",
    )(scalars, spectrum, east_wind, north_wind, land_sea)

    fields = [drive, land_sea]
    for step in range(STEPS):
        first, last = step == 0, step == STEPS - 1
        sums = PACKED_AT + (PACKED_SUMS if first else 0)
        half_sums = sums - SLOPE_AT + HALF_TILES
        operands = [scalars, table, drifted, spectrum if first else kept, *fields, edge_rows]
        operands += [right, left, even, odd] if first else [columns]
        p, excess, mine, *packed_state = pl.pallas_call(
            functools.partial(source_kernel, first),
            in_specs=[smem] + [vmem] * (len(operands) - 1),
            out_specs=[vmem] * (6 if first else 3),
            out_shape=[spread_field, spread_field, tiles(sums)]
            + ([tiles(ND), tiles(ND), tile] if first else []),
            scratch_shapes=[packed]
            + ([received] * 2 + [packed] * 3 if first else []),
            compiler_params=params,
            cost_estimate=cost(whole, 30, 3),
            name="sources",
        )(*operands)
        other = lax.ppermute(mine, "freq", swap_core)
        pair = pl.pallas_call(
            pair_kernel,
            in_specs=[vmem] * 2,
            out_specs=vmem,
            out_shape=tiles(half_sums),
            compiler_params=params,
            cost_estimate=cost(half_sums, 1, 3),
            name="pair_sums",
        )(mine, other)
        near = lax.ppermute(pair, "freq", swap_chip)
        excess, _ = lax.optimization_barrier((excess, pair))
        operands = [scalars, p, excess] + ([] if last else [spectrum, land_sea, edge_rows])
        part, *kept = pl.pallas_call(
            functools.partial(local_kernel, last),
            in_specs=[smem] + [vmem] * (len(operands) - 1),
            out_specs=[vmem] * (1 if last else 2),
            out_shape=[spread_field] * (1 if last else 2),
            compiler_params=params,
            cost_estimate=cost(whole, 8, 3),
            name="local_rate",
        )(*operands)
        kept = None if last else kept[0]
        near, part = lax.optimization_barrier((near, part))
        far = lax.ppermute(near, "freq", swap_core)

        near_half = jax.ShapeDtypeStruct((bands, HALF, LAT, WIDTH), f32)

        def grow(is_near, operands, shapes):
            write = last and not is_near
            scratch = [pltpu.VMEM((HALF, TILES, 8, WIDTH), f32)]
            if write:
                scratch += [pltpu.VMEM(near_half.shape, f32), pltpu.SemaphoreType.DMA((2, bands))]
            elif last:
                scratch += [pltpu.VMEM(plane.shape, f32), pltpu.SemaphoreType.DMA(())]
            alias = not last and not is_near
            return pl.pallas_call(
                functools.partial(growth_kernel, last, is_near),
                in_specs=[smem] + [vmem] * (len(operands) - 1),
                out_specs=[hbm] if write else [vmem, hbm if last else vmem][: len(shapes)],
                out_shape=shapes,
                input_output_aliases={len(operands) - 1: 0} if alias else {},
                scratch_shapes=scratch,
                compiler_params=params,
                cost_estimate=cost(whole, 6 if last else 12, 1),
                name="grow_near" if is_near else "grow_far",
            )(*operands)

        operands = [scalars, part, mine, other, near]
        extra = [] if last else [table, *packed_state]
        shapes = [near_half, plane] if last else [spread_field, tiles(ND)]
        made, columns = grow(True, operands + [near, *fields, *extra], shapes)
        shapes = [field if last else spread_field]
        (drifted,) = grow(False, operands + [far, *fields, made], shapes)
    return drifted, columns


def solution(mesh):
    in_specs = (
        P("freq", None, None, "lon"),
        P(None, "lon"),
        P(None, "lon"),
        P(None, "lon"),
        P(None, "lon"),
    )
    out_specs = (P("freq", None, None, "lon"), P(None, "lon"))
    return jax.shard_map(
        per_device, mesh=mesh, in_specs=in_specs, out_specs=out_specs, check_vma=False
    )
```

```python
import functools
import math

import jax
import jax.numpy as jnp
import numpy as np
from jax import lax
from jax.experimental import pallas as pl
from jax.experimental.pallas import tpu as pltpu
from jax.sharding import PartitionSpec as P

NF = 32
STEPS = 2

COURANT_MAX = 0.9
FREQ_RATIO = 1.1
WIND_REF = 8.0
WIND_CLIP = 2.0
GROWTH = 0.01
BREAKING = 0.3
SATURATION_REF = 0.4
CUMULATIVE = 2.0
SWELL_DAMP = 0.1
ICE_DAMP = 0.5

ND = 36
HALF = ND // 2
QUARTER = ND // 4
DTHETA = 2.0 * math.pi / ND
LOG2E = 1.0 / math.log(2.0)
ROOT_REF = math.sqrt(SATURATION_REF)
TILES = 3
LAT = 8 * TILES
WIDTH = 128
STRIDE = 6 * ND + 8

ANGLES = np.arange(ND) * DTHETA
COS = np.cos(ANGLES)
SIN = np.sin(ANGLES)
COS2 = np.cos(2.0 * ANGLES)
SIN2 = np.sin(2.0 * ANGLES)
BACK_LON = [bool(c >= 0.0) for c in COS]
BACK_LAT = [bool(s >= 0.0) for s in SIN]
RANK = [sum(BACK_LON[:j]) if BACK_LON[j] else j - sum(BACK_LON[:j]) for j in range(ND)]


def one_sided(courant):
    c = np.abs(courant)
    return 1.0 - 1.5 * c + 0.5 * c * c, 2.0 * c - c * c, 0.5 * c * c - 0.5 * c


GROUP = 32
BANDS = 8
SENT = HALF + QUARTER + 1
FIELDS = 5
PACKED_AT = ND * TILES
PACKED_SUMS = 5
HALF_TILES = HALF * TILES
SCALE = 0.25 * DTHETA
CAP = SATURATION_REF / SCALE
ROOT_CAP = math.sqrt(CAP)
LOWER = CUMULATIVE / NF * SCALE


def make_tables():
    ratios = FREQ_RATIO ** np.arange(NF)
    root = np.sqrt(ratios)
    lon = one_sided(COURANT_MAX * COS[None, :] / ratios[:, None])
    lat = one_sided(0.5 * COURANT_MAX * SIN[None, :] / ratios[:, None])
    scalars = np.zeros((NF, STRIDE))
    for i, value in enumerate(
        (lon[1] / lon[0], lon[2] / lon[0], lat[1] / lat[0], lat[2] / lat[0], lon[0] * lat[0])
    ):
        scalars[:, i : 6 * ND : 6] = value
    rest = [
        -BREAKING / SATURATION_REF * SCALE * root,
        -LOWER * root,
        ratios * ratios * DTHETA / np.sum(ratios * ratios),
        ratios * root * DTHETA / np.sum(ratios * root),
        root,
        1.0 / ratios,
    ]
    packed = np.zeros((NF // BANDS, len(rest), 8, WIDTH))
    for i, value in enumerate(rest):
        scalars[:, 6 * ND + i] = value
        for lane in range(TILES * GROUP):
            packed[:, i, :, lane] = value[lane // 4 % BANDS :: BANDS, None]
    return scalars.reshape(-1).astype(np.float32), packed.astype(np.float32)


SCALARS, PACKED_TABLE = make_tables()


def lanes():
    return lax.broadcasted_iota(jnp.int32, (8, WIDTH), 1)


def sublanes():
    return lax.broadcasted_iota(jnp.int32, (8, WIDTH), 0)


def turn(tile, shift):
    shift = shift % WIDTH
    return tile if shift == 0 else pltpu.roll(tile, shift, 1)


def tile_rows(r):
    return slice(8 * r, 8 * r + 8)


def pack_kernel(spec_ref, *refs):
    sources, (copy_ref, right_ref, left_ref), held_refs = refs[:4], refs[4:7], refs[7:11]
    to_even_ref, to_odd_ref, arrived, four_ref, two_ref = refs[11:]

    def fetch(k):
        return pltpu.make_async_copy(spec_ref.at[k], copy_ref.at[k], arrived.at[k])

    small = [
        pltpu.make_async_copy(source, target, arrived.at[BANDS + i])
        for i, (source, target) in enumerate(zip(sources, held_refs))
    ]
    for k in range(BANDS):
        fetch(k).start()
    for copy in small:
        copy.start()
    lane = lanes()
    zero = jnp.zeros((8, WIDTH), jnp.float32)

    def by_tile(spot, tiles):
        return jnp.where(spot < GROUP, tiles[0], jnp.where(spot < 2 * GROUP, tiles[1], tiles[2]))

    first = {True: WIDTH - 4, False: 0}
    aside = {True: 4, False: -2}
    spot = {back: (lane - aside[back]) % WIDTH for back in aside}
    for k in range(BANDS):
        fetch(k).wait()
        for j in range(ND):
            back = BACK_LON[j]
            tiles = [
                turn(copy_ref[k, j, tile_rows(r), :], GROUP * r + 4 * k - first[back])
                for r in range(TILES)
            ]
            four, two = by_tile(lane, tiles), by_tile(spot[back], tiles)
            if k:
                four = jnp.where(lane // 4 % BANDS == k, four, four_ref[j])
                two = jnp.where(spot[back] // 4 % BANDS == k, two, two_ref[j])
            four_ref[j] = four
            two_ref[j] = two
    held = [zero, zero]
    for j in range(ND):
        back = BACK_LON[j]
        wide, narrow = (right_ref, left_ref) if back else (left_ref, right_ref)
        half = RANK[j] % 2
        wide[RANK[j]] = jnp.where(lane < TILES * GROUP, four_ref[j], 0.0)
        two = turn(two_ref[j], 2 * half - aside[back])
        if half:
            narrow[HALF + RANK[j] // 2] = jnp.where(lane % 4 < 2, held[back], two)
        else:
            held[back] = two
    for copy in small:
        copy.wait()
    east_ref, north_ref, land_ref, rows_ref = held_refs
    fields = [
        [f(r) for r in range(TILES)]
        for f in (
            lambda r: east_ref[tile_rows(r), :],
            lambda r: north_ref[tile_rows(r), :],
            lambda r: land_ref[tile_rows(r), :].astype(jnp.float32),
            lambda r: jnp.broadcast_to(rows_ref[0:1, :].astype(jnp.float32), (8, WIDTH)),
            lambda r: jnp.broadcast_to(rows_ref[1:2, :].astype(jnp.float32), (8, WIDTH)),
        )
    ]
    to_right, to_left = zero, zero
    for i in range(FIELDS):
        for r in range(TILES):
            place = GROUP * r + 4 * i
            here = lane // 2 == place // 2
            to_right = jnp.where(here, turn(fields[i][r], place - (WIDTH - 2)), to_right)
            to_left = jnp.where(here, turn(fields[i][r], place), to_left)
    right_ref[SENT - 1] = to_right
    left_ref[SENT - 1] = to_left
    odd = lax.axis_index("lon") % 2 == 1
    for i in range(SENT):
        right, left = right_ref[i], left_ref[i]
        to_even_ref[i] = jnp.where(odd, left, right)
        to_odd_ref[i] = jnp.where(odd, right, left)


def drive_of(j, east, north, open_water):
    along = float(COS[j] / WIND_REF) * east + float(SIN[j] / WIND_REF) * north
    drive = jnp.minimum(jnp.maximum(along, 0.0), WIND_CLIP)
    return drive * drive * open_water


def tree(values):
    values = list(values)
    while len(values) > 1:
        values = [sum(values[i + 1 : i + 2], values[i]) for i in range(0, len(values), 2)]
    return values[0]


def saturation_of(p):
    diff = [p[b] - p[b + HALF] for b in range(HALF)]
    both = [p[b] + p[b + HALF] for b in range(HALF)]
    folded = [both[b] + both[b + QUARTER] for b in range(QUARTER)]
    total = tree(folded)
    fold = [both[b] - both[b + QUARTER] for b in range(QUARTER)]
    total_c = tree([fold[0]] + [fold[b] * float(COS2[b]) for b in range(1, QUARTER)])
    total_s = tree([fold[b] * float(SIN2[b]) for b in range(1, QUARTER)])
    level = [None] * HALF
    for a in range(QUARTER):
        wave = total_c * float(COS2[a])
        if a:
            wave = wave + total_s * float(SIN2[a])
        level[a] = total + wave
        level[a + QUARTER] = total - wave

    def at(b):
        return diff[b % HALF], b // HALF % 2 == 1

    def minus(a, b):
        x, flip_x = at(a)
        y, flip_y = at(b)
        if flip_x:
            return y - x if flip_y else None, (x, y)
        return x + y if flip_y else x - y, None

    def plus_minus(value, a, b):
        gap, opposite = minus(a, b)
        if gap is None:
            return value - (opposite[0] + opposite[1])
        return value + gap

    waves = []
    for a in range(2):
        pairs = [minus(a + d, a - d + HALF)[0] for d in range(1, QUARTER)]
        weighted = [pairs[d - 1] * float(COS2[d]) for d in range(1, QUARTER)]
        waves.append(tree([diff[a]] + weighted))
        if a == 0:
            plain = tree([diff[0]] + pairs)
    twice = float(2.0 * COS2[1])
    odd, below = [None] * HALF, [None] * HALF
    odd[0] = plain + waves[0]
    window, before, now = plain, waves[0], waves[1]
    for a in range(1, QUARTER + 1):
        window = plus_minus(window, a + 8, a - 9)
        odd[a] = window + now
        if a < QUARTER:
            rest = plus_minus(before, a + 10, a + 8)
            before, now = now, twice * now - rest
    window, after, now = plain, waves[1], waves[0]
    for a in range(0, -(QUARTER - 1), -1):
        rest = plus_minus(after, a + 10, a + 8)
        after, now = now, twice * now - rest
        window = plus_minus(window, a - 9 + 2 * HALF, a + 8)
        below[a - 1 + HALF] = window + now
    out = [None] * ND
    for a in range(HALF):
        if odd[a] is not None:
            out[a], out[a + HALF] = level[a] + odd[a], level[a] - odd[a]
        else:
            out[a], out[a + HALF] = level[a] - below[a], level[a] + below[a]
    return out


def inside_masks():
    lane = lanes()
    one = jnp.ones((8, WIDTH), jnp.float32)
    return {
        (True, 1): jnp.where(lane >= 1, one, 0.0),
        (True, 2): jnp.where(lane >= 2, one, 0.0),
        (False, 1): jnp.where(lane < WIDTH - 1, one, 0.0),
        (False, 2): jnp.where(lane < WIDTH - 2, one, 0.0),
    }


def drift(j, base, tiles, scal_ref, inside):
    c1, c2, d1, d2 = (scal_ref[base + 6 * j + i] for i in range(4))
    side = 1 if BACK_LON[j] else -1
    c1 = c1 * inside[BACK_LON[j], 1]
    c2 = c2 * inside[BACK_LON[j], 2]
    x = [q + c1 * turn(q, side) + c2 * turn(q, 2 * side) for q in tiles]
    row = sublanes()
    one, two = (1, 2) if BACK_LAT[j] else (7, 6)
    at_edge = (row < 1, row < 2) if BACK_LAT[j] else (row >= 7, row >= 6)
    order = range(TILES) if BACK_LAT[j] else range(TILES - 1, -1, -1)
    moved = [[pltpu.roll(tile, by, 0) for tile in x] for by in (one, two)]
    y = [None] * TILES
    before = None
    for r in order:
        first = x[r] if before is None else moved[0][before]
        near = jnp.where(at_edge[0], first, moved[0][r])
        second = near if before is None else moved[1][before]
        far = jnp.where(at_edge[1], second, moved[1][r])
        y[r] = x[r] + d1 * near + d2 * far
        before = r
    return y


def drift_kernel(scal_ref, q_ref, east_ref, north_ref, land_ref, out_ref, drive_ref):
    bands = q_ref.shape[0]
    for r in range(TILES):
        rows = tile_rows(r)
        water = jnp.where(land_ref[rows, :] == 2, 0.0, 1.0)
        east, north = east_ref[rows, :], north_ref[rows, :]
        for j in range(ND):
            drive_ref[j, r] = drive_of(j, east, north, water)
    inside = inside_masks()

    def band(k, carry):
        base = (lax.axis_index("freq") * bands + k) * STRIDE
        for j in range(ND):
            factor = scal_ref[base + 6 * j + 4]
            tiles = [q_ref[k, j, tile_rows(r), :] * factor for r in range(TILES)]
            for r, tile in enumerate(drift(j, base, tiles, scal_ref, inside)):
                out_ref[k, j, r] = tile
        return carry

    lax.fori_loop(0, bands, band, 0)


def packed_lat(j, x, d0, d1, d2):
    lane, row = lanes(), sublanes()

    def shifted(x):
        if BACK_LAT[j]:
            moved = pltpu.roll(x, 1, 0)
            over = jnp.where(lane < GROUP, x, turn(moved, GROUP))
            return jnp.where(row >= 1, moved, over)
        moved = pltpu.roll(x, 7, 0)
        over = jnp.where(lane >= (TILES - 1) * GROUP, x, turn(moved, -GROUP))
        return jnp.where(row <= 6, moved, over)

    near = shifted(x)
    return d0 * x + d1 * near + d2 * shifted(near)


def spread(tile, position):
    at_first = lanes() // 4 % BANDS == 0
    tile = jnp.where(at_first, turn(tile, -4 * position), 0.0)
    for step in (1, 2, 4):
        tile = tile + turn(tile, 4 * step)
    return tile


def packed_coefficients(inverse, speed):
    c = inverse * abs(float(speed))
    return 1.0 + c * (0.5 * c - 1.5), c * (2.0 - c), c * (0.5 * c - 0.5)


AHEAD = [j for j in range(ND) if not BACK_LON[j]]
BACK = [j for j in range(ND) if BACK_LON[j]]


def packed_fix(table, columns_ref, fix_ref):
    slot = lanes() % 4
    inverse = table(5)

    def one(j):
        back = BACK_LON[j]
        _, c1, c2 = packed_coefficients(inverse, COURANT_MAX * COS[j])
        tile = columns_ref[j]
        next_one = jnp.where(slot == (0 if back else 3), turn(tile, -1 if back else 1), 0.0)
        first = c2 * tile + c1 * next_one
        lat = packed_coefficients(inverse, 0.5 * COURANT_MAX * SIN[j])
        return packed_lat(j, first, *lat)

    for i in range(HALF):
        fix_ref[i] = jnp.where(slot < 2, one(BACK[i]), turn(one(AHEAD[i]), -4))


def packed_start(mine_right_ref, mine_left_ref, left_ref, right_ref, columns_ref, side_refs):
    near_ref, far_ref = side_refs
    lane = lanes()
    slot = lane % 4
    used = lane < TILES * GROUP
    for j in range(ND):
        half = RANK[j] % 2
        narrow = HALF + RANK[j] // 2
        if BACK_LON[j]:
            wide, own = left_ref[RANK[j]], mine_right_ref[RANK[j]]
            other = turn(right_ref[narrow], 2 - 2 * half)
            centre = jnp.where(slot < 2, turn(wide, -2), other)
            near = turn(jnp.where(slot == 3, own, wide), -1)
            near = jnp.where(slot == 3, turn(centre, 1), near)
            far = jnp.where(slot < 2, wide, own)
        else:
            wide, own = right_ref[RANK[j]], mine_left_ref[RANK[j]]
            other = turn(left_ref[narrow], -2 * half)
            centre = jnp.where(slot < 2, other, turn(wide, 2))
            near = turn(jnp.where(slot == 0, own, wide), 1)
            near = jnp.where(slot == 0, turn(centre, -1), near)
            far = jnp.where(slot < 2, own, wide)
        columns_ref[j] = jnp.where(used, centre, 0.0)
        near_ref[j] = jnp.where(used, near, 0.0)
        far_ref[j] = jnp.where(used, far, 0.0)


def packed_source(
    table, left_ref, right_ref, columns_ref, side_refs, sums_ref, part_ref, drive_ref, ice_ref
):
    near_ref, far_ref = side_refs
    lane = lanes()
    slot, place = lane % 4, lane // 4 % BANDS
    both = jnp.where(slot < 2, left_ref[SENT - 1], turn(right_ref[SENT - 1], 2))
    east, north, land, south_rows, north_rows = (spread(both, i) for i in range(FIELDS))
    row = (sublanes() + lane // GROUP * 8).astype(jnp.float32)
    held = (row < south_rows) | (row >= LAT - north_rows)
    sea = jnp.where(land > 0.5, 1.0, 0.0)
    ice = jnp.where(land > 1.5, 1.0, 0.0)
    ice_ref[...] = ice
    inverse = table(5)
    p, stress = [], []
    for j in range(ND):
        lon = packed_coefficients(inverse, COURANT_MAX * COS[j])
        lat = packed_coefficients(inverse, 0.5 * COURANT_MAX * SIN[j])
        centre = columns_ref[j]
        x = lon[0] * centre + lon[1] * near_ref[j] + lon[2] * far_ref[j]
        x = packed_lat(j, x, *lat)
        p.append(jnp.where(held, centre, jnp.maximum(x, 0.0)) * sea)
        drive = drive_of(j, east, north, 1.0 - ice)
        drive_ref[j] = drive
        stress.append(p[j] * drive)
    slope, stress = tree(p), tree(stress)

    def running(tile):
        for step in (1, 2, 4):
            tile = tile + jnp.where(place >= step, turn(tile, 4 * step), 0.0)
        return tile

    out = [jnp.zeros((8, WIDTH), jnp.float32) for _ in range(PACKED_SUMS)]

    def put(index, tile):
        position = index % BANDS
        moved = turn(tile, 4 * (position - (BANDS - 1)))
        out[index // BANDS] = jnp.where(place == position, moved, out[index // BANDS])

    for j, excess in enumerate(excess_of(p)):
        total = running(excess)
        put(j, total)
        rate = excess * table(0) + (total - excess) * table(1)
        part_ref[j] = p[j] * jnp.exp(rate)
    put(ND, running(slope * table(2)))
    put(ND + 1, running(stress * table(3)))
    for i in range(PACKED_SUMS):
        sums_ref[PACKED_AT + i] = out[i]


def excess_of(p):
    out = []
    for saturation in saturation_of(p):
        capped = jnp.maximum(saturation, CAP)
        excess = capped * lax.rsqrt(capped) - ROOT_CAP
        out.append(excess * excess)
    return out


def held_and_sea(r, land_ref, rows_ref):
    row = sublanes() + 8 * r
    held = (row < rows_ref[0:1, :]) | (row >= LAT - rows_ref[1:2, :])
    return held, jnp.where(land_ref[tile_rows(r), :] != 0, 1.0, 0.0)


def source_kernel(first, *refs):
    table_ref, x_ref, spec_ref, land_ref, rows_ref = refs[:5]
    refs = refs[5:]
    freq = lax.axis_index("freq")
    bands = x_ref.shape[0]

    def table(i):
        return table_ref[freq, i]

    if first:
        mine_right_ref, mine_left_ref, even_ref, odd_ref = refs[:4]
        p_ref, excess_ref, sums_ref, part_ref, packed_drive_ref, ice_ref = refs[4:10]
        fix_ref, left_ref, right_ref, columns_ref, near_ref, far_ref = refs[10:]
        odd = lax.axis_index("lon") % 2 == 1
        for i in range(SENT):
            even, other = even_ref[i], odd_ref[i]
            left_ref[i] = jnp.where(odd, even, other)
            right_ref[i] = jnp.where(odd, other, even)
        sides = (near_ref, far_ref)
        packed_start(mine_right_ref, mine_left_ref, left_ref, right_ref, columns_ref, sides)
        packed_source(
            table, left_ref, right_ref, columns_ref, sides,
            sums_ref, part_ref, packed_drive_ref, ice_ref,
        )
    else:
        columns_ref, p_ref, excess_ref, sums_ref, fix_ref = refs
    packed_fix(table, columns_ref, fix_ref)
    for i in range(PACKED_AT):
        sums_ref[i] = jnp.zeros((8, WIDTH), jnp.float32)

    lane = lanes()
    at_edge = {True: lane < 2, False: lane >= WIDTH - 2}

    def band(k, carry):
        for r in range(TILES):
            rows = tile_rows(r)
            held, sea = held_and_sea(r, land_ref, rows_ref)
            if not first:
                free = jnp.where(held, 0.0, sea)
            shift = jnp.bitwise_and(WIDTH - GROUP * r - 4 * k, WIDTH - 1)
            p = [None] * ND
            for i in range(HALF):
                moved = pltpu.roll(fix_ref[i], shift, 1)
                for j in (BACK[i], AHEAD[i]):
                    x = x_ref[k, j, r] + jnp.where(at_edge[BACK_LON[j]], moved, 0.0)
                    if first:
                        x = jnp.where(held, spec_ref[k, j, rows, :], jnp.maximum(x, 0.0)) * sea
                    else:
                        x = jnp.maximum(x * free, spec_ref[k, j, r])
                    p_ref[k, j, r] = x
                    p[j] = x
            for j, excess in enumerate(excess_of(p)):
                excess_ref[k, j, r] = excess
                sums_ref[TILES * j + r] += excess
        return carry

    lax.fori_loop(0, bands, band, 0)


def weights_kernel(scal_ref, p_ref, drive_ref, out_ref):
    bands = p_ref.shape[0]
    for i in range(2 * TILES):
        out_ref[i] = jnp.zeros((8, WIDTH), jnp.float32)

    def band(k, carry):
        extra = (lax.axis_index("freq") * bands + k) * STRIDE + 6 * ND
        for r in range(TILES):
            p = [p_ref[k, j, r] for j in range(ND)]
            out_ref[r] += tree(p) * scal_ref[extra + 2]
            out_ref[TILES + r] += tree([p[j] * drive_ref[j, r] for j in range(ND)]) * scal_ref[extra + 3]
        return carry

    lax.fori_loop(0, bands, band, 0)


def add_kernel(one_ref, other_ref, out_ref):
    for i in range(out_ref.shape[0]):
        out_ref[i] = one_ref[i] + other_ref[i]


def local_kernel(last, scal_ref, p_ref, excess_ref, *refs):
    if last:
        (out_ref,) = refs
    else:
        spec_ref, land_ref, rows_ref, out_ref, held_ref = refs
    bands = p_ref.shape[0]
    first = (lax.axis_index("freq") * bands) * STRIDE
    extra = first + 6 * ND
    some = 6

    def directions(group, carry):
        for r in range(TILES):
            if not last:
                held, sea = held_and_sea(r, land_ref, rows_ref)
                kept = jnp.where(held, sea, 0.0)
            for i in range(some):
                j = group * some + i
                lower = jnp.zeros((8, WIDTH), jnp.float32)
                for k in range(bands):
                    excess = excess_ref[k, j, r]
                    at = extra + k * STRIDE
                    rate = excess * scal_ref[at] + lower * scal_ref[at + 1]
                    value = p_ref[k, j, r] * jnp.exp(rate)
                    if not last:
                        value = value * scal_ref[first + k * STRIDE + 6 * j + 4]
                        held_ref[k, j, r] = spec_ref[k, j, tile_rows(r), :] * kept
                    out_ref[k, j, r] = value
                    lower = lower + excess
        return carry

    lax.fori_loop(0, ND // some, directions, 0)


def pair_kernel(sums_ref, other_ref, out_ref):
    first = (lax.axis_index("freq") % 2) * HALF_TILES
    for i in range(HALF_TILES):
        out_ref[i] = sums_ref[first + i] + other_ref[first + i]
    for i in range(out_ref.shape[0] - HALF_TILES):
        out_ref[HALF_TILES + i] = sums_ref[PACKED_AT + i] + other_ref[PACKED_AT + i]


def damp_and_gain(slope, stress, ice):
    damp = SWELL_DAMP * (slope / (slope + 1.0)) + ICE_DAMP * ice
    return damp, GROWTH * (1.0 + stress / (stress + 1.0))


def grow_half(half, last, near, refs):
    scal_ref, part_ref, other_ref, lower_ref, pair_ref, rest_ref, drive_ref, land_ref = refs[:8]
    out_ref, rate_ref, near_ref, field_ref, written_ref, sent = refs[8:]
    bands = part_ref.shape[0]
    freq = lax.axis_index("freq")
    odd = jnp.where(freq % 2 == 1, 1.0, 0.0)
    upper = jnp.where(freq >= 2, 1.0, 0.0)
    for r in range(TILES):
        rows = tile_rows(r)
        ice = jnp.where(land_ref[rows, :] == 2, 1.0, 0.0)
        slope, stress = (pair_ref[at + r] + rest_ref[at + r] for at in (0, TILES))
        damp, gain = damp_and_gain(slope, stress, ice)
        for i in range(HALF):
            j = half * HALF + i
            lower = odd * other_ref[TILES * j + r] + upper * lower_ref[TILES * i + r]
            rate_ref[i, r] = gain * drive_ref[j, r] - damp - LOWER * lower

    inside = None if last else inside_masks()
    target_ref = out_ref if near else field_ref

    def send(k, mine):
        source, which = (target_ref, half) if mine else (near_ref, 1 - half)
        place = written_ref.at[k, pl.ds(which * HALF, HALF)]
        return pltpu.make_async_copy(source.at[k], place, sent.at[int(mine), k])

    def band(k, carry):
        base = (freq * bands + k) * STRIDE
        root = scal_ref[base + 6 * ND + 4]
        for i in range(HALF):
            j = half * HALF + i
            tiles = [part_ref[k, j, r] * jnp.exp(rate_ref[i, r] * root) for r in range(TILES)]
            if last:
                for r in range(TILES):
                    target_ref[k, i, tile_rows(r), :] = tiles[r]
            else:
                for r, tile in enumerate(drift(j, base, tiles, scal_ref, inside)):
                    out_ref[k, j, r] = tile
        return carry

    def sent_band(k, carry):
        band(k, carry)
        send(k, True).start()
        return carry

    early = EARLY if near else bands
    if not last:
        lax.fori_loop(0, bands, band, 0)
        return
    if not near:
        for k in range(EARLY, bands):
            send(k, False).start()
    lax.fori_loop(0, early, sent_band, 0)
    lax.fori_loop(early, bands, band, 0)
    for k in range(early):
        send(k, True).wait()
    if not near:
        for k in range(EARLY, bands):
            send(k, False).wait()


EARLY = 4


def growth_kernel(last, near, *refs):
    operands, refs = refs[:8], refs[8:]
    other_ref, mine_ref, pair_ref, rest_ref = operands[2:6]
    freq = lax.axis_index("freq")
    if near and last:
        half_ref, slope_out_ref, written_ref, rate_ref, slope_ref, slope_sent, sent = refs
        results = (half_ref, rate_ref, None, None, written_ref, sent)
        for r in range(TILES):
            slope_ref[tile_rows(r), :] = pair_ref[r] + rest_ref[r]
        slope_copy = pltpu.make_async_copy(slope_ref, slope_out_ref, slope_sent)
        slope_copy.start()
    elif near:
        table_ref, sums_ref, packed_part_ref, packed_drive_ref, ice_ref = refs[:5]
        out_ref, columns_ref, rate_ref = refs[5:]
        results = (out_ref, rate_ref, None, None, None, None)
        odd = jnp.where(freq % 2 == 1, 1.0, 0.0)
        upper = jnp.where(freq >= 2, 1.0, 0.0)
        total, lower = [], []
        for i in range(PACKED_SUMS):
            here, there = PACKED_AT + i, HALF_TILES + i
            total.append((sums_ref[here] + other_ref[here]) + mine_ref[there])
            lower.append(odd * other_ref[here] + upper * mine_ref[there])
        slope, stress = (spread(total[i // BANDS], i % BANDS) for i in (ND, ND + 1))
        damp, gain = damp_and_gain(slope, stress, ice_ref[...])
        root = table_ref[freq, 4]
        for j in range(ND):
            under = spread(lower[j // BANDS], j % BANDS)
            rate = gain * packed_drive_ref[j] - damp - LOWER * under
            columns_ref[j] = packed_part_ref[j] * jnp.exp(root * rate)
    elif last:
        half_ref, _, out_ref, rate_ref, field_ref, sent = refs
        results = (out_ref, rate_ref, half_ref, field_ref, out_ref, sent)
    else:
        _, out_ref, rate_ref = refs
        results = (out_ref, rate_ref, None, None, None, None)
    for half in range(2):

        @pl.when(freq % 2 == (half if near else 1 - half))
        def _():
            grow_half(half, last, near, operands + results)

    if near and last:
        slope_copy.wait()


def cost(tiles, ops, moves):
    return pl.CostEstimate(
        flops=tiles * ops * 8 * WIDTH, bytes_accessed=tiles * moves * 32 * WIDTH, transcendentals=0
    )


def per_device(spectrum, east_wind, north_wind, land_sea, edge_rows):
    bands, count, lat_rows, width = spectrum.shape
    assert (bands, count, lat_rows, width) == (BANDS, ND, LAT, WIDTH)
    ring = lax.axis_size("lon")
    assert lax.axis_size("freq") == 4 and bands * 4 == NF and ring % 2 == 0
    f32 = jnp.float32

    def tiles(count):
        return jax.ShapeDtypeStruct((count, 8, WIDTH), f32)

    field = jax.ShapeDtypeStruct(spectrum.shape, f32)
    spread_field = jax.ShapeDtypeStruct((bands, ND, TILES, 8, WIDTH), f32)
    plane = jax.ShapeDtypeStruct((LAT, WIDTH), f32)
    tile = jax.ShapeDtypeStruct((8, WIDTH), f32)
    smem = pl.BlockSpec(memory_space=pltpu.SMEM)
    vmem = pl.BlockSpec(memory_space=pltpu.VMEM)
    hbm = pl.BlockSpec(memory_space=pltpu.HBM)
    params = pltpu.CompilerParams(vmem_limit_bytes=16 * 1024 * 1024)
    scalars, table = jnp.asarray(SCALARS), jnp.asarray(PACKED_TABLE)
    swap_core = [(0, 1), (1, 0), (2, 3), (3, 2)]
    swap_chip = [(0, 2), (2, 0), (1, 3), (3, 1)]
    swap_even = [(i, i ^ 1) for i in range(ring)]
    swap_odd = [(i, (i + (1 if i % 2 else -1)) % ring) for i in range(ring)]
    whole = bands * ND * TILES
    packed = pltpu.VMEM((ND, 8, WIDTH), f32)
    received = pltpu.VMEM((SENT, 8, WIDTH), f32)

    arguments = [spectrum, east_wind, north_wind, land_sea, edge_rows]
    spectrum, right, left, east_wind, north_wind, land_sea, edge_rows, even, odd = pl.pallas_call(
        pack_kernel,
        in_specs=[hbm] * 5,
        out_specs=[vmem] * 9,
        out_shape=[field, tiles(SENT), tiles(SENT)]
        + [jax.ShapeDtypeStruct(x.shape, x.dtype) for x in arguments[1:]]
        + [tiles(SENT), tiles(SENT)],
        scratch_shapes=[pltpu.SemaphoreType.DMA((bands + 4,)), packed, packed],
        compiler_params=params,
        cost_estimate=cost(whole, 6, 2),
        name="pack_columns",
    )(*(pltpu.with_memory_space_constraint(x, pltpu.HBM) for x in arguments))
    even = lax.ppermute(even, "lon", swap_even)
    odd = lax.ppermute(odd, "lon", swap_odd)
    drifted, drive = pl.pallas_call(
        drift_kernel,
        in_specs=[smem] + [vmem] * 4,
        out_specs=[vmem] * 2,
        out_shape=[spread_field, jax.ShapeDtypeStruct((ND, TILES, 8, WIDTH), f32)],
        compiler_params=params,
        cost_estimate=cost(whole, 12, 2),
        name="drift",
    )(scalars, spectrum, east_wind, north_wind, land_sea)

    for step in range(STEPS):
        first, last = step == 0, step == STEPS - 1
        sums = PACKED_AT + (PACKED_SUMS if first else 0)
        half_sums = sums - PACKED_AT + HALF_TILES
        operands = [table, drifted, spectrum if first else kept, land_sea, edge_rows]
        operands += [right, left, even, odd] if first else [columns]
        p, excess, mine, *packed_state = pl.pallas_call(
            functools.partial(source_kernel, first),
            in_specs=[vmem] * len(operands),
            out_specs=[vmem] * (6 if first else 3),
            out_shape=[spread_field, spread_field, tiles(sums)]
            + ([tiles(ND), tiles(ND), tile] if first else []),
            scratch_shapes=[packed]
            + ([received] * 2 + [packed] * 3 if first else []),
            compiler_params=params,
            cost_estimate=cost(whole, 30, 3),
            name="sources",
        )(*operands)
        other = lax.ppermute(mine, "freq", swap_core)
        pair = pl.pallas_call(
            pair_kernel,
            in_specs=[vmem] * 2,
            out_specs=vmem,
            out_shape=tiles(half_sums),
            compiler_params=params,
            cost_estimate=cost(half_sums, 1, 3),
            name="pair_sums",
        )(mine, other)
        near = lax.ppermute(pair, "freq", swap_chip)
        p, _ = lax.optimization_barrier((p, pair))
        weights = pl.pallas_call(
            weights_kernel,
            in_specs=[smem] + [vmem] * 2,
            out_specs=vmem,
            out_shape=tiles(2 * TILES),
            compiler_params=params,
            cost_estimate=cost(whole, 3, 1),
            name="slope_and_stress",
        )(scalars, p, drive)
        p, excess, weights = lax.optimization_barrier((p, excess, weights))
        weights_other = lax.ppermute(weights, "freq", swap_core)
        operands = [scalars, p, excess] + ([] if last else [spectrum, land_sea, edge_rows])
        part, *kept = pl.pallas_call(
            functools.partial(local_kernel, last),
            in_specs=[smem] + [vmem] * (len(operands) - 1),
            out_specs=[vmem] * (1 if last else 2),
            out_shape=[spread_field] * (1 if last else 2),
            compiler_params=params,
            cost_estimate=cost(whole, 8, 3),
            name="local_rate",
        )(*operands)
        kept = None if last else kept[0]
        weights_other, part = lax.optimization_barrier((weights_other, part))
        weights_pair = pl.pallas_call(
            add_kernel,
            in_specs=[vmem] * 2,
            out_specs=vmem,
            out_shape=tiles(2 * TILES),
            compiler_params=params,
            cost_estimate=cost(2 * TILES, 1, 3),
            name="pair_slope_and_stress",
        )(weights, weights_other)
        weights_rest = lax.ppermute(weights_pair, "freq", swap_chip)
        near, weights_rest = lax.optimization_barrier((near, weights_rest))
        far = lax.ppermute(near, "freq", swap_core)

        common = [weights_pair, weights_rest, drive, land_sea]
        half_rate = pltpu.VMEM((HALF, TILES, 8, WIDTH), f32)
        half_field = (bands, HALF, LAT, WIDTH)
        sent = pltpu.SemaphoreType.DMA((2, bands))

        def grow(is_near, lower, extra, specs, results, shapes, scratch, alias):
            operands = [scalars, part, other, lower, *common, *extra]
            return pl.pallas_call(
                functools.partial(growth_kernel, last, is_near),
                in_specs=[smem] + [vmem] * (len(operands) - 1 - len(specs)) + specs,
                out_specs=results,
                out_shape=shapes,
                input_output_aliases={len(operands) - 1: 0} if alias else {},
                scratch_shapes=[half_rate] + scratch,
                compiler_params=params,
                cost_estimate=cost(whole, 6 if last else 12, 1),
                name="grow_near" if is_near else "grow_far",
            )(*operands)

        if last:
            shapes = [jax.ShapeDtypeStruct(half_field, f32), plane, field]
            scratch = [pltpu.VMEM(plane.shape, f32), pltpu.SemaphoreType.DMA(()), sent]
            made, columns, written = grow(True, near, [], [], [vmem, hbm, hbm], shapes, scratch, False)
            scratch = [pltpu.VMEM(half_field, f32), sent]
            (drifted,) = grow(False, far, [made, written], [hbm], [hbm], [field], scratch, True)
        else:
            shapes = [spread_field, tiles(ND)]
            extra = [table, mine, *packed_state]
            made, columns = grow(True, near, extra, [], [vmem] * 2, shapes, [], False)
            (drifted,) = grow(False, far, [made], [], [vmem], [spread_field], [], True)
    return drifted, columns


def solution(mesh):
    in_specs = (
        P("freq", None, None, "lon"),
        P(None, "lon"),
        P(None, "lon"),
        P(None, "lon"),
        P(None, "lon"),
    )
    out_specs = (P("freq", None, None, "lon"), P(None, "lon"))
    return jax.shard_map(
        per_device, mesh=mesh, in_specs=in_specs, out_specs=out_specs, check_vma=False
    )
```

```python
import functools
import math

import jax
import jax.numpy as jnp
import numpy as np
from jax import lax
from jax.experimental import pallas as pl
from jax.experimental.pallas import tpu as pltpu
from jax.sharding import PartitionSpec as P

NF = 32
STEPS = 2

COURANT_MAX = 0.9
FREQ_RATIO = 1.1
WIND_REF = 8.0
WIND_CLIP = 2.0
GROWTH = 0.01
BREAKING = 0.3
SATURATION_REF = 0.4
CUMULATIVE = 2.0
SWELL_DAMP = 0.1
ICE_DAMP = 0.5

ND = 36
HALF = ND // 2
QUARTER = ND // 4
DTHETA = 2.0 * math.pi / ND
LOG2E = 1.0 / math.log(2.0)
ROOT_REF = math.sqrt(SATURATION_REF)
TILES = 3
LAT = 8 * TILES
WIDTH = 128
STRIDE = 6 * ND + 8

ANGLES = np.arange(ND) * DTHETA
COS = np.cos(ANGLES)
SIN = np.sin(ANGLES)
COS2 = np.cos(2.0 * ANGLES)
SIN2 = np.sin(2.0 * ANGLES)
BACK_LON = [bool(c >= 0.0) for c in COS]
BACK_LAT = [bool(s >= 0.0) for s in SIN]
RANK = [sum(BACK_LON[:j]) if BACK_LON[j] else j - sum(BACK_LON[:j]) for j in range(ND)]


def one_sided(courant):
    c = np.abs(courant)
    return 1.0 - 1.5 * c + 0.5 * c * c, 2.0 * c - c * c, 0.5 * c * c - 0.5 * c


GROUP = 32
BANDS = 8
SENT = HALF + QUARTER + 1
FIELDS = 5
PACKED_AT = ND * TILES
PACKED_SUMS = 5
HALF_TILES = HALF * TILES
SCALE = 0.25 * DTHETA
CAP = SATURATION_REF / SCALE
ROOT_CAP = math.sqrt(CAP)
LOWER = CUMULATIVE / NF * SCALE


def make_tables():
    ratios = FREQ_RATIO ** np.arange(NF)
    root = np.sqrt(ratios)
    lon = one_sided(COURANT_MAX * COS[None, :] / ratios[:, None])
    lat = one_sided(0.5 * COURANT_MAX * SIN[None, :] / ratios[:, None])
    scalars = np.zeros((NF, STRIDE))
    for i, value in enumerate(
        (lon[1] / lon[0], lon[2] / lon[0], lat[1] / lat[0], lat[2] / lat[0], lon[0] * lat[0])
    ):
        scalars[:, i : 6 * ND : 6] = value
    rest = [
        -BREAKING / SATURATION_REF * SCALE * root,
        -LOWER * root,
        ratios * ratios * DTHETA / np.sum(ratios * ratios),
        ratios * root * DTHETA / np.sum(ratios * root),
        root,
        1.0 / ratios,
    ]
    packed = np.zeros((NF // BANDS, len(rest), 8, WIDTH))
    for i, value in enumerate(rest):
        scalars[:, 6 * ND + i] = value
        for lane in range(TILES * GROUP):
            packed[:, i, :, lane] = value[lane // 4 % BANDS :: BANDS, None]
    return scalars.reshape(-1).astype(np.float32), packed.astype(np.float32)


SCALARS, PACKED_TABLE = make_tables()


def lanes():
    return lax.broadcasted_iota(jnp.int32, (8, WIDTH), 1)


def sublanes():
    return lax.broadcasted_iota(jnp.int32, (8, WIDTH), 0)


def turn(tile, shift):
    shift = shift % WIDTH
    return tile if shift == 0 else pltpu.roll(tile, shift, 1)


def tile_rows(r):
    return slice(8 * r, 8 * r + 8)


def pack_kernel(spec_ref, *refs):
    sources, (copy_ref, right_ref, left_ref), held_refs = refs[:4], refs[4:7], refs[7:11]
    to_even_ref, to_odd_ref, arrived, four_ref, two_ref = refs[11:]

    def fetch(k):
        return pltpu.make_async_copy(spec_ref.at[k], copy_ref.at[k], arrived.at[k])

    small = [
        pltpu.make_async_copy(source, target, arrived.at[BANDS + i])
        for i, (source, target) in enumerate(zip(sources, held_refs))
    ]
    for k in range(BANDS):
        fetch(k).start()
    for copy in small:
        copy.start()
    lane = lanes()
    zero = jnp.zeros((8, WIDTH), jnp.float32)

    def by_tile(spot, tiles):
        return jnp.where(spot < GROUP, tiles[0], jnp.where(spot < 2 * GROUP, tiles[1], tiles[2]))

    first = {True: WIDTH - 4, False: 0}
    aside = {True: 4, False: -2}
    spot = {back: (lane - aside[back]) % WIDTH for back in aside}
    for k in range(BANDS):
        fetch(k).wait()
        for j in range(ND):
            back = BACK_LON[j]
            tiles = [
                turn(copy_ref[k, j, tile_rows(r), :], GROUP * r + 4 * k - first[back])
                for r in range(TILES)
            ]
            four, two = by_tile(lane, tiles), by_tile(spot[back], tiles)
            if k:
                four = jnp.where(lane // 4 % BANDS == k, four, four_ref[j])
                two = jnp.where(spot[back] // 4 % BANDS == k, two, two_ref[j])
            four_ref[j] = four
            two_ref[j] = two
    held = [zero, zero]
    for j in range(ND):
        back = BACK_LON[j]
        wide, narrow = (right_ref, left_ref) if back else (left_ref, right_ref)
        half = RANK[j] % 2
        wide[RANK[j]] = jnp.where(lane < TILES * GROUP, four_ref[j], 0.0)
        two = turn(two_ref[j], 2 * half - aside[back])
        if half:
            narrow[HALF + RANK[j] // 2] = jnp.where(lane % 4 < 2, held[back], two)
        else:
            held[back] = two
    for copy in small:
        copy.wait()
    east_ref, north_ref, land_ref, rows_ref = held_refs
    fields = [
        [f(r) for r in range(TILES)]
        for f in (
            lambda r: east_ref[tile_rows(r), :],
            lambda r: north_ref[tile_rows(r), :],
            lambda r: land_ref[tile_rows(r), :].astype(jnp.float32),
            lambda r: jnp.broadcast_to(rows_ref[0:1, :].astype(jnp.float32), (8, WIDTH)),
            lambda r: jnp.broadcast_to(rows_ref[1:2, :].astype(jnp.float32), (8, WIDTH)),
        )
    ]
    to_right, to_left = zero, zero
    for i in range(FIELDS):
        for r in range(TILES):
            place = GROUP * r + 4 * i
            here = lane // 2 == place // 2
            to_right = jnp.where(here, turn(fields[i][r], place - (WIDTH - 2)), to_right)
            to_left = jnp.where(here, turn(fields[i][r], place), to_left)
    right_ref[SENT - 1] = to_right
    left_ref[SENT - 1] = to_left
    odd = lax.axis_index("lon") % 2 == 1
    for i in range(SENT):
        right, left = right_ref[i], left_ref[i]
        to_even_ref[i] = jnp.where(odd, left, right)
        to_odd_ref[i] = jnp.where(odd, right, left)


def drive_of(j, east, north, open_water):
    along = float(COS[j] / WIND_REF) * east + float(SIN[j] / WIND_REF) * north
    drive = jnp.minimum(jnp.maximum(along, 0.0), WIND_CLIP)
    return drive * drive * open_water


def tree(values):
    values = list(values)
    while len(values) > 1:
        values = [sum(values[i + 1 : i + 2], values[i]) for i in range(0, len(values), 2)]
    return values[0]


def saturation_of(p):
    diff = [p[b] - p[b + HALF] for b in range(HALF)]
    both = [p[b] + p[b + HALF] for b in range(HALF)]
    folded = [both[b] + both[b + QUARTER] for b in range(QUARTER)]
    total = tree(folded)
    fold = [both[b] - both[b + QUARTER] for b in range(QUARTER)]
    total_c = tree([fold[0]] + [fold[b] * float(COS2[b]) for b in range(1, QUARTER)])
    total_s = tree([fold[b] * float(SIN2[b]) for b in range(1, QUARTER)])
    level = [None] * HALF
    for a in range(QUARTER):
        wave = total_c * float(COS2[a])
        if a:
            wave = wave + total_s * float(SIN2[a])
        level[a] = total + wave
        level[a + QUARTER] = total - wave

    def at(b):
        return diff[b % HALF], b // HALF % 2 == 1

    def minus(a, b):
        x, flip_x = at(a)
        y, flip_y = at(b)
        if flip_x:
            return y - x if flip_y else None, (x, y)
        return x + y if flip_y else x - y, None

    def plus_minus(value, a, b):
        gap, opposite = minus(a, b)
        if gap is None:
            return value - (opposite[0] + opposite[1])
        return value + gap

    waves = []
    for a in range(2):
        pairs = [minus(a + d, a - d + HALF)[0] for d in range(1, QUARTER)]
        weighted = [pairs[d - 1] * float(COS2[d]) for d in range(1, QUARTER)]
        waves.append(tree([diff[a]] + weighted))
        if a == 0:
            plain = tree([diff[0]] + pairs)
    twice = float(2.0 * COS2[1])
    odd, below = [None] * HALF, [None] * HALF
    odd[0] = plain + waves[0]
    window, before, now = plain, waves[0], waves[1]
    for a in range(1, QUARTER + 1):
        window = plus_minus(window, a + 8, a - 9)
        odd[a] = window + now
        if a < QUARTER:
            rest = plus_minus(before, a + 10, a + 8)
            before, now = now, twice * now - rest
    window, after, now = plain, waves[1], waves[0]
    for a in range(0, -(QUARTER - 1), -1):
        rest = plus_minus(after, a + 10, a + 8)
        after, now = now, twice * now - rest
        window = plus_minus(window, a - 9 + 2 * HALF, a + 8)
        below[a - 1 + HALF] = window + now
    out = [None] * ND
    for a in range(HALF):
        if odd[a] is not None:
            out[a], out[a + HALF] = level[a] + odd[a], level[a] - odd[a]
        else:
            out[a], out[a + HALF] = level[a] - below[a], level[a] + below[a]
    return out


def inside_masks():
    lane = lanes()
    one = jnp.ones((8, WIDTH), jnp.float32)
    return {
        (True, 1): jnp.where(lane >= 1, one, 0.0),
        (True, 2): jnp.where(lane >= 2, one, 0.0),
        (False, 1): jnp.where(lane < WIDTH - 1, one, 0.0),
        (False, 2): jnp.where(lane < WIDTH - 2, one, 0.0),
    }


def drift(j, base, tiles, scal_ref, inside):
    c1, c2, d1, d2 = (scal_ref[base + 6 * j + i] for i in range(4))
    side = 1 if BACK_LON[j] else -1
    c1 = c1 * inside[BACK_LON[j], 1]
    c2 = c2 * inside[BACK_LON[j], 2]
    x = [q + c1 * turn(q, side) + c2 * turn(q, 2 * side) for q in tiles]
    row = sublanes()
    one, two = (1, 2) if BACK_LAT[j] else (7, 6)
    at_edge = (row < 1, row < 2) if BACK_LAT[j] else (row >= 7, row >= 6)
    order = range(TILES) if BACK_LAT[j] else range(TILES - 1, -1, -1)
    moved = [[pltpu.roll(tile, by, 0) for tile in x] for by in (one, two)]
    y = [None] * TILES
    before = None
    for r in order:
        first = x[r] if before is None else moved[0][before]
        near = jnp.where(at_edge[0], first, moved[0][r])
        second = near if before is None else moved[1][before]
        far = jnp.where(at_edge[1], second, moved[1][r])
        y[r] = x[r] + d1 * near + d2 * far
        before = r
    return y


def drift_kernel(scal_ref, q_ref, east_ref, north_ref, land_ref, out_ref, drive_ref):
    bands = q_ref.shape[0]
    for r in range(TILES):
        rows = tile_rows(r)
        water = jnp.where(land_ref[rows, :] == 2, 0.0, 1.0)
        east, north = east_ref[rows, :], north_ref[rows, :]
        for j in range(ND):
            drive_ref[j, r] = drive_of(j, east, north, water)
    inside = inside_masks()

    def band(k, carry):
        base = (lax.axis_index("freq") * bands + k) * STRIDE
        for j in range(ND):
            factor = scal_ref[base + 6 * j + 4]
            tiles = [q_ref[k, j, tile_rows(r), :] * factor for r in range(TILES)]
            for r, tile in enumerate(drift(j, base, tiles, scal_ref, inside)):
                out_ref[k, j, r] = tile
        return carry

    lax.fori_loop(0, bands, band, 0)


def packed_lat(j, x, d0, d1, d2):
    lane, row = lanes(), sublanes()

    def shifted(x):
        if BACK_LAT[j]:
            moved = pltpu.roll(x, 1, 0)
            over = jnp.where(lane < GROUP, x, turn(moved, GROUP))
            return jnp.where(row >= 1, moved, over)
        moved = pltpu.roll(x, 7, 0)
        over = jnp.where(lane >= (TILES - 1) * GROUP, x, turn(moved, -GROUP))
        return jnp.where(row <= 6, moved, over)

    near = shifted(x)
    return d0 * x + d1 * near + d2 * shifted(near)


def spread(tile, position):
    at_first = lanes() // 4 % BANDS == 0
    tile = jnp.where(at_first, turn(tile, -4 * position), 0.0)
    for step in (1, 2, 4):
        tile = tile + turn(tile, 4 * step)
    return tile


def packed_coefficients(inverse, speed):
    c = inverse * abs(float(speed))
    return 1.0 + c * (0.5 * c - 1.5), c * (2.0 - c), c * (0.5 * c - 0.5)


AHEAD = [j for j in range(ND) if not BACK_LON[j]]
BACK = [j for j in range(ND) if BACK_LON[j]]


def packed_fix(table, columns_ref, fix_ref):
    slot = lanes() % 4
    inverse = table(5)

    def one(j):
        back = BACK_LON[j]
        _, c1, c2 = packed_coefficients(inverse, COURANT_MAX * COS[j])
        tile = columns_ref[j]
        next_one = jnp.where(slot == (0 if back else 3), turn(tile, -1 if back else 1), 0.0)
        first = c2 * tile + c1 * next_one
        lat = packed_coefficients(inverse, 0.5 * COURANT_MAX * SIN[j])
        return packed_lat(j, first, *lat)

    for i in range(HALF):
        fix_ref[i] = jnp.where(slot < 2, one(BACK[i]), turn(one(AHEAD[i]), -4))


def packed_start(mine_right_ref, mine_left_ref, left_ref, right_ref, columns_ref, side_refs):
    near_ref, far_ref = side_refs
    lane = lanes()
    slot = lane % 4
    used = lane < TILES * GROUP
    for j in range(ND):
        half = RANK[j] % 2
        narrow = HALF + RANK[j] // 2
        if BACK_LON[j]:
            wide, own = left_ref[RANK[j]], mine_right_ref[RANK[j]]
            other = turn(right_ref[narrow], 2 - 2 * half)
            centre = jnp.where(slot < 2, turn(wide, -2), other)
            near = turn(jnp.where(slot == 3, own, wide), -1)
            near = jnp.where(slot == 3, turn(centre, 1), near)
            far = jnp.where(slot < 2, wide, own)
        else:
            wide, own = right_ref[RANK[j]], mine_left_ref[RANK[j]]
            other = turn(left_ref[narrow], -2 * half)
            centre = jnp.where(slot < 2, other, turn(wide, 2))
            near = turn(jnp.where(slot == 0, own, wide), 1)
            near = jnp.where(slot == 0, turn(centre, -1), near)
            far = jnp.where(slot < 2, own, wide)
        columns_ref[j] = jnp.where(used, centre, 0.0)
        near_ref[j] = jnp.where(used, near, 0.0)
        far_ref[j] = jnp.where(used, far, 0.0)


def packed_source(
    table, left_ref, right_ref, columns_ref, side_refs, sums_ref, part_ref, drive_ref, ice_ref
):
    near_ref, far_ref = side_refs
    lane = lanes()
    slot, place = lane % 4, lane // 4 % BANDS
    both = jnp.where(slot < 2, left_ref[SENT - 1], turn(right_ref[SENT - 1], 2))
    east, north, land, south_rows, north_rows = (spread(both, i) for i in range(FIELDS))
    row = (sublanes() + lane // GROUP * 8).astype(jnp.float32)
    held = (row < south_rows) | (row >= LAT - north_rows)
    sea = jnp.where(land > 0.5, 1.0, 0.0)
    ice = jnp.where(land > 1.5, 1.0, 0.0)
    ice_ref[...] = ice
    inverse = table(5)
    p, stress = [], []
    for j in range(ND):
        lon = packed_coefficients(inverse, COURANT_MAX * COS[j])
        lat = packed_coefficients(inverse, 0.5 * COURANT_MAX * SIN[j])
        centre = columns_ref[j]
        x = lon[0] * centre + lon[1] * near_ref[j] + lon[2] * far_ref[j]
        x = packed_lat(j, x, *lat)
        p.append(jnp.where(held, centre, jnp.maximum(x, 0.0)) * sea)
        drive = drive_of(j, east, north, 1.0 - ice)
        drive_ref[j] = drive
        stress.append(p[j] * drive)
    slope, stress = tree(p), tree(stress)

    def running(tile):
        for step in (1, 2, 4):
            tile = tile + jnp.where(place >= step, turn(tile, 4 * step), 0.0)
        return tile

    out = [jnp.zeros((8, WIDTH), jnp.float32) for _ in range(PACKED_SUMS)]

    def put(index, tile):
        position = index % BANDS
        moved = turn(tile, 4 * (position - (BANDS - 1)))
        out[index // BANDS] = jnp.where(place == position, moved, out[index // BANDS])

    for j, excess in enumerate(excess_of(p)):
        total = running(excess)
        put(j, total)
        rate = excess * table(0) + (total - excess) * table(1)
        part_ref[j] = p[j] * jnp.exp(rate)
    put(ND, running(slope * table(2)))
    put(ND + 1, running(stress * table(3)))
    for i in range(PACKED_SUMS):
        sums_ref[PACKED_AT + i] = out[i]


def excess_of(p):
    out = []
    for saturation in saturation_of(p):
        capped = jnp.maximum(saturation, CAP)
        excess = capped * lax.rsqrt(capped) - ROOT_CAP
        out.append(excess * excess)
    return out


def held_and_sea(r, land_ref, rows_ref):
    row = sublanes() + 8 * r
    held = (row < rows_ref[0:1, :]) | (row >= LAT - rows_ref[1:2, :])
    return held, jnp.where(land_ref[tile_rows(r), :] != 0, 1.0, 0.0)


def source_kernel(first, *refs):
    table_ref, x_ref, spec_ref, land_ref, rows_ref = refs[:5]
    refs = refs[5:]
    freq = lax.axis_index("freq")
    bands = x_ref.shape[0]

    def table(i):
        return table_ref[freq, i]

    if first:
        mine_right_ref, mine_left_ref, even_ref, odd_ref = refs[:4]
        p_ref, excess_ref, sums_ref, part_ref, packed_drive_ref, ice_ref = refs[4:10]
        fix_ref, left_ref, right_ref, columns_ref, near_ref, far_ref = refs[10:]
        odd = lax.axis_index("lon") % 2 == 1
        for i in range(SENT):
            even, other = even_ref[i], odd_ref[i]
            left_ref[i] = jnp.where(odd, even, other)
            right_ref[i] = jnp.where(odd, other, even)
        sides = (near_ref, far_ref)
        packed_start(mine_right_ref, mine_left_ref, left_ref, right_ref, columns_ref, sides)
        packed_source(
            table, left_ref, right_ref, columns_ref, sides,
            sums_ref, part_ref, packed_drive_ref, ice_ref,
        )
    else:
        columns_ref, p_ref, excess_ref, sums_ref, fix_ref = refs
    packed_fix(table, columns_ref, fix_ref)
    for i in range(PACKED_AT):
        sums_ref[i] = jnp.zeros((8, WIDTH), jnp.float32)

    lane = lanes()
    at_edge = {True: lane < 2, False: lane >= WIDTH - 2}

    def band(k, carry):
        for r in range(TILES):
            rows = tile_rows(r)
            held, sea = held_and_sea(r, land_ref, rows_ref)
            if not first:
                free = jnp.where(held, 0.0, sea)
            shift = jnp.bitwise_and(WIDTH - GROUP * r - 4 * k, WIDTH - 1)
            p = [None] * ND
            for i in range(HALF):
                moved = pltpu.roll(fix_ref[i], shift, 1)
                for j in (BACK[i], AHEAD[i]):
                    x = x_ref[k, j, r] + jnp.where(at_edge[BACK_LON[j]], moved, 0.0)
                    if first:
                        x = jnp.where(held, spec_ref[k, j, rows, :], jnp.maximum(x, 0.0)) * sea
                    else:
                        x = jnp.maximum(x * free, spec_ref[k, j, r])
                    p_ref[k, j, r] = x
                    p[j] = x
            for j, excess in enumerate(excess_of(p)):
                excess_ref[k, j, r] = excess
                sums_ref[TILES * j + r] += excess
        return carry

    lax.fori_loop(0, bands, band, 0)


def weights_kernel(scal_ref, p_ref, drive_ref, out_ref):
    bands = p_ref.shape[0]
    for i in range(2 * TILES):
        out_ref[i] = jnp.zeros((8, WIDTH), jnp.float32)

    def band(k, carry):
        extra = (lax.axis_index("freq") * bands + k) * STRIDE + 6 * ND
        for r in range(TILES):
            p = [p_ref[k, j, r] for j in range(ND)]
            out_ref[r] += tree(p) * scal_ref[extra + 2]
            out_ref[TILES + r] += tree([p[j] * drive_ref[j, r] for j in range(ND)]) * scal_ref[extra + 3]
        return carry

    lax.fori_loop(0, bands, band, 0)


def add_kernel(one_ref, other_ref, out_ref):
    for i in range(out_ref.shape[0]):
        out_ref[i] = one_ref[i] + other_ref[i]


def local_kernel(last, scal_ref, p_ref, excess_ref, *refs):
    if last:
        (out_ref,) = refs
    else:
        spec_ref, land_ref, rows_ref, out_ref, held_ref = refs
    bands = p_ref.shape[0]
    first = (lax.axis_index("freq") * bands) * STRIDE
    extra = first + 6 * ND
    some = 6

    def directions(group, carry):
        for r in range(TILES):
            if not last:
                held, sea = held_and_sea(r, land_ref, rows_ref)
                kept = jnp.where(held, sea, 0.0)
            for i in range(some):
                j = group * some + i
                lower = jnp.zeros((8, WIDTH), jnp.float32)
                for k in range(bands):
                    excess = excess_ref[k, j, r]
                    at = extra + k * STRIDE
                    rate = excess * scal_ref[at] + lower * scal_ref[at + 1]
                    value = p_ref[k, j, r] * jnp.exp(rate)
                    if not last:
                        value = value * scal_ref[first + k * STRIDE + 6 * j + 4]
                        held_ref[k, j, r] = spec_ref[k, j, tile_rows(r), :] * kept
                    out_ref[k, j, r] = value
                    lower = lower + excess
        return carry

    lax.fori_loop(0, ND // some, directions, 0)


def pair_kernel(sums_ref, other_ref, out_ref):
    first = (lax.axis_index("freq") % 2) * HALF_TILES
    for i in range(HALF_TILES):
        out_ref[i] = sums_ref[first + i] + other_ref[first + i]
    for i in range(out_ref.shape[0] - HALF_TILES):
        out_ref[HALF_TILES + i] = sums_ref[PACKED_AT + i] + other_ref[PACKED_AT + i]


def damp_and_gain(slope, stress, ice):
    damp = SWELL_DAMP * (slope / (slope + 1.0)) + ICE_DAMP * ice
    return damp, GROWTH * (1.0 + stress / (stress + 1.0))


def grow_half(half, last, near, refs):
    scal_ref, part_ref, other_ref, lower_ref, pair_ref, rest_ref, drive_ref, land_ref = refs[:8]
    out_ref, rate_ref, near_ref, field_ref, written_ref, sent = refs[8:]
    bands = part_ref.shape[0]
    freq = lax.axis_index("freq")
    odd = jnp.where(freq % 2 == 1, 1.0, 0.0)
    upper = jnp.where(freq >= 2, 1.0, 0.0)
    for r in range(TILES):
        rows = tile_rows(r)
        ice = jnp.where(land_ref[rows, :] == 2, 1.0, 0.0)
        slope, stress = (pair_ref[at + r] + rest_ref[at + r] for at in (0, TILES))
        damp, gain = damp_and_gain(slope, stress, ice)
        for i in range(HALF):
            j = half * HALF + i
            lower = odd * other_ref[TILES * j + r] + upper * lower_ref[TILES * i + r]
            rate_ref[i, r] = gain * drive_ref[j, r] - damp - LOWER * lower

    inside = None if last else inside_masks()
    target_ref = out_ref if near else field_ref

    def send(k, mine):
        source, which = (target_ref, half) if mine else (near_ref, 1 - half)
        place = written_ref.at[k, pl.ds(which * HALF, HALF)]
        return pltpu.make_async_copy(source.at[k], place, sent.at[int(mine), k])

    def band(k, carry):
        base = (freq * bands + k) * STRIDE
        root = scal_ref[base + 6 * ND + 4]
        for i in range(HALF):
            j = half * HALF + i
            tiles = [part_ref[k, j, r] * jnp.exp(rate_ref[i, r] * root) for r in range(TILES)]
            if last:
                for r in range(TILES):
                    target_ref[k, i, tile_rows(r), :] = tiles[r]
            else:
                for r, tile in enumerate(drift(j, base, tiles, scal_ref, inside)):
                    out_ref[k, j, r] = tile
        return carry

    def sent_band(k, carry):
        band(k, carry)
        send(k, True).start()
        return carry

    early = EARLY if near else bands
    if not last:
        lax.fori_loop(0, bands, band, 0)
        return
    if not near:
        for k in range(EARLY, bands):
            send(k, False).start()
    lax.fori_loop(0, early, sent_band, 0)
    lax.fori_loop(early, bands, band, 0)
    for k in range(early):
        send(k, True).wait()
    if not near:
        for k in range(EARLY, bands):
            send(k, False).wait()


EARLY = 1


def growth_kernel(last, near, *refs):
    operands, refs = refs[:8], refs[8:]
    other_ref, mine_ref, pair_ref, rest_ref = operands[2:6]
    freq = lax.axis_index("freq")
    if near and last:
        half_ref, slope_out_ref, written_ref, rate_ref, slope_ref, slope_sent, sent = refs
        results = (half_ref, rate_ref, None, None, written_ref, sent)
        for r in range(TILES):
            slope_ref[tile_rows(r), :] = pair_ref[r] + rest_ref[r]
        slope_copy = pltpu.make_async_copy(slope_ref, slope_out_ref, slope_sent)
        slope_copy.start()
    elif near:
        table_ref, sums_ref, packed_part_ref, packed_drive_ref, ice_ref = refs[:5]
        out_ref, columns_ref, rate_ref = refs[5:]
        results = (out_ref, rate_ref, None, None, None, None)
        odd = jnp.where(freq % 2 == 1, 1.0, 0.0)
        upper = jnp.where(freq >= 2, 1.0, 0.0)
        total, lower = [], []
        for i in range(PACKED_SUMS):
            here, there = PACKED_AT + i, HALF_TILES + i
            total.append((sums_ref[here] + other_ref[here]) + mine_ref[there])
            lower.append(odd * other_ref[here] + upper * mine_ref[there])
        slope, stress = (spread(total[i // BANDS], i % BANDS) for i in (ND, ND + 1))
        damp, gain = damp_and_gain(slope, stress, ice_ref[...])
        root = table_ref[freq, 4]
        for j in range(ND):
            under = spread(lower[j // BANDS], j % BANDS)
            rate = gain * packed_drive_ref[j] - damp - LOWER * under
            columns_ref[j] = packed_part_ref[j] * jnp.exp(root * rate)
    elif last:
        half_ref, _, out_ref, rate_ref, field_ref, sent = refs
        results = (out_ref, rate_ref, half_ref, field_ref, out_ref, sent)
    else:
        _, out_ref, rate_ref = refs
        results = (out_ref, rate_ref, None, None, None, None)
    for half in range(2):

        @pl.when(freq % 2 == (half if near else 1 - half))
        def _():
            grow_half(half, last, near, operands + results)

    if near and last:
        slope_copy.wait()


def cost(tiles, ops, moves):
    return pl.CostEstimate(
        flops=tiles * ops * 8 * WIDTH, bytes_accessed=tiles * moves * 32 * WIDTH, transcendentals=0
    )


def per_device(spectrum, east_wind, north_wind, land_sea, edge_rows):
    bands, count, lat_rows, width = spectrum.shape
    assert (bands, count, lat_rows, width) == (BANDS, ND, LAT, WIDTH)
    ring = lax.axis_size("lon")
    assert lax.axis_size("freq") == 4 and bands * 4 == NF and ring % 2 == 0
    f32 = jnp.float32

    def tiles(count):
        return jax.ShapeDtypeStruct((count, 8, WIDTH), f32)

    field = jax.ShapeDtypeStruct(spectrum.shape, f32)
    spread_field = jax.ShapeDtypeStruct((bands, ND, TILES, 8, WIDTH), f32)
    plane = jax.ShapeDtypeStruct((LAT, WIDTH), f32)
    tile = jax.ShapeDtypeStruct((8, WIDTH), f32)
    smem = pl.BlockSpec(memory_space=pltpu.SMEM)
    vmem = pl.BlockSpec(memory_space=pltpu.VMEM)
    hbm = pl.BlockSpec(memory_space=pltpu.HBM)
    params = pltpu.CompilerParams(vmem_limit_bytes=16 * 1024 * 1024)
    scalars, table = jnp.asarray(SCALARS), jnp.asarray(PACKED_TABLE)
    swap_core = [(0, 1), (1, 0), (2, 3), (3, 2)]
    swap_chip = [(0, 2), (2, 0), (1, 3), (3, 1)]
    swap_even = [(i, i ^ 1) for i in range(ring)]
    swap_odd = [(i, (i + (1 if i % 2 else -1)) % ring) for i in range(ring)]
    whole = bands * ND * TILES
    packed = pltpu.VMEM((ND, 8, WIDTH), f32)
    received = pltpu.VMEM((SENT, 8, WIDTH), f32)

    arguments = [spectrum, east_wind, north_wind, land_sea, edge_rows]
    spectrum, right, left, east_wind, north_wind, land_sea, edge_rows, even, odd = pl.pallas_call(
        pack_kernel,
        in_specs=[hbm] * 5,
        out_specs=[vmem] * 9,
        out_shape=[field, tiles(SENT), tiles(SENT)]
        + [jax.ShapeDtypeStruct(x.shape, x.dtype) for x in arguments[1:]]
        + [tiles(SENT), tiles(SENT)],
        scratch_shapes=[pltpu.SemaphoreType.DMA((bands + 4,)), packed, packed],
        compiler_params=params,
        cost_estimate=cost(whole, 6, 2),
        name="pack_columns",
    )(*(pltpu.with_memory_space_constraint(x, pltpu.HBM) for x in arguments))
    even = lax.ppermute(even, "lon", swap_even)
    odd = lax.ppermute(odd, "lon", swap_odd)
    drifted, drive = pl.pallas_call(
        drift_kernel,
        in_specs=[smem] + [vmem] * 4,
        out_specs=[vmem] * 2,
        out_shape=[spread_field, jax.ShapeDtypeStruct((ND, TILES, 8, WIDTH), f32)],
        compiler_params=params,
        cost_estimate=cost(whole, 12, 2),
        name="drift",
    )(scalars, spectrum, east_wind, north_wind, land_sea)

    for step in range(STEPS):
        first, last = step == 0, step == STEPS - 1
        sums = PACKED_AT + (PACKED_SUMS if first else 0)
        half_sums = sums - PACKED_AT + HALF_TILES
        operands = [table, drifted, spectrum if first else kept, land_sea, edge_rows]
        operands += [right, left, even, odd] if first else [columns]
        p, excess, mine, *packed_state = pl.pallas_call(
            functools.partial(source_kernel, first),
            in_specs=[vmem] * len(operands),
            out_specs=[vmem] * (6 if first else 3),
            out_shape=[spread_field, spread_field, tiles(sums)]
            + ([tiles(ND), tiles(ND), tile] if first else []),
            scratch_shapes=[packed]
            + ([received] * 2 + [packed] * 3 if first else []),
            compiler_params=params,
            cost_estimate=cost(whole, 30, 3),
            name="sources",
        )(*operands)
        other = lax.ppermute(mine, "freq", swap_core)
        weights = pl.pallas_call(
            weights_kernel,
            in_specs=[smem] + [vmem] * 2,
            out_specs=vmem,
            out_shape=tiles(2 * TILES),
            compiler_params=params,
            cost_estimate=cost(whole, 3, 1),
            name="slope_and_stress",
        )(scalars, p, drive)
        other, weights = lax.optimization_barrier((other, weights))
        weights_other = lax.ppermute(weights, "freq", swap_core)
        pair = pl.pallas_call(
            pair_kernel,
            in_specs=[vmem] * 2,
            out_specs=vmem,
            out_shape=tiles(half_sums),
            compiler_params=params,
            cost_estimate=cost(half_sums, 1, 3),
            name="pair_sums",
        )(mine, other)
        near = lax.ppermute(pair, "freq", swap_chip)
        weights_other, _ = lax.optimization_barrier((weights_other, pair))
        weights_pair = pl.pallas_call(
            add_kernel,
            in_specs=[vmem] * 2,
            out_specs=vmem,
            out_shape=tiles(2 * TILES),
            compiler_params=params,
            cost_estimate=cost(2 * TILES, 1, 3),
            name="pair_slope_and_stress",
        )(weights, weights_other)
        weights_rest = lax.ppermute(weights_pair, "freq", swap_chip)
        excess, _ = lax.optimization_barrier((excess, weights_pair))
        operands = [scalars, p, excess] + ([] if last else [spectrum, land_sea, edge_rows])
        part, *kept = pl.pallas_call(
            functools.partial(local_kernel, last),
            in_specs=[smem] + [vmem] * (len(operands) - 1),
            out_specs=[vmem] * (1 if last else 2),
            out_shape=[spread_field] * (1 if last else 2),
            compiler_params=params,
            cost_estimate=cost(whole, 8, 3),
            name="local_rate",
        )(*operands)
        kept = None if last else kept[0]
        near, weights_rest, part = lax.optimization_barrier((near, weights_rest, part))
        far = lax.ppermute(near, "freq", swap_core)

        common = [weights_pair, weights_rest, drive, land_sea]
        half_rate = pltpu.VMEM((HALF, TILES, 8, WIDTH), f32)
        half_field = (bands, HALF, LAT, WIDTH)
        sent = pltpu.SemaphoreType.DMA((2, bands))

        def grow(is_near, lower, extra, specs, results, shapes, scratch, alias):
            operands = [scalars, part, other, lower, *common, *extra]
            return pl.pallas_call(
                functools.partial(growth_kernel, last, is_near),
                in_specs=[smem] + [vmem] * (len(operands) - 1 - len(specs)) + specs,
                out_specs=results,
                out_shape=shapes,
                input_output_aliases={len(operands) - 1: 0} if alias else {},
                scratch_shapes=[half_rate] + scratch,
                compiler_params=params,
                cost_estimate=cost(whole, 6 if last else 12, 1),
                name="grow_near" if is_near else "grow_far",
            )(*operands)

        if last:
            shapes = [jax.ShapeDtypeStruct(half_field, f32), plane, field]
            scratch = [pltpu.VMEM(plane.shape, f32), pltpu.SemaphoreType.DMA(()), sent]
            made, columns, written = grow(True, near, [], [], [vmem, hbm, hbm], shapes, scratch, False)
            scratch = [pltpu.VMEM(half_field, f32), sent]
            (drifted,) = grow(False, far, [made, written], [hbm], [hbm], [field], scratch, True)
        else:
            shapes = [spread_field, tiles(ND)]
            extra = [table, mine, *packed_state]
            made, columns = grow(True, near, extra, [], [vmem] * 2, shapes, [], False)
            (drifted,) = grow(False, far, [made], [], [vmem], [spread_field], [], True)
    return drifted, columns


def solution(mesh):
    in_specs = (
        P("freq", None, None, "lon"),
        P(None, "lon"),
        P(None, "lon"),
        P(None, "lon"),
        P(None, "lon"),
    )
    out_specs = (P("freq", None, None, "lon"), P(None, "lon"))
    return jax.shard_map(
        per_device, mesh=mesh, in_specs=in_specs, out_specs=out_specs, check_vma=False
    )
```

```python
import functools
import math

import jax
import jax.numpy as jnp
import numpy as np
from jax import lax
from jax.experimental import pallas as pl
from jax.experimental.pallas import tpu as pltpu
from jax.sharding import PartitionSpec as P

NF = 32
STEPS = 2

COURANT_MAX = 0.9
FREQ_RATIO = 1.1
WIND_REF = 8.0
WIND_CLIP = 2.0
GROWTH = 0.01
BREAKING = 0.3
SATURATION_REF = 0.4
CUMULATIVE = 2.0
SWELL_DAMP = 0.1
ICE_DAMP = 0.5

ND = 36
HALF = ND // 2
QUARTER = ND // 4
DTHETA = 2.0 * math.pi / ND
LOG2E = 1.0 / math.log(2.0)
ROOT_REF = math.sqrt(SATURATION_REF)
TILES = 3
LAT = 8 * TILES
WIDTH = 128
STRIDE = 6 * ND + 8

ANGLES = np.arange(ND) * DTHETA
COS = np.cos(ANGLES)
SIN = np.sin(ANGLES)
COS2 = np.cos(2.0 * ANGLES)
SIN2 = np.sin(2.0 * ANGLES)
BACK_LON = [bool(c >= 0.0) for c in COS]
BACK_LAT = [bool(s >= 0.0) for s in SIN]
RANK = [sum(BACK_LON[:j]) if BACK_LON[j] else j - sum(BACK_LON[:j]) for j in range(ND)]


def one_sided(courant):
    c = np.abs(courant)
    return 1.0 - 1.5 * c + 0.5 * c * c, 2.0 * c - c * c, 0.5 * c * c - 0.5 * c


GROUP = 32
BANDS = 8
SENT = HALF + QUARTER + 1
FIELDS = 5
PACKED_AT = ND * TILES
PACKED_SUMS = 5
HALF_TILES = HALF * TILES
SCALE = 0.25 * DTHETA
CAP = SATURATION_REF / SCALE
ROOT_CAP = math.sqrt(CAP)
LOWER = CUMULATIVE / NF * SCALE


def make_tables():
    ratios = FREQ_RATIO ** np.arange(NF)
    root = np.sqrt(ratios)
    lon = one_sided(COURANT_MAX * COS[None, :] / ratios[:, None])
    lat = one_sided(0.5 * COURANT_MAX * SIN[None, :] / ratios[:, None])
    scalars = np.zeros((NF, STRIDE))
    for i, value in enumerate(
        (lon[1] / lon[0], lon[2] / lon[0], lat[1] / lat[0], lat[2] / lat[0], lon[0] * lat[0])
    ):
        scalars[:, i : 6 * ND : 6] = value
    rest = [
        -BREAKING / SATURATION_REF * SCALE * root,
        -LOWER * root,
        ratios * ratios * DTHETA / np.sum(ratios * ratios),
        ratios * root * DTHETA / np.sum(ratios * root),
        root,
        1.0 / ratios,
    ]
    packed = np.zeros((NF // BANDS, len(rest), 8, WIDTH))
    for i, value in enumerate(rest):
        scalars[:, 6 * ND + i] = value
        for lane in range(TILES * GROUP):
            packed[:, i, :, lane] = value[lane // 4 % BANDS :: BANDS, None]
    return scalars.reshape(-1).astype(np.float32), packed.astype(np.float32)


SCALARS, PACKED_TABLE = make_tables()


def lanes():
    return lax.broadcasted_iota(jnp.int32, (8, WIDTH), 1)


def sublanes():
    return lax.broadcasted_iota(jnp.int32, (8, WIDTH), 0)


def turn(tile, shift):
    shift = shift % WIDTH
    return tile if shift == 0 else pltpu.roll(tile, shift, 1)


def tile_rows(r):
    return slice(8 * r, 8 * r + 8)


def pack_kernel(spec_ref, *refs):
    sources, (copy_ref, right_ref, left_ref), held_refs = refs[:4], refs[4:7], refs[7:11]
    to_even_ref, to_odd_ref, arrived, four_ref, two_ref = refs[11:]

    def fetch(k):
        return pltpu.make_async_copy(spec_ref.at[k], copy_ref.at[k], arrived.at[k])

    small = [
        pltpu.make_async_copy(source, target, arrived.at[BANDS + i])
        for i, (source, target) in enumerate(zip(sources, held_refs))
    ]
    for k in range(BANDS):
        fetch(k).start()
    for copy in small:
        copy.start()
    lane = lanes()
    zero = jnp.zeros((8, WIDTH), jnp.float32)

    def by_tile(spot, tiles):
        return jnp.where(spot < GROUP, tiles[0], jnp.where(spot < 2 * GROUP, tiles[1], tiles[2]))

    first = {True: WIDTH - 4, False: 0}
    aside = {True: 4, False: -2}
    spot = {back: (lane - aside[back]) % WIDTH for back in aside}
    for k in range(BANDS):
        fetch(k).wait()
        for j in range(ND):
            back = BACK_LON[j]
            tiles = [
                turn(copy_ref[k, j, tile_rows(r), :], GROUP * r + 4 * k - first[back])
                for r in range(TILES)
            ]
            four, two = by_tile(lane, tiles), by_tile(spot[back], tiles)
            if k:
                four = jnp.where(lane // 4 % BANDS == k, four, four_ref[j])
                two = jnp.where(spot[back] // 4 % BANDS == k, two, two_ref[j])
            four_ref[j] = four
            two_ref[j] = two
    held = [zero, zero]
    for j in range(ND):
        back = BACK_LON[j]
        wide, narrow = (right_ref, left_ref) if back else (left_ref, right_ref)
        half = RANK[j] % 2
        wide[RANK[j]] = jnp.where(lane < TILES * GROUP, four_ref[j], 0.0)
        two = turn(two_ref[j], 2 * half - aside[back])
        if half:
            narrow[HALF + RANK[j] // 2] = jnp.where(lane % 4 < 2, held[back], two)
        else:
            held[back] = two
    for copy in small:
        copy.wait()
    east_ref, north_ref, land_ref, rows_ref = held_refs
    fields = [
        [f(r) for r in range(TILES)]
        for f in (
            lambda r: east_ref[tile_rows(r), :],
            lambda r: north_ref[tile_rows(r), :],
            lambda r: land_ref[tile_rows(r), :].astype(jnp.float32),
            lambda r: jnp.broadcast_to(rows_ref[0:1, :].astype(jnp.float32), (8, WIDTH)),
            lambda r: jnp.broadcast_to(rows_ref[1:2, :].astype(jnp.float32), (8, WIDTH)),
        )
    ]
    to_right, to_left = zero, zero
    for i in range(FIELDS):
        for r in range(TILES):
            place = GROUP * r + 4 * i
            here = lane // 2 == place // 2
            to_right = jnp.where(here, turn(fields[i][r], place - (WIDTH - 2)), to_right)
            to_left = jnp.where(here, turn(fields[i][r], place), to_left)
    right_ref[SENT - 1] = to_right
    left_ref[SENT - 1] = to_left
    odd = lax.axis_index("lon") % 2 == 1
    for i in range(SENT):
        right, left = right_ref[i], left_ref[i]
        to_even_ref[i] = jnp.where(odd, left, right)
        to_odd_ref[i] = jnp.where(odd, right, left)


def drive_of(j, east, north, open_water):
    along = float(COS[j] / WIND_REF) * east + float(SIN[j] / WIND_REF) * north
    drive = jnp.minimum(jnp.maximum(along, 0.0), WIND_CLIP)
    return drive * drive * open_water


def tree(values):
    values = list(values)
    while len(values) > 1:
        values = [sum(values[i + 1 : i + 2], values[i]) for i in range(0, len(values), 2)]
    return values[0]


def saturation_of(p):
    diff = [p[b] - p[b + HALF] for b in range(HALF)]
    both = [p[b] + p[b + HALF] for b in range(HALF)]
    folded = [both[b] + both[b + QUARTER] for b in range(QUARTER)]
    total = tree(folded)
    fold = [both[b] - both[b + QUARTER] for b in range(QUARTER)]
    total_c = tree([fold[0]] + [fold[b] * float(COS2[b]) for b in range(1, QUARTER)])
    total_s = tree([fold[b] * float(SIN2[b]) for b in range(1, QUARTER)])
    level = [None] * HALF
    for a in range(QUARTER):
        wave = total_c * float(COS2[a])
        if a:
            wave = wave + total_s * float(SIN2[a])
        level[a] = total + wave
        level[a + QUARTER] = total - wave

    def at(b):
        return diff[b % HALF], b // HALF % 2 == 1

    def minus(a, b):
        x, flip_x = at(a)
        y, flip_y = at(b)
        if flip_x:
            return y - x if flip_y else None, (x, y)
        return x + y if flip_y else x - y, None

    def plus_minus(value, a, b):
        gap, opposite = minus(a, b)
        if gap is None:
            return value - (opposite[0] + opposite[1])
        return value + gap

    waves = []
    for a in range(2):
        pairs = [minus(a + d, a - d + HALF)[0] for d in range(1, QUARTER)]
        weighted = [pairs[d - 1] * float(COS2[d]) for d in range(1, QUARTER)]
        waves.append(tree([diff[a]] + weighted))
        if a == 0:
            plain = tree([diff[0]] + pairs)
    twice = float(2.0 * COS2[1])
    odd, below = [None] * HALF, [None] * HALF
    odd[0] = plain + waves[0]
    window, before, now = plain, waves[0], waves[1]
    for a in range(1, QUARTER + 1):
        window = plus_minus(window, a + 8, a - 9)
        odd[a] = window + now
        if a < QUARTER:
            rest = plus_minus(before, a + 10, a + 8)
            before, now = now, twice * now - rest
    window, after, now = plain, waves[1], waves[0]
    for a in range(0, -(QUARTER - 1), -1):
        rest = plus_minus(after, a + 10, a + 8)
        after, now = now, twice * now - rest
        window = plus_minus(window, a - 9 + 2 * HALF, a + 8)
        below[a - 1 + HALF] = window + now
    out = [None] * ND
    for a in range(HALF):
        if odd[a] is not None:
            out[a], out[a + HALF] = level[a] + odd[a], level[a] - odd[a]
        else:
            out[a], out[a + HALF] = level[a] - below[a], level[a] + below[a]
    return out


def inside_masks():
    lane = lanes()
    one = jnp.ones((8, WIDTH), jnp.float32)
    return {
        (True, 1): jnp.where(lane >= 1, one, 0.0),
        (True, 2): jnp.where(lane >= 2, one, 0.0),
        (False, 1): jnp.where(lane < WIDTH - 1, one, 0.0),
        (False, 2): jnp.where(lane < WIDTH - 2, one, 0.0),
    }


def drift(j, base, tiles, scal_ref, inside):
    c1, c2, d1, d2 = (scal_ref[base + 6 * j + i] for i in range(4))
    side = 1 if BACK_LON[j] else -1
    c1 = c1 * inside[BACK_LON[j], 1]
    c2 = c2 * inside[BACK_LON[j], 2]
    x = [q + c1 * turn(q, side) + c2 * turn(q, 2 * side) for q in tiles]
    row = sublanes()
    one, two = (1, 2) if BACK_LAT[j] else (7, 6)
    at_edge = (row < 1, row < 2) if BACK_LAT[j] else (row >= 7, row >= 6)
    order = range(TILES) if BACK_LAT[j] else range(TILES - 1, -1, -1)
    moved = [[pltpu.roll(tile, by, 0) for tile in x] for by in (one, two)]
    y = [None] * TILES
    before = None
    for r in order:
        first = x[r] if before is None else moved[0][before]
        near = jnp.where(at_edge[0], first, moved[0][r])
        second = near if before is None else moved[1][before]
        far = jnp.where(at_edge[1], second, moved[1][r])
        y[r] = x[r] + d1 * near + d2 * far
        before = r
    return y


def drift_kernel(scal_ref, q_ref, east_ref, north_ref, land_ref, out_ref, drive_ref):
    bands = q_ref.shape[0]
    for r in range(TILES):
        rows = tile_rows(r)
        water = jnp.where(land_ref[rows, :] == 2, 0.0, 1.0)
        east, north = east_ref[rows, :], north_ref[rows, :]
        for j in range(ND):
            drive_ref[j, r] = drive_of(j, east, north, water)
    inside = inside_masks()

    def band(k, carry):
        base = (lax.axis_index("freq") * bands + k) * STRIDE
        for j in range(ND):
            factor = scal_ref[base + 6 * j + 4]
            tiles = [q_ref[k, j, tile_rows(r), :] * factor for r in range(TILES)]
            for r, tile in enumerate(drift(j, base, tiles, scal_ref, inside)):
                out_ref[k, j, r] = tile
        return carry

    lax.fori_loop(0, bands, band, 0)


def packed_lat(j, x, d0, d1, d2):
    lane, row = lanes(), sublanes()

    def shifted(x):
        if BACK_LAT[j]:
            moved = pltpu.roll(x, 1, 0)
            over = jnp.where(lane < GROUP, x, turn(moved, GROUP))
            return jnp.where(row >= 1, moved, over)
        moved = pltpu.roll(x, 7, 0)
        over = jnp.where(lane >= (TILES - 1) * GROUP, x, turn(moved, -GROUP))
        return jnp.where(row <= 6, moved, over)

    near = shifted(x)
    return d0 * x + d1 * near + d2 * shifted(near)


def spread(tile, position):
    at_first = lanes() // 4 % BANDS == 0
    tile = jnp.where(at_first, turn(tile, -4 * position), 0.0)
    for step in (1, 2, 4):
        tile = tile + turn(tile, 4 * step)
    return tile


def packed_coefficients(inverse, speed):
    c = inverse * abs(float(speed))
    return 1.0 + c * (0.5 * c - 1.5), c * (2.0 - c), c * (0.5 * c - 0.5)


AHEAD = [j for j in range(ND) if not BACK_LON[j]]
BACK = [j for j in range(ND) if BACK_LON[j]]


def packed_fix(table, columns_ref, fix_ref):
    slot = lanes() % 4
    inverse = table(5)

    def one(j):
        back = BACK_LON[j]
        _, c1, c2 = packed_coefficients(inverse, COURANT_MAX * COS[j])
        tile = columns_ref[j]
        next_one = jnp.where(slot == (0 if back else 3), turn(tile, -1 if back else 1), 0.0)
        first = c2 * tile + c1 * next_one
        lat = packed_coefficients(inverse, 0.5 * COURANT_MAX * SIN[j])
        return packed_lat(j, first, *lat)

    for i in range(HALF):
        fix_ref[i] = jnp.where(slot < 2, one(BACK[i]), turn(one(AHEAD[i]), -4))


def packed_start(mine_right_ref, mine_left_ref, left_ref, right_ref, columns_ref, side_refs):
    near_ref, far_ref = side_refs
    lane = lanes()
    slot = lane % 4
    used = lane < TILES * GROUP
    for j in range(ND):
        half = RANK[j] % 2
        narrow = HALF + RANK[j] // 2
        if BACK_LON[j]:
            wide, own = left_ref[RANK[j]], mine_right_ref[RANK[j]]
            other = turn(right_ref[narrow], 2 - 2 * half)
            centre = jnp.where(slot < 2, turn(wide, -2), other)
            near = turn(jnp.where(slot == 3, own, wide), -1)
            near = jnp.where(slot == 3, turn(centre, 1), near)
            far = jnp.where(slot < 2, wide, own)
        else:
            wide, own = right_ref[RANK[j]], mine_left_ref[RANK[j]]
            other = turn(left_ref[narrow], -2 * half)
            centre = jnp.where(slot < 2, other, turn(wide, 2))
            near = turn(jnp.where(slot == 0, own, wide), 1)
            near = jnp.where(slot == 0, turn(centre, -1), near)
            far = jnp.where(slot < 2, own, wide)
        columns_ref[j] = jnp.where(used, centre, 0.0)
        near_ref[j] = jnp.where(used, near, 0.0)
        far_ref[j] = jnp.where(used, far, 0.0)


def packed_source(
    table, left_ref, right_ref, columns_ref, side_refs, sums_ref, part_ref, drive_ref, ice_ref
):
    near_ref, far_ref = side_refs
    lane = lanes()
    slot, place = lane % 4, lane // 4 % BANDS
    both = jnp.where(slot < 2, left_ref[SENT - 1], turn(right_ref[SENT - 1], 2))
    east, north, land, south_rows, north_rows = (spread(both, i) for i in range(FIELDS))
    row = (sublanes() + lane // GROUP * 8).astype(jnp.float32)
    held = (row < south_rows) | (row >= LAT - north_rows)
    sea = jnp.where(land > 0.5, 1.0, 0.0)
    ice = jnp.where(land > 1.5, 1.0, 0.0)
    ice_ref[...] = ice
    inverse = table(5)
    p, slope, stress = [], [None] * 4, [None] * 4
    for j in range(ND):
        lon = packed_coefficients(inverse, COURANT_MAX * COS[j])
        lat = packed_coefficients(inverse, 0.5 * COURANT_MAX * SIN[j])
        centre = columns_ref[j]
        x = lon[0] * centre + lon[1] * near_ref[j] + lon[2] * far_ref[j]
        x = packed_lat(j, x, *lat)
        p.append(jnp.where(held, centre, jnp.maximum(x, 0.0)) * sea)
        drive = drive_of(j, east, north, 1.0 - ice)
        drive_ref[j] = drive
        push = p[j] * drive
        slope[j % 4] = p[j] if j < 4 else slope[j % 4] + p[j]
        stress[j % 4] = push if j < 4 else stress[j % 4] + push
    slope, stress = tree(slope), tree(stress)

    def running(tile):
        for step in (1, 2, 4):
            tile = tile + jnp.where(place >= step, turn(tile, 4 * step), 0.0)
        return tile

    out = [jnp.zeros((8, WIDTH), jnp.float32) for _ in range(PACKED_SUMS)]

    def put(index, tile):
        position = index % BANDS
        moved = turn(tile, 4 * (position - (BANDS - 1)))
        out[index // BANDS] = jnp.where(place == position, moved, out[index // BANDS])

    for j, excess in enumerate(excess_of(p)):
        total = running(excess)
        put(j, total)
        rate = excess * table(0) + (total - excess) * table(1)
        part_ref[j] = p[j] * jnp.exp(rate)
    put(ND, running(slope * table(2)))
    put(ND + 1, running(stress * table(3)))
    for i in range(PACKED_SUMS):
        sums_ref[PACKED_AT + i] = out[i]


def excess_of(p):
    out = []
    for saturation in saturation_of(p):
        capped = jnp.maximum(saturation, CAP)
        excess = capped * lax.rsqrt(capped) - ROOT_CAP
        out.append(excess * excess)
    return out


def held_and_sea(r, land_ref, rows_ref):
    row = sublanes() + 8 * r
    held = (row < rows_ref[0:1, :]) | (row >= LAT - rows_ref[1:2, :])
    return held, jnp.where(land_ref[tile_rows(r), :] != 0, 1.0, 0.0)


def source_kernel(first, *refs):
    table_ref, x_ref, spec_ref, land_ref, rows_ref = refs[:5]
    refs = refs[5:]
    freq = lax.axis_index("freq")
    bands = x_ref.shape[0]

    def table(i):
        return table_ref[freq, i]

    if first:
        mine_right_ref, mine_left_ref, even_ref, odd_ref = refs[:4]
        p_ref, excess_ref, sums_ref, part_ref, packed_drive_ref, ice_ref = refs[4:10]
        fix_ref, left_ref, right_ref, columns_ref, near_ref, far_ref = refs[10:]
        odd = lax.axis_index("lon") % 2 == 1
        for i in range(SENT):
            even, other = even_ref[i], odd_ref[i]
            left_ref[i] = jnp.where(odd, even, other)
            right_ref[i] = jnp.where(odd, other, even)
        sides = (near_ref, far_ref)
        packed_start(mine_right_ref, mine_left_ref, left_ref, right_ref, columns_ref, sides)
        packed_source(
            table, left_ref, right_ref, columns_ref, sides,
            sums_ref, part_ref, packed_drive_ref, ice_ref,
        )
    else:
        columns_ref, p_ref, excess_ref, sums_ref, fix_ref = refs
    packed_fix(table, columns_ref, fix_ref)
    for i in range(PACKED_AT):
        sums_ref[i] = jnp.zeros((8, WIDTH), jnp.float32)

    lane = lanes()
    at_edge = {True: lane < 2, False: lane >= WIDTH - 2}

    def band(k, carry):
        for r in range(TILES):
            rows = tile_rows(r)
            held, sea = held_and_sea(r, land_ref, rows_ref)
            if not first:
                free = jnp.where(held, 0.0, sea)
            shift = jnp.bitwise_and(WIDTH - GROUP * r - 4 * k, WIDTH - 1)
            p = [None] * ND
            for i in range(HALF):
                moved = pltpu.roll(fix_ref[i], shift, 1)
                for j in (BACK[i], AHEAD[i]):
                    x = x_ref[k, j, r] + jnp.where(at_edge[BACK_LON[j]], moved, 0.0)
                    if first:
                        x = jnp.where(held, spec_ref[k, j, rows, :], jnp.maximum(x, 0.0)) * sea
                    else:
                        x = jnp.maximum(x * free, spec_ref[k, j, r])
                    p_ref[k, j, r] = x
                    p[j] = x
            for j, excess in enumerate(excess_of(p)):
                excess_ref[k, j, r] = excess
                sums_ref[TILES * j + r] += excess
        return carry

    lax.fori_loop(0, bands, band, 0)


def weights_kernel(scal_ref, p_ref, drive_ref, out_ref):
    bands = p_ref.shape[0]
    for i in range(2 * TILES):
        out_ref[i] = jnp.zeros((8, WIDTH), jnp.float32)

    def band(k, carry):
        extra = (lax.axis_index("freq") * bands + k) * STRIDE + 6 * ND
        for r in range(TILES):
            slope, stress = [None] * 4, [None] * 4
            for j in range(ND):
                p = p_ref[k, j, r]
                push = p * drive_ref[j, r]
                slope[j % 4] = p if j < 4 else slope[j % 4] + p
                stress[j % 4] = push if j < 4 else stress[j % 4] + push
            out_ref[r] += tree(slope) * scal_ref[extra + 2]
            out_ref[TILES + r] += tree(stress) * scal_ref[extra + 3]
        return carry

    lax.fori_loop(0, bands, band, 0)


def add_kernel(one_ref, other_ref, out_ref):
    for i in range(out_ref.shape[0]):
        out_ref[i] = one_ref[i] + other_ref[i]


def local_kernel(last, scal_ref, p_ref, excess_ref, *refs):
    if last:
        (out_ref,) = refs
    else:
        spec_ref, land_ref, rows_ref, out_ref, held_ref = refs
    bands = p_ref.shape[0]
    first = (lax.axis_index("freq") * bands) * STRIDE
    extra = first + 6 * ND
    some = 6

    def directions(group, carry):
        for r in range(TILES):
            if not last:
                held, sea = held_and_sea(r, land_ref, rows_ref)
                kept = jnp.where(held, sea, 0.0)
            for i in range(some):
                j = group * some + i
                lower = jnp.zeros((8, WIDTH), jnp.float32)
                for k in range(bands):
                    excess = excess_ref[k, j, r]
                    at = extra + k * STRIDE
                    rate = excess * scal_ref[at] + lower * scal_ref[at + 1]
                    value = p_ref[k, j, r] * jnp.exp(rate)
                    if not last:
                        value = value * scal_ref[first + k * STRIDE + 6 * j + 4]
                        held_ref[k, j, r] = spec_ref[k, j, tile_rows(r), :] * kept
                    out_ref[k, j, r] = value
                    lower = lower + excess
        return carry

    lax.fori_loop(0, ND // some, directions, 0)


def pair_kernel(sums_ref, other_ref, out_ref):
    first = (lax.axis_index("freq") % 2) * HALF_TILES
    for i in range(HALF_TILES):
        out_ref[i] = sums_ref[first + i] + other_ref[first + i]
    for i in range(out_ref.shape[0] - HALF_TILES):
        out_ref[HALF_TILES + i] = sums_ref[PACKED_AT + i] + other_ref[PACKED_AT + i]


def damp_and_gain(slope, stress, ice):
    damp = SWELL_DAMP * (slope / (slope + 1.0)) + ICE_DAMP * ice
    return damp, GROWTH * (1.0 + stress / (stress + 1.0))


def grow_half(half, last, near, refs):
    scal_ref, part_ref, other_ref, lower_ref, pair_ref, rest_ref, drive_ref, land_ref = refs[:8]
    out_ref, rate_ref, near_ref, field_ref, written_ref, sent = refs[8:]
    bands = part_ref.shape[0]
    freq = lax.axis_index("freq")
    odd = jnp.where(freq % 2 == 1, 1.0, 0.0)
    upper = jnp.where(freq >= 2, 1.0, 0.0)
    for r in range(TILES):
        rows = tile_rows(r)
        ice = jnp.where(land_ref[rows, :] == 2, 1.0, 0.0)
        slope, stress = (pair_ref[at + r] + rest_ref[at + r] for at in (0, TILES))
        damp, gain = damp_and_gain(slope, stress, ice)
        for i in range(HALF):
            j = half * HALF + i
            lower = odd * other_ref[TILES * j + r] + upper * lower_ref[TILES * i + r]
            rate_ref[i, r] = gain * drive_ref[j, r] - damp - LOWER * lower

    inside = None if last else inside_masks()
    target_ref = out_ref if near else field_ref

    def send(k, mine):
        source, which = (target_ref, half) if mine else (near_ref, 1 - half)
        place = written_ref.at[k, pl.ds(which * HALF, HALF)]
        return pltpu.make_async_copy(source.at[k], place, sent.at[int(mine), k])

    def band(k, carry):
        base = (freq * bands + k) * STRIDE
        root = scal_ref[base + 6 * ND + 4]
        for i in range(HALF):
            j = half * HALF + i
            tiles = [part_ref[k, j, r] * jnp.exp(rate_ref[i, r] * root) for r in range(TILES)]
            if last:
                for r in range(TILES):
                    target_ref[k, i, tile_rows(r), :] = tiles[r]
            else:
                for r, tile in enumerate(drift(j, base, tiles, scal_ref, inside)):
                    out_ref[k, j, r] = tile
        return carry

    def sent_band(k, carry):
        band(k, carry)
        send(k, True).start()
        return carry

    early = EARLY if near else bands
    if not last:
        lax.fori_loop(0, bands, band, 0)
        return
    if not near:
        for k in range(EARLY, bands):
            send(k, False).start()
    lax.fori_loop(0, early, sent_band, 0)
    lax.fori_loop(early, bands, band, 0)
    for k in range(early):
        send(k, True).wait()
    if not near:
        for k in range(EARLY, bands):
            send(k, False).wait()


EARLY = 0


def growth_kernel(last, near, *refs):
    operands, refs = refs[:8], refs[8:]
    other_ref, mine_ref, pair_ref, rest_ref = operands[2:6]
    freq = lax.axis_index("freq")
    if near and last:
        half_ref, slope_out_ref, written_ref, rate_ref, slope_ref, slope_sent, sent = refs
        results = (half_ref, rate_ref, None, None, written_ref, sent)
        for r in range(TILES):
            slope_ref[tile_rows(r), :] = pair_ref[r] + rest_ref[r]
        slope_copy = pltpu.make_async_copy(slope_ref, slope_out_ref, slope_sent)
        slope_copy.start()
    elif near:
        table_ref, sums_ref, packed_part_ref, packed_drive_ref, ice_ref = refs[:5]
        out_ref, columns_ref, rate_ref = refs[5:]
        results = (out_ref, rate_ref, None, None, None, None)
        odd = jnp.where(freq % 2 == 1, 1.0, 0.0)
        upper = jnp.where(freq >= 2, 1.0, 0.0)
        total, lower = [], []
        for i in range(PACKED_SUMS):
            here, there = PACKED_AT + i, HALF_TILES + i
            total.append((sums_ref[here] + other_ref[here]) + mine_ref[there])
            lower.append(odd * other_ref[here] + upper * mine_ref[there])
        slope, stress = (spread(total[i // BANDS], i % BANDS) for i in (ND, ND + 1))
        damp, gain = damp_and_gain(slope, stress, ice_ref[...])
        root = table_ref[freq, 4]
        for j in range(ND):
            under = spread(lower[j // BANDS], j % BANDS)
            rate = gain * packed_drive_ref[j] - damp - LOWER * under
            columns_ref[j] = packed_part_ref[j] * jnp.exp(root * rate)
    elif last:
        half_ref, _, out_ref, rate_ref, field_ref, sent = refs
        results = (out_ref, rate_ref, half_ref, field_ref, out_ref, sent)
    else:
        _, out_ref, rate_ref = refs
        results = (out_ref, rate_ref, None, None, None, None)
    for half in range(2):

        @pl.when(freq % 2 == (half if near else 1 - half))
        def _():
            grow_half(half, last, near, operands + results)

    if near and last:
        slope_copy.wait()


def cost(tiles, ops, moves):
    return pl.CostEstimate(
        flops=tiles * ops * 8 * WIDTH, bytes_accessed=tiles * moves * 32 * WIDTH, transcendentals=0
    )


def per_device(spectrum, east_wind, north_wind, land_sea, edge_rows):
    bands, count, lat_rows, width = spectrum.shape
    assert (bands, count, lat_rows, width) == (BANDS, ND, LAT, WIDTH)
    ring = lax.axis_size("lon")
    assert lax.axis_size("freq") == 4 and bands * 4 == NF and ring % 2 == 0
    f32 = jnp.float32

    def tiles(count):
        return jax.ShapeDtypeStruct((count, 8, WIDTH), f32)

    field = jax.ShapeDtypeStruct(spectrum.shape, f32)
    spread_field = jax.ShapeDtypeStruct((bands, ND, TILES, 8, WIDTH), f32)
    plane = jax.ShapeDtypeStruct((LAT, WIDTH), f32)
    tile = jax.ShapeDtypeStruct((8, WIDTH), f32)
    smem = pl.BlockSpec(memory_space=pltpu.SMEM)
    vmem = pl.BlockSpec(memory_space=pltpu.VMEM)
    hbm = pl.BlockSpec(memory_space=pltpu.HBM)
    params = pltpu.CompilerParams(vmem_limit_bytes=16 * 1024 * 1024)
    scalars, table = jnp.asarray(SCALARS), jnp.asarray(PACKED_TABLE)
    swap_core = [(0, 1), (1, 0), (2, 3), (3, 2)]
    swap_chip = [(0, 2), (2, 0), (1, 3), (3, 1)]
    swap_even = [(i, i ^ 1) for i in range(ring)]
    swap_odd = [(i, (i + (1 if i % 2 else -1)) % ring) for i in range(ring)]
    whole = bands * ND * TILES
    packed = pltpu.VMEM((ND, 8, WIDTH), f32)
    received = pltpu.VMEM((SENT, 8, WIDTH), f32)

    arguments = [spectrum, east_wind, north_wind, land_sea, edge_rows]
    spectrum, right, left, east_wind, north_wind, land_sea, edge_rows, even, odd = pl.pallas_call(
        pack_kernel,
        in_specs=[hbm] * 5,
        out_specs=[vmem] * 9,
        out_shape=[field, tiles(SENT), tiles(SENT)]
        + [jax.ShapeDtypeStruct(x.shape, x.dtype) for x in arguments[1:]]
        + [tiles(SENT), tiles(SENT)],
        scratch_shapes=[pltpu.SemaphoreType.DMA((bands + 4,)), packed, packed],
        compiler_params=params,
        cost_estimate=cost(whole, 6, 2),
        name="pack_columns",
    )(*(pltpu.with_memory_space_constraint(x, pltpu.HBM) for x in arguments))
    even = lax.ppermute(even, "lon", swap_even)
    odd = lax.ppermute(odd, "lon", swap_odd)
    drifted, drive = pl.pallas_call(
        drift_kernel,
        in_specs=[smem] + [vmem] * 4,
        out_specs=[vmem] * 2,
        out_shape=[spread_field, jax.ShapeDtypeStruct((ND, TILES, 8, WIDTH), f32)],
        compiler_params=params,
        cost_estimate=cost(whole, 12, 2),
        name="drift",
    )(scalars, spectrum, east_wind, north_wind, land_sea)

    for step in range(STEPS):
        first, last = step == 0, step == STEPS - 1
        sums = PACKED_AT + (PACKED_SUMS if first else 0)
        half_sums = sums - PACKED_AT + HALF_TILES
        operands = [table, drifted, spectrum if first else kept, land_sea, edge_rows]
        operands += [right, left, even, odd] if first else [columns]
        p, excess, mine, *packed_state = pl.pallas_call(
            functools.partial(source_kernel, first),
            in_specs=[vmem] * len(operands),
            out_specs=[vmem] * (6 if first else 3),
            out_shape=[spread_field, spread_field, tiles(sums)]
            + ([tiles(ND), tiles(ND), tile] if first else []),
            scratch_shapes=[packed]
            + ([received] * 2 + [packed] * 3 if first else []),
            compiler_params=params,
            cost_estimate=cost(whole, 30, 3),
            name="sources",
        )(*operands)
        other = lax.ppermute(mine, "freq", swap_core)
        weights = pl.pallas_call(
            weights_kernel,
            in_specs=[smem] + [vmem] * 2,
            out_specs=vmem,
            out_shape=tiles(2 * TILES),
            compiler_params=params,
            cost_estimate=cost(whole, 3, 1),
            name="slope_and_stress",
        )(scalars, p, drive)
        other, weights = lax.optimization_barrier((other, weights))
        weights_other = lax.ppermute(weights, "freq", swap_core)
        pair = pl.pallas_call(
            pair_kernel,
            in_specs=[vmem] * 2,
            out_specs=vmem,
            out_shape=tiles(half_sums),
            compiler_params=params,
            cost_estimate=cost(half_sums, 1, 3),
            name="pair_sums",
        )(mine, other)
        near = lax.ppermute(pair, "freq", swap_chip)
        weights_other, _ = lax.optimization_barrier((weights_other, pair))
        weights_pair = pl.pallas_call(
            add_kernel,
            in_specs=[vmem] * 2,
            out_specs=vmem,
            out_shape=tiles(2 * TILES),
            compiler_params=params,
            cost_estimate=cost(2 * TILES, 1, 3),
            name="pair_slope_and_stress",
        )(weights, weights_other)
        weights_rest = lax.ppermute(weights_pair, "freq", swap_chip)
        excess, _ = lax.optimization_barrier((excess, weights_pair))
        operands = [scalars, p, excess] + ([] if last else [spectrum, land_sea, edge_rows])
        part, *kept = pl.pallas_call(
            functools.partial(local_kernel, last),
            in_specs=[smem] + [vmem] * (len(operands) - 1),
            out_specs=[vmem] * (1 if last else 2),
            out_shape=[spread_field] * (1 if last else 2),
            compiler_params=params,
            cost_estimate=cost(whole, 8, 3),
            name="local_rate",
        )(*operands)
        kept = None if last else kept[0]
        near, weights_rest, part = lax.optimization_barrier((near, weights_rest, part))
        far = lax.ppermute(near, "freq", swap_core)

        common = [weights_pair, weights_rest, drive, land_sea]
        half_rate = pltpu.VMEM((HALF, TILES, 8, WIDTH), f32)
        half_field = (bands, HALF, LAT, WIDTH)
        sent = pltpu.SemaphoreType.DMA((2, bands))

        def grow(is_near, lower, extra, specs, results, shapes, scratch, alias):
            operands = [scalars, part, other, lower, *common, *extra]
            return pl.pallas_call(
                functools.partial(growth_kernel, last, is_near),
                in_specs=[smem] + [vmem] * (len(operands) - 1 - len(specs)) + specs,
                out_specs=results,
                out_shape=shapes,
                input_output_aliases={len(operands) - 1: 0} if alias else {},
                scratch_shapes=[half_rate] + scratch,
                compiler_params=params,
                cost_estimate=cost(whole, 6 if last else 12, 1),
                name="grow_near" if is_near else "grow_far",
            )(*operands)

        if last:
            shapes = [jax.ShapeDtypeStruct(half_field, f32), plane, field]
            scratch = [pltpu.VMEM(plane.shape, f32), pltpu.SemaphoreType.DMA(()), sent]
            made, columns, written = grow(True, near, [], [], [vmem, hbm, hbm], shapes, scratch, False)
            scratch = [pltpu.VMEM(half_field, f32), sent]
            (drifted,) = grow(False, far, [made, written], [hbm], [hbm], [field], scratch, True)
        else:
            shapes = [spread_field, tiles(ND)]
            extra = [table, mine, *packed_state]
            made, columns = grow(True, near, extra, [], [vmem] * 2, shapes, [], False)
            (drifted,) = grow(False, far, [made], [], [vmem], [spread_field], [], True)
    return drifted, columns


def solution(mesh):
    in_specs = (
        P("freq", None, None, "lon"),
        P(None, "lon"),
        P(None, "lon"),
        P(None, "lon"),
        P(None, "lon"),
    )
    out_specs = (P("freq", None, None, "lon"), P(None, "lon"))
    return jax.shard_map(
        per_device, mesh=mesh, in_specs=in_specs, out_specs=out_specs, check_vma=False
    )
```

```python
import functools
import math

import jax
import jax.numpy as jnp
import numpy as np
from jax import lax
from jax.experimental import pallas as pl
from jax.experimental.pallas import tpu as pltpu
from jax.sharding import PartitionSpec as P

NF = 32
STEPS = 2

COURANT_MAX = 0.9
FREQ_RATIO = 1.1
WIND_REF = 8.0
WIND_CLIP = 2.0
GROWTH = 0.01
BREAKING = 0.3
SATURATION_REF = 0.4
CUMULATIVE = 2.0
SWELL_DAMP = 0.1
ICE_DAMP = 0.5

ND = 36
HALF = ND // 2
QUARTER = ND // 4
DTHETA = 2.0 * math.pi / ND
LOG2E = 1.0 / math.log(2.0)
ROOT_REF = math.sqrt(SATURATION_REF)
TILES = 3
LAT = 8 * TILES
WIDTH = 128
STRIDE = 6 * ND + 8

ANGLES = np.arange(ND) * DTHETA
COS = np.cos(ANGLES)
SIN = np.sin(ANGLES)
COS2 = np.cos(2.0 * ANGLES)
SIN2 = np.sin(2.0 * ANGLES)
BACK_LON = [bool(c >= 0.0) for c in COS]
BACK_LAT = [bool(s >= 0.0) for s in SIN]
RANK = [sum(BACK_LON[:j]) if BACK_LON[j] else j - sum(BACK_LON[:j]) for j in range(ND)]


def one_sided(courant):
    c = np.abs(courant)
    return 1.0 - 1.5 * c + 0.5 * c * c, 2.0 * c - c * c, 0.5 * c * c - 0.5 * c


GROUP = 32
BANDS = 8
SENT = HALF + QUARTER + 1
FIELDS = 5
PACKED_AT = ND * TILES
PACKED_SUMS = 5
HALF_TILES = HALF * TILES
SCALE = 0.25 * DTHETA
CAP = SATURATION_REF / SCALE
ROOT_CAP = math.sqrt(CAP)
LOWER = CUMULATIVE / NF * SCALE


def make_tables():
    ratios = FREQ_RATIO ** np.arange(NF)
    root = np.sqrt(ratios)
    lon = one_sided(COURANT_MAX * COS[None, :] / ratios[:, None])
    lat = one_sided(0.5 * COURANT_MAX * SIN[None, :] / ratios[:, None])
    scalars = np.zeros((NF, STRIDE))
    for i, value in enumerate(
        (lon[1] / lon[0], lon[2] / lon[0], lat[1] / lat[0], lat[2] / lat[0], lon[0] * lat[0])
    ):
        scalars[:, i : 6 * ND : 6] = value
    rest = [
        -BREAKING / SATURATION_REF * SCALE * root,
        -LOWER * root,
        ratios * ratios * DTHETA / np.sum(ratios * ratios),
        ratios * root * DTHETA / np.sum(ratios * root),
        root,
        1.0 / ratios,
    ]
    packed = np.zeros((NF // BANDS, len(rest), 8, WIDTH))
    for i, value in enumerate(rest):
        scalars[:, 6 * ND + i] = value
        for lane in range(TILES * GROUP):
            packed[:, i, :, lane] = value[lane // 4 % BANDS :: BANDS, None]
    return scalars.reshape(-1).astype(np.float32), packed.astype(np.float32)


SCALARS, PACKED_TABLE = make_tables()


def lanes():
    return lax.broadcasted_iota(jnp.int32, (8, WIDTH), 1)


def sublanes():
    return lax.broadcasted_iota(jnp.int32, (8, WIDTH), 0)


def turn(tile, shift):
    shift = shift % WIDTH
    return tile if shift == 0 else pltpu.roll(tile, shift, 1)


def tile_rows(r):
    return slice(8 * r, 8 * r + 8)


def pack_kernel(spec_ref, *refs):
    sources, (copy_ref, right_ref, left_ref), held_refs = refs[:4], refs[4:7], refs[7:11]
    to_even_ref, to_odd_ref, arrived, four_ref, two_ref = refs[11:]

    def fetch(k):
        return pltpu.make_async_copy(spec_ref.at[k], copy_ref.at[k], arrived.at[k])

    small = [
        pltpu.make_async_copy(source, target, arrived.at[BANDS + i])
        for i, (source, target) in enumerate(zip(sources, held_refs))
    ]
    for k in range(BANDS):
        fetch(k).start()
    for copy in small:
        copy.start()
    lane = lanes()
    zero = jnp.zeros((8, WIDTH), jnp.float32)

    def by_tile(spot, tiles):
        return jnp.where(spot < GROUP, tiles[0], jnp.where(spot < 2 * GROUP, tiles[1], tiles[2]))

    first = {True: WIDTH - 4, False: 0}
    aside = {True: 4, False: -2}
    spot = {back: (lane - aside[back]) % WIDTH for back in aside}
    for k in range(BANDS):
        fetch(k).wait()
        for j in range(ND):
            back = BACK_LON[j]
            tiles = [
                turn(copy_ref[k, j, tile_rows(r), :], GROUP * r + 4 * k - first[back])
                for r in range(TILES)
            ]
            four, two = by_tile(lane, tiles), by_tile(spot[back], tiles)
            if k:
                four = jnp.where(lane // 4 % BANDS == k, four, four_ref[j])
                two = jnp.where(spot[back] // 4 % BANDS == k, two, two_ref[j])
            four_ref[j] = four
            two_ref[j] = two
    held = [zero, zero]
    for j in range(ND):
        back = BACK_LON[j]
        wide, narrow = (right_ref, left_ref) if back else (left_ref, right_ref)
        half = RANK[j] % 2
        wide[RANK[j]] = jnp.where(lane < TILES * GROUP, four_ref[j], 0.0)
        two = turn(two_ref[j], 2 * half - aside[back])
        if half:
            narrow[HALF + RANK[j] // 2] = jnp.where(lane % 4 < 2, held[back], two)
        else:
            held[back] = two
    for copy in small:
        copy.wait()
    east_ref, north_ref, land_ref, rows_ref = held_refs
    fields = [
        [f(r) for r in range(TILES)]
        for f in (
            lambda r: east_ref[tile_rows(r), :],
            lambda r: north_ref[tile_rows(r), :],
            lambda r: land_ref[tile_rows(r), :].astype(jnp.float32),
            lambda r: jnp.broadcast_to(rows_ref[0:1, :].astype(jnp.float32), (8, WIDTH)),
            lambda r: jnp.broadcast_to(rows_ref[1:2, :].astype(jnp.float32), (8, WIDTH)),
        )
    ]
    to_right, to_left = zero, zero
    for i in range(FIELDS):
        for r in range(TILES):
            place = GROUP * r + 4 * i
            here = lane // 2 == place // 2
            to_right = jnp.where(here, turn(fields[i][r], place - (WIDTH - 2)), to_right)
            to_left = jnp.where(here, turn(fields[i][r], place), to_left)
    right_ref[SENT - 1] = to_right
    left_ref[SENT - 1] = to_left
    odd = lax.axis_index("lon") % 2 == 1
    for i in range(SENT):
        right, left = right_ref[i], left_ref[i]
        to_even_ref[i] = jnp.where(odd, left, right)
        to_odd_ref[i] = jnp.where(odd, right, left)


def drive_of(j, east, north, open_water):
    along = float(COS[j] / WIND_REF) * east + float(SIN[j] / WIND_REF) * north
    drive = jnp.minimum(jnp.maximum(along, 0.0), WIND_CLIP)
    return drive * drive * open_water


def in_pairs(count, body):
    def both(i, carry):
        body(2 * i, carry)
        return body(2 * i + 1, carry)

    lax.fori_loop(0, count // 2, both, 0)


def tree(values):
    values = list(values)
    while len(values) > 1:
        values = [sum(values[i + 1 : i + 2], values[i]) for i in range(0, len(values), 2)]
    return values[0]


def saturation_of(p):
    diff = [p[b] - p[b + HALF] for b in range(HALF)]
    both = [p[b] + p[b + HALF] for b in range(HALF)]
    folded = [both[b] + both[b + QUARTER] for b in range(QUARTER)]
    total = tree(folded)
    fold = [both[b] - both[b + QUARTER] for b in range(QUARTER)]
    total_c = tree([fold[0]] + [fold[b] * float(COS2[b]) for b in range(1, QUARTER)])
    total_s = tree([fold[b] * float(SIN2[b]) for b in range(1, QUARTER)])
    level = [None] * HALF
    for a in range(QUARTER):
        wave = total_c * float(COS2[a])
        if a:
            wave = wave + total_s * float(SIN2[a])
        level[a] = total + wave
        level[a + QUARTER] = total - wave

    def at(b):
        return diff[b % HALF], b // HALF % 2 == 1

    def minus(a, b):
        x, flip_x = at(a)
        y, flip_y = at(b)
        if flip_x:
            return y - x if flip_y else None, (x, y)
        return x + y if flip_y else x - y, None

    def plus_minus(value, a, b):
        gap, opposite = minus(a, b)
        if gap is None:
            return value - (opposite[0] + opposite[1])
        return value + gap

    waves = []
    for a in range(2):
        pairs = [minus(a + d, a - d + HALF)[0] for d in range(1, QUARTER)]
        weighted = [pairs[d - 1] * float(COS2[d]) for d in range(1, QUARTER)]
        waves.append(tree([diff[a]] + weighted))
        if a == 0:
            plain = tree([diff[0]] + pairs)
    twice = float(2.0 * COS2[1])
    odd, below = [None] * HALF, [None] * HALF
    odd[0] = plain + waves[0]
    window, before, now = plain, waves[0], waves[1]
    for a in range(1, QUARTER + 1):
        window = plus_minus(window, a + 8, a - 9)
        odd[a] = window + now
        if a < QUARTER:
            rest = plus_minus(before, a + 10, a + 8)
            before, now = now, twice * now - rest
    window, after, now = plain, waves[1], waves[0]
    for a in range(0, -(QUARTER - 1), -1):
        rest = plus_minus(after, a + 10, a + 8)
        after, now = now, twice * now - rest
        window = plus_minus(window, a - 9 + 2 * HALF, a + 8)
        below[a - 1 + HALF] = window + now
    out = [None] * ND
    for a in range(HALF):
        if odd[a] is not None:
            out[a], out[a + HALF] = level[a] + odd[a], level[a] - odd[a]
        else:
            out[a], out[a + HALF] = level[a] - below[a], level[a] + below[a]
    return out


def inside_masks():
    lane = lanes()
    one = jnp.ones((8, WIDTH), jnp.float32)
    return {
        (True, 1): jnp.where(lane >= 1, one, 0.0),
        (True, 2): jnp.where(lane >= 2, one, 0.0),
        (False, 1): jnp.where(lane < WIDTH - 1, one, 0.0),
        (False, 2): jnp.where(lane < WIDTH - 2, one, 0.0),
    }


def drift(j, base, tiles, scal_ref, inside):
    c1, c2, d1, d2 = (scal_ref[base + 6 * j + i] for i in range(4))
    side = 1 if BACK_LON[j] else -1
    c1 = c1 * inside[BACK_LON[j], 1]
    c2 = c2 * inside[BACK_LON[j], 2]
    x = [q + c1 * turn(q, side) + c2 * turn(q, 2 * side) for q in tiles]
    row = sublanes()
    one, two = (1, 2) if BACK_LAT[j] else (7, 6)
    at_edge = (row < 1, row < 2) if BACK_LAT[j] else (row >= 7, row >= 6)
    order = range(TILES) if BACK_LAT[j] else range(TILES - 1, -1, -1)
    moved = [[pltpu.roll(tile, by, 0) for tile in x] for by in (one, two)]
    y = [None] * TILES
    before = None
    for r in order:
        first = x[r] if before is None else moved[0][before]
        near = jnp.where(at_edge[0], first, moved[0][r])
        second = near if before is None else moved[1][before]
        far = jnp.where(at_edge[1], second, moved[1][r])
        y[r] = x[r] + d1 * near + d2 * far
        before = r
    return y


def drift_kernel(scal_ref, q_ref, east_ref, north_ref, land_ref, out_ref, drive_ref):
    bands = q_ref.shape[0]
    for r in range(TILES):
        rows = tile_rows(r)
        water = jnp.where(land_ref[rows, :] == 2, 0.0, 1.0)
        east, north = east_ref[rows, :], north_ref[rows, :]
        for j in range(ND):
            drive_ref[j, r] = drive_of(j, east, north, water)
    inside = inside_masks()

    def band(k, carry):
        base = (lax.axis_index("freq") * bands + k) * STRIDE
        for j in range(ND):
            factor = scal_ref[base + 6 * j + 4]
            tiles = [q_ref[k, j, tile_rows(r), :] * factor for r in range(TILES)]
            for r, tile in enumerate(drift(j, base, tiles, scal_ref, inside)):
                out_ref[k, j, r] = tile
        return carry

    lax.fori_loop(0, bands, band, 0)


def packed_lat(j, x, d0, d1, d2):
    lane, row = lanes(), sublanes()

    def shifted(x):
        if BACK_LAT[j]:
            moved = pltpu.roll(x, 1, 0)
            over = jnp.where(lane < GROUP, x, turn(moved, GROUP))
            return jnp.where(row >= 1, moved, over)
        moved = pltpu.roll(x, 7, 0)
        over = jnp.where(lane >= (TILES - 1) * GROUP, x, turn(moved, -GROUP))
        return jnp.where(row <= 6, moved, over)

    near = shifted(x)
    return d0 * x + d1 * near + d2 * shifted(near)


def spread(tile, position):
    at_first = lanes() // 4 % BANDS == 0
    tile = jnp.where(at_first, turn(tile, -4 * position), 0.0)
    for step in (1, 2, 4):
        tile = tile + turn(tile, 4 * step)
    return tile


def packed_coefficients(inverse, speed):
    c = inverse * abs(float(speed))
    return 1.0 + c * (0.5 * c - 1.5), c * (2.0 - c), c * (0.5 * c - 0.5)


AHEAD = [j for j in range(ND) if not BACK_LON[j]]
BACK = [j for j in range(ND) if BACK_LON[j]]


def packed_fix(table, columns_ref, fix_ref):
    slot = lanes() % 4
    inverse = table(5)

    def one(j):
        back = BACK_LON[j]
        _, c1, c2 = packed_coefficients(inverse, COURANT_MAX * COS[j])
        tile = columns_ref[j]
        next_one = jnp.where(slot == (0 if back else 3), turn(tile, -1 if back else 1), 0.0)
        first = c2 * tile + c1 * next_one
        lat = packed_coefficients(inverse, 0.5 * COURANT_MAX * SIN[j])
        return packed_lat(j, first, *lat)

    for i in range(HALF):
        fix_ref[i] = jnp.where(slot < 2, one(BACK[i]), turn(one(AHEAD[i]), -4))


def packed_start(mine_right_ref, mine_left_ref, left_ref, right_ref, columns_ref, side_refs):
    near_ref, far_ref = side_refs
    lane = lanes()
    slot = lane % 4
    used = lane < TILES * GROUP
    for j in range(ND):
        half = RANK[j] % 2
        narrow = HALF + RANK[j] // 2
        if BACK_LON[j]:
            wide, own = left_ref[RANK[j]], mine_right_ref[RANK[j]]
            other = turn(right_ref[narrow], 2 - 2 * half)
            centre = jnp.where(slot < 2, turn(wide, -2), other)
            near = turn(jnp.where(slot == 3, own, wide), -1)
            near = jnp.where(slot == 3, turn(centre, 1), near)
            far = jnp.where(slot < 2, wide, own)
        else:
            wide, own = right_ref[RANK[j]], mine_left_ref[RANK[j]]
            other = turn(left_ref[narrow], -2 * half)
            centre = jnp.where(slot < 2, other, turn(wide, 2))
            near = turn(jnp.where(slot == 0, own, wide), 1)
            near = jnp.where(slot == 0, turn(centre, -1), near)
            far = jnp.where(slot < 2, own, wide)
        columns_ref[j] = jnp.where(used, centre, 0.0)
        near_ref[j] = jnp.where(used, near, 0.0)
        far_ref[j] = jnp.where(used, far, 0.0)


def packed_source(
    table, left_ref, right_ref, columns_ref, side_refs, sums_ref, part_ref, drive_ref, ice_ref
):
    near_ref, far_ref = side_refs
    lane = lanes()
    slot, place = lane % 4, lane // 4 % BANDS
    both = jnp.where(slot < 2, left_ref[SENT - 1], turn(right_ref[SENT - 1], 2))
    east, north, land, south_rows, north_rows = (spread(both, i) for i in range(FIELDS))
    row = (sublanes() + lane // GROUP * 8).astype(jnp.float32)
    held = (row < south_rows) | (row >= LAT - north_rows)
    sea = jnp.where(land > 0.5, 1.0, 0.0)
    ice = jnp.where(land > 1.5, 1.0, 0.0)
    ice_ref[...] = ice
    inverse = table(5)
    p, slope, stress = [], [None] * 4, [None] * 4
    for j in range(ND):
        lon = packed_coefficients(inverse, COURANT_MAX * COS[j])
        lat = packed_coefficients(inverse, 0.5 * COURANT_MAX * SIN[j])
        centre = columns_ref[j]
        x = lon[0] * centre + lon[1] * near_ref[j] + lon[2] * far_ref[j]
        x = packed_lat(j, x, *lat)
        p.append(jnp.where(held, centre, jnp.maximum(x, 0.0)) * sea)
        drive = drive_of(j, east, north, 1.0 - ice)
        drive_ref[j] = drive
        push = p[j] * drive
        slope[j % 4] = p[j] if j < 4 else slope[j % 4] + p[j]
        stress[j % 4] = push if j < 4 else stress[j % 4] + push
    slope, stress = tree(slope), tree(stress)

    def running(tile):
        for step in (1, 2, 4):
            tile = tile + jnp.where(place >= step, turn(tile, 4 * step), 0.0)
        return tile

    out = [jnp.zeros((8, WIDTH), jnp.float32) for _ in range(PACKED_SUMS)]

    def put(index, tile):
        position = index % BANDS
        moved = turn(tile, 4 * (position - (BANDS - 1)))
        out[index // BANDS] = jnp.where(place == position, moved, out[index // BANDS])

    for j, excess in enumerate(excess_of(p)):
        total = running(excess)
        put(j, total)
        rate = excess * table(0) + (total - excess) * table(1)
        part_ref[j] = p[j] * jnp.exp(rate)
    put(ND, running(slope * table(2)))
    put(ND + 1, running(stress * table(3)))
    for i in range(PACKED_SUMS):
        sums_ref[PACKED_AT + i] = out[i]


def excess_of(p):
    out = []
    for saturation in saturation_of(p):
        capped = jnp.maximum(saturation, CAP)
        excess = capped * lax.rsqrt(capped) - ROOT_CAP
        out.append(excess * excess)
    return out


def held_and_sea(r, land_ref, rows_ref):
    row = sublanes() + 8 * r
    held = (row < rows_ref[0:1, :]) | (row >= LAT - rows_ref[1:2, :])
    return held, jnp.where(land_ref[tile_rows(r), :] != 0, 1.0, 0.0)


def source_kernel(first, *refs):
    table_ref, x_ref, spec_ref, land_ref, rows_ref = refs[:5]
    refs = refs[5:]
    freq = lax.axis_index("freq")
    bands = x_ref.shape[0]

    def table(i):
        return table_ref[freq, i]

    if first:
        mine_right_ref, mine_left_ref, even_ref, odd_ref = refs[:4]
        p_ref, excess_ref, sums_ref, part_ref, packed_drive_ref, ice_ref = refs[4:10]
        fix_ref, left_ref, right_ref, columns_ref, near_ref, far_ref = refs[10:]
        odd = lax.axis_index("lon") % 2 == 1
        for i in range(SENT):
            even, other = even_ref[i], odd_ref[i]
            left_ref[i] = jnp.where(odd, even, other)
            right_ref[i] = jnp.where(odd, other, even)
        sides = (near_ref, far_ref)
        packed_start(mine_right_ref, mine_left_ref, left_ref, right_ref, columns_ref, sides)
        packed_source(
            table, left_ref, right_ref, columns_ref, sides,
            sums_ref, part_ref, packed_drive_ref, ice_ref,
        )
    else:
        columns_ref, p_ref, excess_ref, sums_ref, fix_ref = refs
    packed_fix(table, columns_ref, fix_ref)
    for i in range(PACKED_AT):
        sums_ref[i] = jnp.zeros((8, WIDTH), jnp.float32)

    lane = lanes()
    at_edge = {True: lane < 2, False: lane >= WIDTH - 2}

    def band(k, carry):
        for r in range(TILES):
            rows = tile_rows(r)
            held, sea = held_and_sea(r, land_ref, rows_ref)
            if not first:
                free = jnp.where(held, 0.0, sea)
            shift = jnp.bitwise_and(WIDTH - GROUP * r - 4 * k, WIDTH - 1)
            p = [None] * ND
            for i in range(HALF):
                moved = pltpu.roll(fix_ref[i], shift, 1)
                for j in (BACK[i], AHEAD[i]):
                    x = x_ref[k, j, r] + jnp.where(at_edge[BACK_LON[j]], moved, 0.0)
                    if first:
                        x = jnp.where(held, spec_ref[k, j, rows, :], jnp.maximum(x, 0.0)) * sea
                    else:
                        x = jnp.maximum(x * free, spec_ref[k, j, r])
                    p_ref[k, j, r] = x
                    p[j] = x
            for j, excess in enumerate(excess_of(p)):
                excess_ref[k, j, r] = excess
                sums_ref[TILES * j + r] += excess
        return carry

    in_pairs(bands, band)


def weights_kernel(scal_ref, p_ref, drive_ref, out_ref):
    bands = p_ref.shape[0]
    for i in range(2 * TILES):
        out_ref[i] = jnp.zeros((8, WIDTH), jnp.float32)

    def band(k, carry):
        extra = (lax.axis_index("freq") * bands + k) * STRIDE + 6 * ND
        for r in range(TILES):
            slope, stress = [None] * 4, [None] * 4
            for j in range(ND):
                p = p_ref[k, j, r]
                push = p * drive_ref[j, r]
                slope[j % 4] = p if j < 4 else slope[j % 4] + p
                stress[j % 4] = push if j < 4 else stress[j % 4] + push
            out_ref[r] += tree(slope) * scal_ref[extra + 2]
            out_ref[TILES + r] += tree(stress) * scal_ref[extra + 3]
        return carry

    lax.fori_loop(0, bands, band, 0)


def add_kernel(one_ref, other_ref, out_ref):
    for i in range(out_ref.shape[0]):
        out_ref[i] = one_ref[i] + other_ref[i]


def local_kernel(last, scal_ref, p_ref, excess_ref, *refs):
    if last:
        (out_ref,) = refs
    else:
        spec_ref, land_ref, rows_ref, out_ref, held_ref = refs
    bands = p_ref.shape[0]
    first = (lax.axis_index("freq") * bands) * STRIDE
    extra = first + 6 * ND
    some = 6

    def directions(group, carry):
        for r in range(TILES):
            if not last:
                held, sea = held_and_sea(r, land_ref, rows_ref)
                kept = jnp.where(held, sea, 0.0)
            for i in range(some):
                j = group * some + i
                lower = jnp.zeros((8, WIDTH), jnp.float32)
                for k in range(bands):
                    excess = excess_ref[k, j, r]
                    at = extra + k * STRIDE
                    rate = excess * scal_ref[at] + lower * scal_ref[at + 1]
                    value = p_ref[k, j, r] * jnp.exp(rate)
                    if not last:
                        value = value * scal_ref[first + k * STRIDE + 6 * j + 4]
                        held_ref[k, j, r] = spec_ref[k, j, tile_rows(r), :] * kept
                    out_ref[k, j, r] = value
                    lower = lower + excess
        return carry

    lax.fori_loop(0, ND // some, directions, 0)


def pair_kernel(sums_ref, other_ref, out_ref):
    first = (lax.axis_index("freq") % 2) * HALF_TILES
    for i in range(HALF_TILES):
        out_ref[i] = sums_ref[first + i] + other_ref[first + i]
    for i in range(out_ref.shape[0] - HALF_TILES):
        out_ref[HALF_TILES + i] = sums_ref[PACKED_AT + i] + other_ref[PACKED_AT + i]


def damp_and_gain(slope, stress, ice):
    damp = SWELL_DAMP * (slope / (slope + 1.0)) + ICE_DAMP * ice
    return damp, GROWTH * (1.0 + stress / (stress + 1.0))


def grow_half(half, last, near, refs):
    scal_ref, part_ref, other_ref, lower_ref, pair_ref, rest_ref, drive_ref, land_ref = refs[:8]
    out_ref, rate_ref, near_ref, field_ref, written_ref, sent = refs[8:]
    bands = part_ref.shape[0]
    freq = lax.axis_index("freq")
    odd = jnp.where(freq % 2 == 1, 1.0, 0.0)
    upper = jnp.where(freq >= 2, 1.0, 0.0)
    for r in range(TILES):
        rows = tile_rows(r)
        ice = jnp.where(land_ref[rows, :] == 2, 1.0, 0.0)
        slope, stress = (pair_ref[at + r] + rest_ref[at + r] for at in (0, TILES))
        damp, gain = damp_and_gain(slope, stress, ice)
        for i in range(HALF):
            j = half * HALF + i
            lower = odd * other_ref[TILES * j + r] + upper * lower_ref[TILES * i + r]
            rate_ref[i, r] = gain * drive_ref[j, r] - damp - LOWER * lower

    inside = None if last else inside_masks()
    target_ref = out_ref if near else field_ref

    def send(k, mine):
        source, which = (target_ref, half) if mine else (near_ref, 1 - half)
        place = written_ref.at[k, pl.ds(which * HALF, HALF)]
        return pltpu.make_async_copy(source.at[k], place, sent.at[int(mine), k])

    def band(k, carry):
        base = (freq * bands + k) * STRIDE
        root = scal_ref[base + 6 * ND + 4]
        for i in range(HALF):
            j = half * HALF + i
            tiles = [part_ref[k, j, r] * jnp.exp(rate_ref[i, r] * root) for r in range(TILES)]
            if last:
                for r in range(TILES):
                    target_ref[k, i, tile_rows(r), :] = tiles[r]
            else:
                for r, tile in enumerate(drift(j, base, tiles, scal_ref, inside)):
                    out_ref[k, j, r] = tile
        return carry

    def sent_band(k, carry):
        band(k, carry)
        send(k, True).start()
        return carry

    if not last:
        in_pairs(bands, band)
        return
    if near:
        in_pairs(bands, band)
        return
    for k in range(bands):
        send(k, False).start()
    in_pairs(bands, sent_band)
    for k in range(bands):
        send(k, True).wait()
        send(k, False).wait()


def growth_kernel(last, near, *refs):
    operands, refs = refs[:8], refs[8:]
    other_ref, mine_ref, pair_ref, rest_ref = operands[2:6]
    freq = lax.axis_index("freq")
    if near and last:
        half_ref, slope_out_ref, written_ref, rate_ref, slope_ref, slope_sent, sent = refs
        results = (half_ref, rate_ref, None, None, written_ref, sent)
        for r in range(TILES):
            slope_ref[tile_rows(r), :] = pair_ref[r] + rest_ref[r]
        slope_copy = pltpu.make_async_copy(slope_ref, slope_out_ref, slope_sent)
        slope_copy.start()
    elif near:
        table_ref, sums_ref, packed_part_ref, packed_drive_ref, ice_ref = refs[:5]
        out_ref, columns_ref, rate_ref = refs[5:]
        results = (out_ref, rate_ref, None, None, None, None)
        odd = jnp.where(freq % 2 == 1, 1.0, 0.0)
        upper = jnp.where(freq >= 2, 1.0, 0.0)
        total, lower = [], []
        for i in range(PACKED_SUMS):
            here, there = PACKED_AT + i, HALF_TILES + i
            total.append((sums_ref[here] + other_ref[here]) + mine_ref[there])
            lower.append(odd * other_ref[here] + upper * mine_ref[there])
        slope, stress = (spread(total[i // BANDS], i % BANDS) for i in (ND, ND + 1))
        damp, gain = damp_and_gain(slope, stress, ice_ref[...])
        root = table_ref[freq, 4]
        for j in range(ND):
            under = spread(lower[j // BANDS], j % BANDS)
            rate = gain * packed_drive_ref[j] - damp - LOWER * under
            columns_ref[j] = packed_part_ref[j] * jnp.exp(root * rate)
    elif last:
        half_ref, _, out_ref, rate_ref, field_ref, sent = refs
        results = (out_ref, rate_ref, half_ref, field_ref, out_ref, sent)
    else:
        _, out_ref, rate_ref = refs
        results = (out_ref, rate_ref, None, None, None, None)
    for half in range(2):

        @pl.when(freq % 2 == (half if near else 1 - half))
        def _():
            grow_half(half, last, near, operands + results)

    if near and last:
        slope_copy.wait()


def cost(tiles, ops, moves):
    return pl.CostEstimate(
        flops=tiles * ops * 8 * WIDTH, bytes_accessed=tiles * moves * 32 * WIDTH, transcendentals=0
    )


def per_device(spectrum, east_wind, north_wind, land_sea, edge_rows):
    bands, count, lat_rows, width = spectrum.shape
    assert (bands, count, lat_rows, width) == (BANDS, ND, LAT, WIDTH)
    ring = lax.axis_size("lon")
    assert lax.axis_size("freq") == 4 and bands * 4 == NF and ring % 2 == 0
    f32 = jnp.float32

    def tiles(count):
        return jax.ShapeDtypeStruct((count, 8, WIDTH), f32)

    field = jax.ShapeDtypeStruct(spectrum.shape, f32)
    spread_field = jax.ShapeDtypeStruct((bands, ND, TILES, 8, WIDTH), f32)
    plane = jax.ShapeDtypeStruct((LAT, WIDTH), f32)
    tile = jax.ShapeDtypeStruct((8, WIDTH), f32)
    smem = pl.BlockSpec(memory_space=pltpu.SMEM)
    vmem = pl.BlockSpec(memory_space=pltpu.VMEM)
    hbm = pl.BlockSpec(memory_space=pltpu.HBM)
    params = pltpu.CompilerParams(vmem_limit_bytes=16 * 1024 * 1024)
    scalars, table = jnp.asarray(SCALARS), jnp.asarray(PACKED_TABLE)
    swap_core = [(0, 1), (1, 0), (2, 3), (3, 2)]
    swap_chip = [(0, 2), (2, 0), (1, 3), (3, 1)]
    swap_even = [(i, i ^ 1) for i in range(ring)]
    swap_odd = [(i, (i + (1 if i % 2 else -1)) % ring) for i in range(ring)]
    whole = bands * ND * TILES
    packed = pltpu.VMEM((ND, 8, WIDTH), f32)
    received = pltpu.VMEM((SENT, 8, WIDTH), f32)

    arguments = [spectrum, east_wind, north_wind, land_sea, edge_rows]
    spectrum, right, left, east_wind, north_wind, land_sea, edge_rows, even, odd = pl.pallas_call(
        pack_kernel,
        in_specs=[hbm] * 5,
        out_specs=[vmem] * 9,
        out_shape=[field, tiles(SENT), tiles(SENT)]
        + [jax.ShapeDtypeStruct(x.shape, x.dtype) for x in arguments[1:]]
        + [tiles(SENT), tiles(SENT)],
        scratch_shapes=[pltpu.SemaphoreType.DMA((bands + 4,)), packed, packed],
        compiler_params=params,
        cost_estimate=cost(whole, 6, 2),
        name="pack_columns",
    )(*(pltpu.with_memory_space_constraint(x, pltpu.HBM) for x in arguments))
    even = lax.ppermute(even, "lon", swap_even)
    odd = lax.ppermute(odd, "lon", swap_odd)
    drifted, drive = pl.pallas_call(
        drift_kernel,
        in_specs=[smem] + [vmem] * 4,
        out_specs=[vmem] * 2,
        out_shape=[spread_field, jax.ShapeDtypeStruct((ND, TILES, 8, WIDTH), f32)],
        compiler_params=params,
        cost_estimate=cost(whole, 12, 2),
        name="drift",
    )(scalars, spectrum, east_wind, north_wind, land_sea)

    for step in range(STEPS):
        first, last = step == 0, step == STEPS - 1
        sums = PACKED_AT + (PACKED_SUMS if first else 0)
        half_sums = sums - PACKED_AT + HALF_TILES
        operands = [table, drifted, spectrum if first else kept, land_sea, edge_rows]
        operands += [right, left, even, odd] if first else [columns]
        p, excess, mine, *packed_state = pl.pallas_call(
            functools.partial(source_kernel, first),
            in_specs=[vmem] * len(operands),
            out_specs=[vmem] * (6 if first else 3),
            out_shape=[spread_field, spread_field, tiles(sums)]
            + ([tiles(ND), tiles(ND), tile] if first else []),
            scratch_shapes=[packed]
            + ([received] * 2 + [packed] * 3 if first else []),
            compiler_params=params,
            cost_estimate=cost(whole, 30, 3),
            name="sources",
        )(*operands)
        other = lax.ppermute(mine, "freq", swap_core)
        weights = pl.pallas_call(
            weights_kernel,
            in_specs=[smem] + [vmem] * 2,
            out_specs=vmem,
            out_shape=tiles(2 * TILES),
            compiler_params=params,
            cost_estimate=cost(whole, 3, 1),
            name="slope_and_stress",
        )(scalars, p, drive)
        other, weights = lax.optimization_barrier((other, weights))
        weights_other = lax.ppermute(weights, "freq", swap_core)
        pair = pl.pallas_call(
            pair_kernel,
            in_specs=[vmem] * 2,
            out_specs=vmem,
            out_shape=tiles(half_sums),
            compiler_params=params,
            cost_estimate=cost(half_sums, 1, 3),
            name="pair_sums",
        )(mine, other)
        near = lax.ppermute(pair, "freq", swap_chip)
        weights_other, _ = lax.optimization_barrier((weights_other, pair))
        weights_pair = pl.pallas_call(
            add_kernel,
            in_specs=[vmem] * 2,
            out_specs=vmem,
            out_shape=tiles(2 * TILES),
            compiler_params=params,
            cost_estimate=cost(2 * TILES, 1, 3),
            name="pair_slope_and_stress",
        )(weights, weights_other)
        weights_rest = lax.ppermute(weights_pair, "freq", swap_chip)
        excess, _ = lax.optimization_barrier((excess, weights_pair))
        operands = [scalars, p, excess] + ([] if last else [spectrum, land_sea, edge_rows])
        part, *kept = pl.pallas_call(
            functools.partial(local_kernel, last),
            in_specs=[smem] + [vmem] * (len(operands) - 1),
            out_specs=[vmem] * (1 if last else 2),
            out_shape=[spread_field] * (1 if last else 2),
            compiler_params=params,
            cost_estimate=cost(whole, 8, 3),
            name="local_rate",
        )(*operands)
        kept = None if last else kept[0]
        near, weights_rest, part = lax.optimization_barrier((near, weights_rest, part))
        far = lax.ppermute(near, "freq", swap_core)

        common = [weights_pair, weights_rest, drive, land_sea]
        half_rate = pltpu.VMEM((HALF, TILES, 8, WIDTH), f32)
        half_field = (bands, HALF, LAT, WIDTH)
        sent = pltpu.SemaphoreType.DMA((2, bands))

        def grow(is_near, lower, extra, specs, results, shapes, scratch, alias):
            operands = [scalars, part, other, lower, *common, *extra]
            return pl.pallas_call(
                functools.partial(growth_kernel, last, is_near),
                in_specs=[smem] + [vmem] * (len(operands) - 1 - len(specs)) + specs,
                out_specs=results,
                out_shape=shapes,
                input_output_aliases={len(operands) - 1: 0} if alias else {},
                scratch_shapes=[half_rate] + scratch,
                compiler_params=params,
                cost_estimate=cost(whole, 6 if last else 12, 1),
                name="grow_near" if is_near else "grow_far",
            )(*operands)

        if last:
            shapes = [jax.ShapeDtypeStruct(half_field, f32), plane, field]
            scratch = [pltpu.VMEM(plane.shape, f32), pltpu.SemaphoreType.DMA(()), sent]
            made, columns, written = grow(True, near, [], [], [vmem, hbm, hbm], shapes, scratch, False)
            scratch = [pltpu.VMEM(half_field, f32), sent]
            (drifted,) = grow(False, far, [made, written], [hbm], [hbm], [field], scratch, True)
        else:
            shapes = [spread_field, tiles(ND)]
            extra = [table, mine, *packed_state]
            made, columns = grow(True, near, extra, [], [vmem] * 2, shapes, [], False)
            (drifted,) = grow(False, far, [made], [], [vmem], [spread_field], [], True)
    return drifted, columns


def solution(mesh):
    in_specs = (
        P("freq", None, None, "lon"),
        P(None, "lon"),
        P(None, "lon"),
        P(None, "lon"),
        P(None, "lon"),
    )
    out_specs = (P("freq", None, None, "lon"), P(None, "lon"))
    return jax.shard_map(
        per_device, mesh=mesh, in_specs=in_specs, out_specs=out_specs, check_vma=False
    )
```
